32 devices in a mesh: cfg: 2 (over x), pr: 16 (over z, y, core).
Axes of the slice: x: 2, y: 2, z: 4, core: 2. Of those that a mesh axis runs over, the one named last changes fastest.
Arguments:
- sep_inv: float32 [4096, 2048], P(('cfg', 'pr')), parts along dimension 0, as said below
- factor: float32 [1024, 65536], P('cfg', 'pr'), parts along dimension 0, may hold values from -0.5 to 0.5
- widths: int32 [16, 8], P('pr'), may hold values from 1 to 8, 32 in all within a row
- patterns: int32 [128, 4], P('pr'), may hold values from 0 to 15, all different within a row; in each aligned block of 8 rows (0 to 7, 8 to 15, ...) at most 2 rows name the same one
- dinv: float32 [131072], P(('cfg', 'pr')), parts along dimension 0, may hold values from 2 to 20
Outputs:
- sel_offdiag: float32 [1024, 65536], P('cfg', 'pr'), parts along dimension 0
- marg_var: float32 [131072], P(('cfg', 'pr')), parts along dimension 0
The draws below stay inside these ranges and needn't reach their ends.
There are 2 independent parts, one for each index of `cfg`. The reference program is written for one: setup_inputs(seed, part) draws one part's arguments, and reference() takes and returns one part's arrays. A program takes and returns all parts, laid end to end along the dimension named above; an argument that names none is the same for every part. Nothing has to cross between parts.
Inputs may be any that keep to these rules, and one draw needn't show every extreme that they name: sep_inv is symmetric. `widths`: each aligned block of 8 entries of one index of pr sums to 32, and its largest is 8. `patterns`: each row names 4 different separator tiles; among the 8 rows of one index of pr no tile is named more than 2 times, and on some index a tile is named exactly 2 times.
All inputs are finite; a program needn't handle non-finite values.
Results may differ from the reference program's by a relative error of at most 0.0003.
Values sent between devices are 32-bit elements; how exact they have to be, the bound alone decides.
No kernel may reach another device: no remote copies, remote signals or barrier semaphores. Data moves between devices by JAX's collectives and lax.ppermute only.
A program may use at most 128 MiB of HBM per device.

```python
import math
import jax
import jax.numpy as jnp
import numpy as np
from jax import lax

TILE = 128
P_SIZE = 4
WMAX = 8
SEP_TILES = 16
TILES_DEV = 32
NS = 8
MOST = 2
MS = 2048
PT = 512
NCOLS = 65536
N_PR = 16


def draw_sep_inv(key, part):
    key = jax.random.fold_in(key, 11)
    key_base, key_diag = jax.random.split(key, 2)
    base = jax.random.normal(key_base, (MS, MS), jnp.float32)
    coupling = (base + base.T) * (1.06 / math.sqrt(MS))
    diagonal = jax.random.uniform(key_diag, (MS,), jnp.float32, 2.0, 4.0)
    index = jnp.arange(MS, dtype=jnp.int32)
    on_diag = index[:, None] == index[None, :]
    return jnp.where(on_diag, diagonal[:, None] * jnp.ones((1, MS), jnp.float32), coupling)


def shard_levels(stream_key, shape, shards, smallest, high):
    level = 1.0
    for dim, parts in shards:
        steps = jax.random.uniform(jax.random.fold_in(jax.random.fold_in(stream_key, 6), dim), (parts,), jnp.float32, smallest / len(shards), high / len(shards))
        level = level * jnp.repeat(jnp.exp(steps), shape[dim] // parts).reshape((-1,) + (1,) * (len(shape) - 1 - dim))
    return level


def split_up(count, total, limit, slope):
    loads = [(1 << 20) // math.isqrt(grade ** slope) + 1 for grade in range(2, count + 1)]
    spare, counts = total - limit - (count - 1), [1] * (count - 1)
    while spare > 0:
        candidates = [i for i in range(count - 1) if counts[i] < limit]
        pool, left = sum([loads[i] for i in candidates]), spare
        for i in candidates:
            extra = min(limit - counts[i], max(1, left * loads[i] // pool), spare)
            counts[i] = counts[i] + extra
            spare = spare - extra
    return np.array([limit] + counts)


def uneven(stream_key, amount, total, most, skew):
    if amount == 2:
        one = jax.random.randint(stream_key, (), max(1, total - most), min(most, total - 1) + 1)
        return jnp.stack([one, total - one])
    tallies = jnp.asarray(split_up(amount, total, most, skew), jnp.int32)
    twos = (amount - 1) // 2
    giver, taker = tallies[1:1 + 2 * twos:2], tallies[2:2 + 2 * twos:2]
    margin = jnp.minimum(giver - 1, most - taker)
    moved = jax.random.randint(jax.random.fold_in(stream_key, 1), (twos,), 0, 1 << 20) % (margin + 1)
    tallies = tallies.at[1:1 + 2 * twos:2].set(giver - moved).at[2:2 + 2 * twos:2].set(taker + moved)
    return tallies[jax.random.permutation(jax.random.fold_in(stream_key, 2), amount)]


def deal_out(stream_key, own, number, rows, number_of, top, bound, skew):
    ranking = jax.random.permutation(stream_key, number_of)
    crowded, common = load_shares(number_of, rows * top, bound, skew, True), load_shares(number_of, rows * top, bound, skew, False)
    places = jnp.arange(number_of)

    def named(sizes, turn):
        used = int((sizes > 0).sum())
        fixed = max(1, used // 4)
        moved = fixed + (places - fixed + turn * (used - fixed)) % max(1, number_of - fixed)
        return jnp.zeros((number_of,), jnp.int32).at[ranking[jnp.where(places < fixed, places, moved)]].set(jnp.asarray(sizes, jnp.int32))

    sizes = jnp.where(number % 4 == 0, named(crowded, number // 4), named(common, number - number // 4 - 1))
    mixed = jax.random.permutation(jax.random.fold_in(own, 3), number_of)
    source_of, sink = mixed[0:number_of // 2 * 2:2], mixed[1:number_of // 2 * 2:2]
    margin = jnp.minimum(sizes[source_of] - 1, bound - sizes[sink]) // 2
    margin = jnp.where((source_of == ranking[0]) | (sink == ranking[0]) | (sizes[sink] == 0), 0, jnp.maximum(margin, 0))
    moved = jax.random.randint(jax.random.fold_in(own, 4), (number_of // 2,), 0, 1 << 20) % (margin + 1)
    sizes = sizes.at[source_of].add(-moved).at[sink].add(moved)
    labels = jnp.searchsorted(jnp.cumsum(sizes), jnp.arange(rows * top), side="right").astype(jnp.int32)
    grid = labels.reshape(top, rows).T
    grid = grid[jax.random.permutation(jax.random.fold_in(own, 1), rows)]
    turn = jax.random.randint(jax.random.fold_in(own, 2), (rows, 1), 0, top)
    return jnp.take_along_axis(grid, (jnp.arange(top)[None, :] + turn) % top, axis=1)


def load_shares(number_of, total, most, skew, full):
    portions = [(1 << 20) // math.isqrt(grade ** skew) + 1 for grade in range(1, number_of + 1)]
    largest = most if full else min(most, max(-(-total // number_of), total * portions[0] // sum(portions)))
    least = 1 if total - largest >= number_of - 1 else 0
    holding, surplus = [largest] + [least] * (number_of - 1), total - largest - least * (number_of - 1)
    while surplus > 0:
        movable = [i for i in range(1, number_of) if holding[i] < largest] or [i for i in range(1, number_of) if holding[i] < most]
        pool, budget = sum([portions[i] for i in movable]), surplus
        for i in movable:
            extra = min(most - holding[i], max(1, budget * portions[i] // pool), surplus)
            holding[i] = holding[i] + extra
            surplus = surplus - extra
    return np.array(holding)


def normal_values(stream_key, extent, width, bound, pieces=(), kind=jnp.bfloat16):
    array = jax.random.normal(stream_key, extent, jnp.float32) * width
    if len(pieces) > 0:
        array = shard_levels(stream_key, extent, pieces, -0.22, 0.18) * array
    return jnp.clip(array, min=-bound, max=bound).astype(kind)


def setup_inputs(seed: int = 0, part: int = 0) -> dict:
    key_of = jax.random.split(jax.random.key(seed), 6)
    part_splits = jax.random.split(jax.random.fold_in(key_of[5], part), 6)
    sep_inv = draw_sep_inv(jax.random.fold_in(jax.random.fold_in(key_of[5], part), 71), part)
    factor = normal_values(part_splits[1], (PT, NCOLS), (2.0 / (P_SIZE * TILE) ** 0.5), 0.5, ((1, 16),), jnp.float32)
    widths = jax.vmap(lambda own: uneven(own, NS, TILES_DEV, WMAX, 2))(jax.random.split(key_of[2], N_PR)).reshape((N_PR, NS)).astype(jnp.int32)
    patterns_keys = jax.random.split(jax.random.fold_in(key_of[3], 1), (N_PR * NS) // NS)
    patterns_turns = jax.random.permutation(jax.random.fold_in(key_of[3], 3), (N_PR * NS) // NS)
    patterns = jax.vmap(lambda own, number: deal_out(jax.random.fold_in(key_of[3], 2), own, number, NS, SEP_TILES, P_SIZE, MOST, 2))(patterns_keys, patterns_turns).reshape((N_PR * NS, P_SIZE))
    dinv = jnp.clip(jnp.exp(math.log(20.0) - 2.3025851 * jax.random.uniform(part_splits[4], (NCOLS,), jnp.float32) ** shard_levels(part_splits[4], (NCOLS,), ((0, 16),), -0.2, 0.2)), 2.0, 20.0)
    return {"sep_inv": sep_inv, "factor": factor, "widths": widths, "patterns": patterns, "dinv": dinv}


def supernode_of_tile(dev_widths):
    tile_ends = jnp.cumsum(dev_widths).astype(jnp.int32)
    tile_ids = jnp.arange(TILES_DEV, dtype=jnp.int32)
    return jnp.sum((tile_ids[:, None] >= tile_ends[None, :]).astype(jnp.int32), axis=1)


def device_part(sep_inv, dev_factor, dev_widths, dev_patterns, dev_dinv):
    offsets = jnp.arange(TILE, dtype=jnp.int32)
    row_index = (dev_patterns[:, :, None] * TILE + offsets[None, None, :]).reshape(NS, P_SIZE * TILE).astype(jnp.int32)

    def pick_block(index):
        return jnp.take(jnp.take(sep_inv, index, axis=0), index, axis=1)

    blocks = lax.map(pick_block, row_index)
    per_tile = jnp.take(blocks, supernode_of_tile(dev_widths), axis=0)
    factor_cols = dev_factor.reshape(P_SIZE * TILE, TILES_DEV, TILE)
    product = -jnp.einsum("tab,btc->atc", per_tile, factor_cols, precision=lax.Precision.HIGHEST)
    offdiag = product.reshape(P_SIZE * TILE, TILES_DEV * TILE)
    variance = dev_dinv - jnp.sum(dev_factor * offdiag, axis=0)
    return offdiag, variance


def reference(sep_inv, factor, widths, patterns, dinv):
    per_factor = factor.reshape(P_SIZE * TILE, N_PR, TILES_DEV * TILE).transpose(1, 0, 2)
    per_patterns = patterns.reshape(N_PR, NS, P_SIZE)
    per_dinv = dinv.reshape(N_PR, TILES_DEV * TILE)

    def one_device(item):
        return device_part(sep_inv, item[0], item[1], item[2], item[3])

    offdiag, variance = lax.map(one_device, (per_factor, widths, per_patterns, per_dinv))
    sel_offdiag = offdiag.transpose(1, 0, 2).reshape(P_SIZE * TILE, N_PR * TILES_DEV * TILE)
    return sel_offdiag, variance.reshape(N_PR * TILES_DEV * TILE)
```

```python
import functools

import jax
import jax.numpy as jnp
from jax import lax
from jax.experimental import pallas as pl
from jax.experimental.pallas import tpu as pltpu
from jax.sharding import PartitionSpec as P

TILE = 128
HALF = TILE // 2
MIB = 1024 * 1024


def split(value):
    high = value.astype(jnp.bfloat16)
    low = (value - high.astype(jnp.float32)).astype(jnp.bfloat16)
    return high, low


def pack_kernel(tiles, me_ref, rows_ref, packed_ref):
    me = me_ref[0]
    half = tiles // 2
    for d in range(half):
        col = lax.rem(me + d, tiles) * TILE
        packed_ref[d * TILE : (d + 1) * TILE, :] = rows_ref[:, pl.ds(pl.multiple_of(col, TILE), TILE)]
    col = lax.rem(me + half, tiles) * TILE
    opposite = rows_ref[:, pl.ds(pl.multiple_of(col, TILE), TILE)]

    @pl.when(me < half)
    def _():
        packed_ref[half * TILE :, :] = opposite[:HALF, :]

    @pl.when(me >= half)
    def _():
        packed_ref[half * TILE :, :] = opposite.T[HALF:, :]


def pack(sep_rows, me, tiles):
    return pl.pallas_call(
        functools.partial(pack_kernel, tiles),
        out_shape=jax.ShapeDtypeStruct((tiles * HALF + HALF, TILE), jnp.float32),
        in_specs=[pl.BlockSpec(memory_space=pltpu.SMEM), pl.BlockSpec(memory_space=pltpu.VMEM)],
        out_specs=pl.BlockSpec(memory_space=pltpu.VMEM),
        compiler_params=pltpu.CompilerParams(vmem_limit_bytes=8 * MIB),
        name="pack_share",
    )(me, sep_rows)


def place(high_ref, low_ref, node, a, b, high, low):
    rows = pl.ds(pl.multiple_of(a * TILE, TILE), TILE)
    cols = pl.ds(pl.multiple_of(b * TILE, TILE), TILE)
    high_ref[node, rows, cols] = high
    low_ref[node, rows, cols] = low


def assemble_kernel(tiles, nodes, sides, patterns_ref, packed_ref, high_ref, low_ref):
    half = tiles // 2
    share = tiles * HALF + HALF

    def one(step, _):
        node = step // (sides * sides)
        a = lax.rem(step // sides, sides)
        b = lax.rem(step, sides)
        r = patterns_ref[node, a]
        q = patterns_ref[node, b]
        d = lax.rem(q - r + tiles, tiles)

        @pl.when(d < half)
        def _():
            start = pl.multiple_of(r * share + d * TILE, HALF)
            value = packed_ref[pl.ds(start, TILE), :]
            high, low = split(value)
            place(high_ref, low_ref, node, a, b, high, low)

            @pl.when(d > 0)
            def _():
                high, low = split(value.T)
                place(high_ref, low_ref, node, b, a, high, low)

        @pl.when((d == half) & (r < half))
        def _():
            first = pl.multiple_of(r * share + half * TILE, HALF)
            second = pl.multiple_of(q * share + half * TILE, HALF)
            value = jnp.concatenate([packed_ref[pl.ds(first, HALF), :], packed_ref[pl.ds(second, HALF), :]], axis=0)
            high, low = split(value)
            place(high_ref, low_ref, node, a, b, high, low)
            high, low = split(value.T)
            place(high_ref, low_ref, node, b, a, high, low)

        return 0

    lax.fori_loop(0, nodes * sides * sides, one, 0)


def assemble_full_kernel(nodes, sides, patterns_ref, whole_ref, high_ref, low_ref):
    def one(step, _):
        node = step // (sides * sides)
        a = lax.rem(step // sides, sides)
        b = lax.rem(step, sides)
        rows = pl.ds(pl.multiple_of(patterns_ref[node, a] * TILE, TILE), TILE)
        cols = pl.ds(pl.multiple_of(patterns_ref[node, b] * TILE, TILE), TILE)
        high, low = split(whole_ref[rows, cols])
        place(high_ref, low_ref, node, a, b, high, low)
        return 0

    lax.fori_loop(0, nodes * sides * sides, one, 0)


def assemble(kernel, patterns, source):
    nodes, sides = patterns.shape
    side = sides * TILE
    return pl.pallas_call(
        kernel,
        out_shape=[pltpu.VMEM((nodes, side, side), jnp.bfloat16)] * 2,
        in_specs=[pl.BlockSpec(memory_space=pltpu.SMEM), pl.BlockSpec(memory_space=pltpu.VMEM)],
        out_specs=[pl.BlockSpec(memory_space=pltpu.VMEM)] * 2,
        compiler_params=pltpu.CompilerParams(vmem_limit_bytes=32 * MIB),
        name="assemble_blocks",
    )(patterns, source)


def halves_kernel(factor_ref, high_ref, low_ref):
    high_ref[...], low_ref[...] = split(factor_ref[...])


def factor_halves(factor):
    rows, cols = factor.shape
    step = 512
    spec = pl.BlockSpec((rows, step), lambda i: (0, i))
    return pl.pallas_call(
        halves_kernel,
        grid=(cols // step,),
        out_shape=[jax.ShapeDtypeStruct((rows, cols), jnp.bfloat16)] * 2,
        in_specs=[spec],
        out_specs=[spec] * 2,
        name="factor_halves",
        cost_estimate=pl.CostEstimate(flops=4 * rows * cols, bytes_accessed=8 * rows * cols, transcendentals=0),
    )(factor)


def product_kernel(nodes, widths_ref, high_ref, low_ref, factor_ref, dinv_ref, out_ref, marg_ref):
    pair = pl.program_id(0)

    def node_of(tile):
        node, end = 0, 0
        for j in range(nodes):
            end = end + widths_ref[0, j]
            node = node + (tile >= end).astype(jnp.int32)
        return jnp.minimum(node, nodes - 1)

    first, second = node_of(2 * pair), node_of(2 * pair + 1)

    def columns(node, where):
        factor = factor_ref[:, where]
        f_high, f_low = split(factor)
        high, low = high_ref[node], low_ref[node]
        dot = functools.partial(jnp.dot, preferred_element_type=jnp.float32)
        product = -(dot(high, f_high) + (dot(high, f_low) + dot(low, f_high)))
        out_ref[:, where] = product
        total = jnp.sum(factor * product, axis=0, keepdims=True)
        for k in range(factor.shape[1] // TILE):
            row = pl.ds(2 * pair + where.start // TILE + k, 1)
            marg_ref[row, :] = dinv_ref[row, :] - total[:, k * TILE : (k + 1) * TILE]

    @pl.when(first == second)
    def _():
        columns(first, slice(0, 2 * TILE))

    @pl.when(first != second)
    def _():
        columns(first, slice(0, TILE))
        columns(second, slice(TILE, 2 * TILE))


def products(widths, high, low, factor, dinv):
    rows, cols = factor.shape
    nodes = widths.shape[1]
    whole = pl.BlockSpec(memory_space=pltpu.VMEM)
    spec = pl.BlockSpec((rows, 2 * TILE), lambda i: (0, i))
    out, marg = pl.pallas_call(
        functools.partial(product_kernel, nodes),
        grid=(cols // (2 * TILE),),
        out_shape=[jax.ShapeDtypeStruct((rows, cols), jnp.float32), jax.ShapeDtypeStruct((cols // TILE, TILE), jnp.float32)],
        in_specs=[pl.BlockSpec(memory_space=pltpu.SMEM), whole, whole, spec, whole],
        out_specs=[spec, whole],
        compiler_params=pltpu.CompilerParams(vmem_limit_bytes=40 * MIB),
        name="products",
        cost_estimate=pl.CostEstimate(flops=6 * rows * rows * cols, bytes_accessed=8 * rows * cols, transcendentals=0),
    )(widths, high, low, factor, dinv.reshape(cols // TILE, TILE))
    return out, marg.reshape(cols)


def shards(sep_inv, factor, widths, patterns, dinv):
    own_rows, order = sep_inv.shape
    tiles = order // TILE
    nodes, sides = patterns.shape
    if own_rows == TILE and tiles % 2 == 0:
        me = lax.axis_index("pr").astype(jnp.int32).reshape(1)
        packed = pack(sep_inv, me, tiles)
        gathered = lax.all_gather(packed, "pr", axis=0, tiled=True)
        kernel = functools.partial(assemble_kernel, tiles, nodes, sides)
    else:
        gathered = lax.all_gather(sep_inv, "pr", axis=0, tiled=True)
        kernel = functools.partial(assemble_full_kernel, nodes, sides)
    high, low = assemble(kernel, patterns, gathered)
    return products(widths, high, low, factor, dinv)


def solution(mesh):
    placed = (
        P(("cfg", "pr"), None),
        P("cfg", "pr"),
        P("pr", None),
        P("pr", None),
        P(("cfg", "pr")),
    )
    return jax.shard_map(
        shards,
        mesh=mesh,
        in_specs=placed,
        out_specs=(P("cfg", "pr"), P(("cfg", "pr"))),
        check_vma=False,
    )
```

```python
import functools

import jax
import jax.numpy as jnp
from jax import lax
from jax.experimental import pallas as pl
from jax.experimental.pallas import tpu as pltpu
from jax.sharding import PartitionSpec as P

TILE = 128
HALF = TILE // 2
MIB = 1024 * 1024

ORDER = (0, 2, 1, 3, 4, 6, 5, 7)
PIECES = {
    "near": (2, True, (4, 6, 5, 7)),
    "near_rest": (2, False, (1, 3)),
    "side": (1, True, (3, 4, 6, 5, 7)),
    "mid": (4, True, (6,)),
    "mid_rest": (4, False, (5, 7)),
    "far": (6, True, ()),
    "far_rest": (6, False, (5, 7)),
    "side_near": (3, True, (5, 7, 4, 6)),
    "side_mid": (5, True, (7,)),
    "side_far": (7, True, ()),
}
SENT = ("side", "near", "mid", "far", "near_rest", "mid_rest", "far_rest")
PASSED_ON = {"side_near": "near", "side_mid": "mid", "side_far": "far"}
PHASES = (("rows",), ("near", "side"), ("near_rest", "mid", "far", "side_near"), ("mid_rest", "far_rest", "side_mid", "side_far"))
KINDS = ("rows",) + tuple(PIECES)
DEVICES = 16
CLASSES = DEVICES // 2


def piece_rows(name):
    _, own, classes = PIECES[name]
    return 2 * TILE * len(classes) + (TILE + HALF if own else 0)


def piece_table():
    table = [0] * (CLASSES * CLASSES)
    for name, (owner, own, classes) in PIECES.items():
        kind = KINDS.index(name)
        for place, column in enumerate(classes):
            table[owner * CLASSES + column] = kind * 64 + 4 * place + (2 if own else 0)
        if own:
            table[owner * CLASSES + owner] = kind * 64 + 4 * len(classes) + 2
    return jnp.array(table, jnp.int32)


def split(value):
    high = value.astype(jnp.bfloat16)
    low = (value - high.astype(jnp.float32)).astype(jnp.bfloat16)
    return high, low


def pack_kernel(names, me_ref, rows_ref, *packed_refs):
    me = me_ref[0]

    def tile(q):
        return rows_ref[:, pl.ds(pl.multiple_of(q * TILE, TILE), TILE)]

    diagonal, pair = tile(me), tile(me ^ 1)
    half = jnp.where(me % 2 == 0, pair[:HALF, :], pair.T[HALF:, :])
    for name, packed_ref in zip(names, packed_refs, strict=True):
        owner, own, classes = PIECES[name]
        row = 0
        if own:
            packed_ref[:TILE, :] = diagonal
            row = TILE
        for column in classes:
            for core in range(2):
                q = (me & ~1) ^ (2 * (owner ^ column)) ^ core
                packed_ref[row : row + TILE, :] = tile(q)
                row += TILE
        if own:
            packed_ref[row : row + HALF, :] = half


def pack(names, me, sep_rows):
    return pl.pallas_call(
        functools.partial(pack_kernel, names),
        out_shape=[jax.ShapeDtypeStruct((piece_rows(name), TILE), jnp.float32) for name in names],
        in_specs=[pl.BlockSpec(memory_space=pltpu.SMEM), pl.BlockSpec(memory_space=pltpu.VMEM)],
        out_specs=[pl.BlockSpec(memory_space=pltpu.VMEM)] * len(names),
        compiler_params=pltpu.CompilerParams(vmem_limit_bytes=16 * MIB),
        name="pack_" + names[0],
    )(me, sep_rows)


def jobs_kernel(nodes, sides, me_ref, table_ref, patterns_ref, jobs_ref, count_ref):
    room = jobs_ref.shape[1]
    me = me_ref[0]
    ranks = sum(ORDER.index(c) << (3 * c) for c in range(CLASSES))
    for s in range(2 * len(KINDS)):
        count_ref[s] = 0

    def one(step, _):
        node, a, b = step // (sides * sides), (step // sides) % sides, step % sides
        r, q = patterns_ref[node, a], patterns_ref[node, b]
        owner, column = (r ^ me) >> 1, (q ^ me) >> 1
        core = r & 1
        rank_r, rank_q = (ranks >> (3 * owner)) & 7, (ranks >> (3 * column)) & 7
        same = owner == column
        here = owner == 0
        entry = table_ref[owner * CLASSES + column]
        kind = jnp.where(here, 0, entry // 64)
        first = jnp.where(same, jnp.where(r == q, 0, entry % 64), entry % 64 + 2 * (q & 1))
        first = jnp.where(here, q, first)
        halved = same & (r != q) & (owner != 0)
        sends = jnp.where(same, (r == q) | (owner != 0) | (core == 0), rank_r < rank_q)
        swap = halved & (core == 1)
        low_a, low_b = jnp.where(swap, b, a), jnp.where(swap, a, b)

        @pl.when(sends)
        def _():
            slot = kind * 2 + ((r ^ me) & 1)
            at = count_ref[slot]
            code = ((first * nodes + node) * sides + low_a) * sides + low_b
            jobs_ref[slot, at] = code * 2 + halved.astype(jnp.int32)
            count_ref[slot] = at + 1

        return 0

    lax.fori_loop(0, nodes * sides * sides, one, 0)


def plan_jobs(me, patterns):
    nodes, sides = patterns.shape
    smem = pl.BlockSpec(memory_space=pltpu.SMEM)
    return pl.pallas_call(
        functools.partial(jobs_kernel, nodes, sides),
        out_shape=[
            jax.ShapeDtypeStruct((2 * len(KINDS), nodes * sides), jnp.int32),
            jax.ShapeDtypeStruct((2 * len(KINDS),), jnp.int32),
        ],
        in_specs=[smem] * 3,
        out_specs=[smem] * 2,
        name="plan_jobs",
    )(me, piece_table(), patterns)


def place(high_ref, low_ref, node, a, b, high, low):
    rows = pl.ds(pl.multiple_of(a * TILE, TILE), TILE)
    cols = pl.ds(pl.multiple_of(b * TILE, TILE), TILE)
    high_ref[node, rows, cols] = high
    low_ref[node, rows, cols] = low


def assemble_kernel(names, nodes, sides, me_ref, jobs_ref, count_ref, *refs):
    sources, (high_ref, low_ref) = refs[: 2 * len(names)], refs[-2:]
    mine = me_ref[0] & 1

    def work(name, other, source):
        slot = KINDS.index(name) * 2 + other
        core = mine ^ other

        def one(i, _):
            code = jobs_ref[slot, i]
            halved, code = code % 2, code // 2
            b, code = code % sides, code // sides
            a, code = code % sides, code // sides
            node, first = code % nodes, code // nodes

            @pl.when(halved == 0)
            def _():
                if name == "rows":
                    value = source[:, pl.ds(pl.multiple_of(first * TILE, TILE), TILE)]
                else:
                    value = source[pl.ds(pl.multiple_of(first * HALF, HALF), TILE), :]
                high, low = split(value)
                place(high_ref, low_ref, node, a, b, high, low)

                @pl.when(a != b)
                def _():
                    high, low = split(value.T)
                    place(high_ref, low_ref, node, b, a, high, low)

            if name == "rows" or not PIECES[name][1]:
                return 0

            @pl.when(halved == 1)
            def _():
                value = source[pl.ds(pl.multiple_of(first * HALF, HALF), HALF), :]
                high, low = split(value)
                rows = pl.ds(pl.multiple_of(a * TILE + core * HALF, HALF), HALF)
                cols = pl.ds(pl.multiple_of(b * TILE, TILE), TILE)
                high_ref[node, rows, cols] = high
                low_ref[node, rows, cols] = low
                rows = pl.ds(pl.multiple_of(b * TILE, TILE), TILE)
                cols = pl.ds(pl.multiple_of(a * TILE, TILE), TILE)
                for ref, part in zip((high_ref, low_ref), split(value.T), strict=True):
                    old = ref[node, rows, cols]
                    both = jnp.concatenate([part, part], axis=1)
                    column = lax.broadcasted_iota(jnp.int32, both.shape, 1)
                    ref[node, rows, cols] = jnp.where(column // HALF == core, both, old)

            return 0

        lax.fori_loop(0, count_ref[slot], one, 0)

    for i, name in enumerate(names):
        for other in range(2):
            work(name, other, sources[2 * i + other])


def assemble(names, me, jobs, count, patterns, sources, blocks):
    nodes, sides = patterns.shape
    side = sides * TILE
    smem, vmem = pl.BlockSpec(memory_space=pltpu.SMEM), pl.BlockSpec(memory_space=pltpu.VMEM)
    given = [pltpu.with_memory_space_constraint(block, pltpu.VMEM) for block in blocks]
    return pl.pallas_call(
        functools.partial(assemble_kernel, names, nodes, sides),
        out_shape=[pltpu.VMEM((nodes, side, side), jnp.bfloat16)] * 2,
        in_specs=[smem] * 3 + [vmem] * (len(sources) + len(given)),
        out_specs=[vmem] * 2,
        input_output_aliases={3 + len(sources) + i: i for i in range(len(given))},
        compiler_params=pltpu.CompilerParams(vmem_limit_bytes=32 * MIB),
        name="assemble_" + names[0],
    )(me, jobs, count, *sources, *given)


def assemble_full_kernel(nodes, sides, patterns_ref, whole_ref, high_ref, low_ref):
    def one(step, _):
        node = step // (sides * sides)
        a = lax.rem(step // sides, sides)
        b = lax.rem(step, sides)
        rows = pl.ds(pl.multiple_of(patterns_ref[node, a] * TILE, TILE), TILE)
        cols = pl.ds(pl.multiple_of(patterns_ref[node, b] * TILE, TILE), TILE)
        high, low = split(whole_ref[rows, cols])
        place(high_ref, low_ref, node, a, b, high, low)
        return 0

    lax.fori_loop(0, nodes * sides * sides, one, 0)


def assemble_full(patterns, source):
    nodes, sides = patterns.shape
    side = sides * TILE
    return pl.pallas_call(
        functools.partial(assemble_full_kernel, nodes, sides),
        out_shape=[pltpu.VMEM((nodes, side, side), jnp.bfloat16)] * 2,
        in_specs=[pl.BlockSpec(memory_space=pltpu.SMEM), pl.BlockSpec(memory_space=pltpu.VMEM)],
        out_specs=[pl.BlockSpec(memory_space=pltpu.VMEM)] * 2,
        compiler_params=pltpu.CompilerParams(vmem_limit_bytes=32 * MIB),
        name="assemble_full",
    )(patterns, source)


def halves_kernel(factor_ref, high_ref, low_ref):
    high_ref[...], low_ref[...] = split(factor_ref[...])


def factor_halves(factor):
    rows, cols = factor.shape
    step = 512
    spec = pl.BlockSpec((rows, step), lambda i: (0, i))
    return pl.pallas_call(
        halves_kernel,
        grid=(cols // step,),
        out_shape=[jax.ShapeDtypeStruct((rows, cols), jnp.bfloat16)] * 2,
        in_specs=[spec],
        out_specs=[spec] * 2,
        name="factor_halves",
        cost_estimate=pl.CostEstimate(flops=4 * rows * cols, bytes_accessed=8 * rows * cols, transcendentals=0),
    )(factor)


def product_kernel(nodes, widths_ref, high_ref, low_ref, factor_ref, dinv_ref, out_ref, marg_ref):
    pair = pl.program_id(0)

    def node_of(tile):
        node, end = 0, 0
        for j in range(nodes):
            end = end + widths_ref[0, j]
            node = node + (tile >= end).astype(jnp.int32)
        return jnp.minimum(node, nodes - 1)

    first, second = node_of(2 * pair), node_of(2 * pair + 1)

    def columns(node, where):
        factor = factor_ref[:, where]
        f_high, f_low = split(factor)
        high, low = high_ref[node], low_ref[node]
        dot = functools.partial(jnp.dot, preferred_element_type=jnp.float32)
        product = -(dot(high, f_high) + (dot(high, f_low) + dot(low, f_high)))
        out_ref[:, where] = product
        total = jnp.sum(factor * product, axis=0, keepdims=True)
        for k in range(factor.shape[1] // TILE):
            row = pl.ds(2 * pair + where.start // TILE + k, 1)
            marg_ref[row, :] = dinv_ref[row, :] - total[:, k * TILE : (k + 1) * TILE]

    @pl.when(first == second)
    def _():
        columns(first, slice(0, 2 * TILE))

    @pl.when(first != second)
    def _():
        columns(first, slice(0, TILE))
        columns(second, slice(TILE, 2 * TILE))


def products(widths, high, low, factor, dinv):
    rows, cols = factor.shape
    nodes = widths.shape[1]
    whole = pl.BlockSpec(memory_space=pltpu.VMEM)
    spec = pl.BlockSpec((rows, 2 * TILE), lambda i: (0, i))
    out, marg = pl.pallas_call(
        functools.partial(product_kernel, nodes),
        grid=(cols // (2 * TILE),),
        out_shape=[jax.ShapeDtypeStruct((rows, cols), jnp.float32), jax.ShapeDtypeStruct((cols // TILE, TILE), jnp.float32)],
        in_specs=[pl.BlockSpec(memory_space=pltpu.SMEM), whole, whole, spec, whole],
        out_specs=[spec, whole],
        compiler_params=pltpu.CompilerParams(vmem_limit_bytes=40 * MIB),
        name="products",
        cost_estimate=pl.CostEstimate(flops=6 * rows * rows * cols, bytes_accessed=8 * rows * cols, transcendentals=0),
    )(widths, high, low, factor, dinv.reshape(cols // TILE, TILE))
    return out, marg.reshape(cols)


def swap(value, mask):
    return lax.ppermute(value, "pr", [(i, i ^ mask) for i in range(DEVICES)])


def planned_blocks(sep_inv, patterns):
    me = lax.axis_index("pr").astype(jnp.int32).reshape(1)
    packed = {}
    for names in (SENT[:2], SENT[2:]):
        packed |= zip(names, pack(names, me, sep_inv), strict=True)
    here = {"rows": sep_inv}
    for name in SENT:
        here[name] = swap(packed[name], 2 * PIECES[name][0])
    for name, source in PASSED_ON.items():
        here[name] = swap(here[source], 2)
    jobs, count = plan_jobs(me, patterns)
    blocks = ()
    for names in PHASES:
        sources = []
        for name in names:
            sources += [here[name], swap(here[name], 1)]
        blocks = assemble(names, me, jobs, count, patterns, sources, blocks)
    return blocks


def shards(sep_inv, factor, widths, patterns, dinv):
    own_rows, order = sep_inv.shape
    if own_rows == TILE and order == DEVICES * TILE:
        high, low = planned_blocks(sep_inv, patterns)
    else:
        high, low = assemble_full(patterns, lax.all_gather(sep_inv, "pr", axis=0, tiled=True))
    return products(widths, high, low, factor, dinv)


def solution(mesh):
    placed = (
        P(("cfg", "pr"), None),
        P("cfg", "pr"),
        P("pr", None),
        P("pr", None),
        P(("cfg", "pr")),
    )
    return jax.shard_map(
        shards,
        mesh=mesh,
        in_specs=placed,
        out_specs=(P("cfg", "pr"), P(("cfg", "pr"))),
        check_vma=False,
    )
```

```python
import functools

import jax
import jax.numpy as jnp
from jax import lax
from jax.experimental import pallas as pl
from jax.experimental.pallas import tpu as pltpu
from jax.sharding import PartitionSpec as P

TILE = 128
HALF = TILE // 2
MIB = 1024 * 1024

ORDER = (0, 2, 1, 3, 4, 6, 5, 7)
PIECES = {
    "near": (2, True, (4, 6, 5, 7, 1, 3)),
    "side": (1, True, (3, 4, 6, 5, 7)),
    "mid": (4, True, (6, 5, 7)),
    "side_near": (3, True, (5, 7, 4, 6)),
    "far": (6, True, ()),
    "side_mid": (5, True, (7,)),
    "side_far": (7, True, ()),
    "far_rest": (6, False, (5, 7)),
}
ROUNDS = (("near", "side"), ("mid", "side_near", "far"), ("side_mid", "side_far", "far_rest"))
KINDS = ("rows",) + tuple(PIECES)
DEVICES = 16
CLASSES = DEVICES // 2


def class_of(device, seen_from):
    place, here = device >> 2, seen_from >> 2
    outer = ((place >> 1) ^ place ^ 1) & 1
    z = jnp.where((place ^ here) >> 1 != 0, 2 + outer, (place ^ here) & 1)
    return 2 * z + (((device ^ seen_from) >> 1) & 1)


def device_of(column, seen_from, core):
    here, z = seen_from >> 2, column >> 1
    half = (here >> 1) ^ (z >> 1)
    inner_first = half ^ 1 ^ (z & 1)
    place = 2 * half + (inner_first if z >= 2 else (here & 1) ^ z)
    return 4 * place + 2 * (((seen_from >> 1) & 1) ^ (column & 1)) + core


def piece_rows(*names):
    return sum((TILE + HALF if PIECES[name][1] else 0) + 2 * TILE * len(PIECES[name][2]) for name in names)


def piece_table():
    table = [0] * (CLASSES * CLASSES)
    for name, (owner, own, classes) in PIECES.items():
        kind = KINDS.index(name)
        for place, column in enumerate(classes):
            table[owner * CLASSES + column] = kind * 64 + (3 if own else 0) + 4 * place
        if own:
            table[owner * CLASSES + owner] = kind * 64 + 2
    return jnp.array(table, jnp.int32)


def call(kernel, name, given, out_shape, out_specs, after=(), vmem=6, cost=0, **more):
    places = {"smem": pltpu.SMEM, "vmem": pltpu.VMEM, "any": pl.ANY}
    arrays = [pltpu.with_memory_space_constraint(x, pltpu.VMEM) if space == "vmem" else x for space, x in given]
    inputs = len(given)

    def body(*refs):
        kernel(*refs[:inputs], *refs[inputs + len(after) :])

    return pl.pallas_call(
        body,
        out_shape=out_shape,
        in_specs=[pl.BlockSpec(memory_space=places[space]) for space, _ in given] + [pl.BlockSpec(memory_space=pl.ANY)] * len(after),
        out_specs=out_specs,
        compiler_params=pltpu.CompilerParams(vmem_limit_bytes=vmem * MIB),
        cost_estimate=pl.CostEstimate(flops=0, bytes_accessed=cost, transcendentals=0),
        name=name,
        **more,
    )(*arrays, *after)


SMEM = pl.BlockSpec(memory_space=pltpu.SMEM)
VMEM = pl.BlockSpec(memory_space=pltpu.VMEM)
US = 3_000_000


def split(value):
    high = value.astype(jnp.bfloat16)
    low = (value - high.astype(jnp.float32)).astype(jnp.bfloat16)
    return high, low


def pack_kernel(sets, me_ref, rows_ref, *packed_refs):
    me = me_ref[0]

    def tile(q):
        return rows_ref[:, pl.ds(pl.multiple_of(q * TILE, TILE), TILE)]

    diagonal, pair = tile(me), tile(me ^ 1)
    half = jnp.where(me % 2 == 0, pair[:HALF, :], pair.T[HALF:, :])
    for names, packed_ref in zip(sets, packed_refs, strict=True):
        row = 0
        for name in names:
            owner, own, classes = PIECES[name]
            receiver = device_of(owner, me, 0) if owner < 4 else me ^ 12
            if own:
                packed_ref[row : row + TILE, :] = diagonal
                packed_ref[row + TILE : row + TILE + HALF, :] = half
                row += TILE + HALF
            for column in classes:
                for core in range(2):
                    packed_ref[row : row + TILE, :] = tile(device_of(column, receiver, core))
                    row += TILE


def pack(sets, me, sep_rows):
    return call(
        functools.partial(pack_kernel, sets),
        "pack",
        [("smem", me), ("vmem", sep_rows)],
        [pltpu.VMEM((piece_rows(*names), TILE), jnp.float32) for names in sets],
        [VMEM] * len(sets),
    )


def jobs_kernel(nodes, sides, me_ref, table_ref, patterns_ref, jobs_ref, count_ref):
    me = me_ref[0]
    ranks = sum(ORDER.index(c) << (3 * c) for c in range(CLASSES))
    for s in range(2 * len(KINDS)):
        count_ref[s] = 0

    def add(kind, core, code):
        slot = kind * 2 + ((core ^ me) & 1)
        at = count_ref[slot]
        jobs_ref[slot, at] = code
        count_ref[slot] = at + 1

    def one(node, _):
        tiles = [patterns_ref[node, a] for a in range(sides)]
        classes = [class_of(tile, me) for tile in tiles]
        order = [(ranks >> (3 * c)) & 7 for c in classes]
        for a in range(sides):
            r, c = tiles[a], classes[a]
            entry = table_ref[c * CLASSES + c]
            first = jnp.where(c == 0, r, 0)
            add(entry // 64, r & 1, (((first * nodes + node) * sides + a) * sides + a) * 2)
        for a in range(sides):
            for b in range(a + 1, sides):
                turned = jnp.where(classes[a] == classes[b], (tiles[a] & 1) == 1, order[a] > order[b])
                r, q = jnp.where(turned, tiles[b], tiles[a]), jnp.where(turned, tiles[a], tiles[b])
                c, d = jnp.where(turned, classes[b], classes[a]), jnp.where(turned, classes[a], classes[b])
                i, j = jnp.where(turned, b, a), jnp.where(turned, a, b)
                entry = table_ref[c * CLASSES + d]
                halved = (c == d) & (c != 0)
                first = entry % 64 + jnp.where(halved, 0, 2 * (q & 1))
                first = jnp.where(c == 0, q, first)
                code = (((first * nodes + node) * sides + i) * sides + j) * 2 + halved.astype(jnp.int32)
                add(entry // 64, r & 1, code)

                @pl.when(halved)
                def _():
                    add(entry // 64, q & 1, code)

        return 0

    lax.fori_loop(0, nodes, one, 0)


def place(high_ref, low_ref, node, a, b, high, low):
    rows = pl.ds(pl.multiple_of(a * TILE, TILE), TILE)
    cols = pl.ds(pl.multiple_of(b * TILE, TILE), TILE)
    high_ref[node, rows, cols] = high
    low_ref[node, rows, cols] = low


def assemble_kernel(sets, nodes, sides, me_ref, jobs_ref, count_ref, *refs):
    sources, (high_ref, low_ref) = refs[:-2], refs[-2:]
    mine = me_ref[0] & 1

    def work(name, other, source, start):
        slot = KINDS.index(name) * 2 + other
        core = mine ^ other

        def one(i, _):
            code = jobs_ref[slot, i]
            halved, code = code % 2, code // 2
            b, code = code % sides, code // sides
            a, code = code % sides, code // sides
            node, first = code % nodes, code // nodes

            @pl.when(halved == 0)
            def _():
                if name == "rows":
                    value = source[:, pl.ds(pl.multiple_of(first * TILE, TILE), TILE)]
                else:
                    value = source[pl.ds(pl.multiple_of(start + first * HALF, HALF), TILE), :]
                high, low = split(value)
                place(high_ref, low_ref, node, a, b, high, low)

                @pl.when(a != b)
                def _():
                    high, low = split(value.T)
                    place(high_ref, low_ref, node, b, a, high, low)

            if name == "rows" or not PIECES[name][1]:
                return 0

            @pl.when(halved == 1)
            def _():
                value = source[pl.ds(pl.multiple_of(start + first * HALF, HALF), HALF), :]
                high, low = split(value)
                rows = pl.ds(pl.multiple_of(a * TILE + core * HALF, HALF), HALF)
                cols = pl.ds(pl.multiple_of(b * TILE, TILE), TILE)
                high_ref[node, rows, cols] = high
                low_ref[node, rows, cols] = low
                rows = pl.ds(pl.multiple_of(b * TILE, TILE), TILE)
                cols = pl.ds(pl.multiple_of(a * TILE, TILE), TILE)
                for ref, part in zip((high_ref, low_ref), split(value.T), strict=True):
                    old = ref[node, rows, cols]
                    both = jnp.concatenate([part, part], axis=1)
                    column = lax.broadcasted_iota(jnp.int32, both.shape, 1)
                    ref[node, rows, cols] = jnp.where(column // HALF == core, both, old)

            return 0

        lax.fori_loop(0, count_ref[slot], one, 0)

    at = 0
    for names in sets:
        start = 0
        for name in names:
            for other in range(2):
                work(name, other, sources[at + other], start)
            start += 0 if name == "rows" else piece_rows(name)
        at += 2


def assemble(sets, me, jobs, count, patterns, sources, blocks, after=()):
    nodes, sides = patterns.shape
    side = sides * TILE
    given = [("smem", me), ("smem", jobs), ("smem", count)]
    given += [("vmem", x) for x in (*sources, *blocks)]
    return call(
        functools.partial(assemble_kernel, sets, nodes, sides),
        "assemble_" + sets[0][0],
        given,
        [pltpu.VMEM((nodes, side, side), jnp.bfloat16)] * 2,
        [VMEM] * 2,
        after,
        input_output_aliases={len(given) - len(blocks) + i: i for i in range(len(blocks))},
    )


def assemble_full_kernel(nodes, sides, patterns_ref, whole_ref, high_ref, low_ref):
    def one(step, _):
        node = step // (sides * sides)
        a = lax.rem(step // sides, sides)
        b = lax.rem(step, sides)
        rows = pl.ds(pl.multiple_of(patterns_ref[node, a] * TILE, TILE), TILE)
        cols = pl.ds(pl.multiple_of(patterns_ref[node, b] * TILE, TILE), TILE)
        high, low = split(whole_ref[rows, cols])
        place(high_ref, low_ref, node, a, b, high, low)
        return 0

    lax.fori_loop(0, nodes * sides * sides, one, 0)


def assemble_full(patterns, source):
    nodes, sides = patterns.shape
    side = sides * TILE
    return call(
        functools.partial(assemble_full_kernel, nodes, sides),
        "assemble_full",
        [("smem", patterns), ("vmem", source)],
        [pltpu.VMEM((nodes, side, side), jnp.bfloat16)] * 2,
        [VMEM] * 2,
    )


def halves_kernel(factor_ref, high_ref, low_ref):
    step = 4 * TILE
    for start in range(0, factor_ref.shape[1], step):
        where = slice(start, start + step)
        high_ref[:, where], low_ref[:, where] = split(factor_ref[:, where])


def factor_halves(factor, after=()):
    out = [pltpu.VMEM(factor.shape, jnp.bfloat16)] * 2
    return call(halves_kernel, "factor_halves", [("vmem", factor)], out, [VMEM] * 2, after)


def product_kernel(nodes, widths_ref, high_ref, low_ref, f_high_ref, f_low_ref, dinv_ref, out_ref, marg_ref, product_ref, sems):
    rows, cols = product_ref.shape
    step = 2 * TILE
    dot = functools.partial(jnp.dot, preferred_element_type=jnp.float32)

    def node_of(tile):
        node, end = 0, 0
        for j in range(nodes):
            end = end + widths_ref[0, j]
            node = node + (tile >= end).astype(jnp.int32)
        return jnp.minimum(node, nodes - 1)

    def columns(node, tile, count):
        where = pl.ds(pl.multiple_of(tile * TILE, TILE), count * TILE)
        high, low = high_ref[node], low_ref[node]
        f_high, f_low = f_high_ref[:, where], f_low_ref[:, where]
        product = -(dot(high, f_high) + (dot(high, f_low) + dot(low, f_high)))
        product_ref[:, where] = product
        factor = f_high.astype(jnp.float32) + f_low.astype(jnp.float32)
        total = jnp.sum(factor * product, axis=0, keepdims=True)
        for k in range(count):
            row = pl.ds(tile + k, 1)
            marg_ref[row, :] = dinv_ref[row, :] - total[:, k * TILE : (k + 1) * TILE]

    def write(pair):
        where = pl.ds(pl.multiple_of(pair * step, step), step)
        return pltpu.make_async_copy(product_ref.at[:, where], out_ref.at[:, where], sems.at[pair])

    def one(pair, _):
        first, second = node_of(2 * pair), node_of(2 * pair + 1)

        @pl.when(first == second)
        def _():
            columns(first, 2 * pair, 2)

        @pl.when(first != second)
        def _():
            columns(first, 2 * pair, 1)
            columns(second, 2 * pair + 1, 1)

        write(pair).start()
        return 0

    def finish(pair, _):
        write(pair).wait()
        return 0

    lax.fori_loop(0, cols // step, one, 0)
    lax.fori_loop(0, cols // step, finish, 0)


def products(widths, blocks, factors, dinv):
    rows, cols = factors[0].shape
    nodes = widths.shape[1]
    pairs = cols // (2 * TILE)
    given = [("smem", widths)] + [("vmem", part) for part in (*blocks, *factors)] + [("vmem", dinv.reshape(cols // TILE, TILE))]
    out, marg = call(
        functools.partial(product_kernel, nodes),
        "products",
        given,
        [jax.ShapeDtypeStruct((rows, cols), jnp.float32), jax.ShapeDtypeStruct((cols // TILE, TILE), jnp.float32)],
        [pl.BlockSpec(memory_space=pl.ANY), VMEM],
        vmem=14,
        cost=9 * US,
        scratch_shapes=[pltpu.VMEM((rows, cols), jnp.float32), pltpu.SemaphoreType.DMA((pairs,))],
    )
    return out, marg.reshape(cols)


def swap(value, mask):
    return lax.ppermute(value, "pr", [(i, i ^ mask) for i in range(DEVICES)])


def move(value, places):
    pairs = [(4 * old + k, 4 * new + k) for old, new in places.items() for k in range(4)]
    return lax.ppermute(value, "pr", pairs)


def plan_jobs(me, patterns, after):
    nodes, sides = patterns.shape
    shapes = [
        jax.ShapeDtypeStruct((2 * len(KINDS), nodes * sides), jnp.int32),
        jax.ShapeDtypeStruct((2 * len(KINDS),), jnp.int32),
    ]
    given = [("smem", me), ("smem", piece_table()), ("smem", patterns)]
    return call(functools.partial(jobs_kernel, nodes, sides), "plan_jobs", given, shapes, [SMEM] * 2, after)


def turn(name, kernel, me, given, rows, held, after=()):
    shapes = [pltpu.VMEM((n, TILE), jnp.float32) for n in rows] + [pltpu.VMEM(x.shape, x.dtype) for x in held]

    def body(me_ref, *refs):
        place = me_ref[0] >> 2
        kernel((place == 1) | (place == 2), *refs[: len(given)], *refs[len(given) + len(held) :][: len(rows)])

    inputs = [("smem", me)] + [("vmem", x) for x in (*given, *held)]
    aliases = {1 + len(given) + i: len(rows) + i for i in range(len(held))}
    return call(body, name, inputs, shapes, [VMEM] * len(shapes), after, input_output_aliases=aliases)


def copy_rows(target_ref, row, source_ref, first=0, count=None):
    count = source_ref.shape[0] - first if count is None else count
    target_ref[row : row + count, :] = source_ref[first : first + count, :]
    return row + count


def turn_1(inner, near_ref, side_ref, first_ref, part_ref, held_ref, far_ref, far_first_ref):
    copy_rows(part_ref, 0, near_ref, 0, part_ref.shape[0])
    copy_rows(held_ref, copy_rows(held_ref, 0, near_ref), side_ref)
    first, rest = piece_rows("far"), piece_rows("far_rest")
    copy_rows(far_ref, 0, near_ref, 0, first)
    copy_rows(far_ref, first, near_ref, near_ref.shape[0] - rest, rest)
    copy_rows(far_first_ref, 0, first_ref)


def turn_2(inner, mid_ref, mid_outer_ref, far_ref, far_outer_ref, side_near_ref, part_ref, held_ref, rest_ref):
    mid, far, onward = piece_rows("mid"), piece_rows("far"), piece_rows("side_mid")

    def take(m_ref, f_ref):
        copy_rows(part_ref, copy_rows(part_ref, 0, m_ref, 0, onward), f_ref, 0, far)
        copy_rows(held_ref, 0, m_ref)
        copy_rows(held_ref, mid + side_near_ref.shape[0], f_ref, 0, far)

    pl.when(inner)(lambda: take(mid_ref, far_ref))
    pl.when(jnp.logical_not(inner))(lambda: take(mid_outer_ref, far_outer_ref))
    copy_rows(held_ref, mid, side_near_ref)
    copy_rows(rest_ref, 0, far_ref, far)


def turn_3(inner, side_last_ref, rest_ref, rest_outer_ref, held_ref):
    row = copy_rows(held_ref, 0, side_last_ref)

    def take(ref):
        copy_rows(held_ref, row, ref)

    pl.when(inner)(lambda: take(rest_ref))
    pl.when(jnp.logical_not(inner))(lambda: take(rest_outer_ref))


def planned_blocks(sep_inv, factor, patterns):
    me = lax.axis_index("pr").astype(jnp.int32).reshape(1)
    between_inner, outward, between_outer = {1: 2, 2: 1}, {1: 0, 2: 3}, {0: 3, 3: 0}

    near, side, mid, first = pack((("near",), ("side",), ("mid",), ("far",)), me, sep_inv)
    rows_other = swap(sep_inv, 1)
    near, side, mid = swap(near, 4), swap(side, 2), move(mid, between_inner)
    jobs, count = plan_jobs(me, patterns, (rows_other,))
    rows = (piece_rows("side_near"), piece_rows(*ROUNDS[0]), piece_rows("far", "far_rest"), piece_rows("far"))
    part, held, far, first, mid = turn("turn_1", turn_1, me, (near, side, first), rows, (mid,), (count,))

    def put(sets, sources, blocks):
        return assemble(sets, me, jobs, count, patterns, sources, blocks)

    side_near, mid_outer = swap(part, 2), move(mid, outward)
    far, far_outer = move(far, between_inner), move(first, between_outer)
    blocks = put((("rows",), ROUNDS[0]), (sep_inv, rows_other, held, swap(held, 1)), ())
    rows = (piece_rows("side_mid", "side_far"), piece_rows(*ROUNDS[1]), piece_rows("far_rest"))
    part, held, rest = turn("turn_2", turn_2, me, (mid, mid_outer, far, far_outer, side_near), rows, (), blocks[:1])

    side_last, rest_outer = swap(part, 2), move(rest, outward)
    blocks = put(ROUNDS[1:2], (held, swap(held, 1)), blocks)
    factors = factor_halves(factor, blocks[:1])
    (held,) = turn("turn_3", turn_3, me, (side_last, rest, rest_outer), (piece_rows(*ROUNDS[2]),), (), factors[:1])
    return put(ROUNDS[2:], (held, swap(held, 1)), blocks), factors


def shards(sep_inv, factor, widths, patterns, dinv):
    own_rows, order = sep_inv.shape
    if own_rows == TILE and order == DEVICES * TILE:
        blocks, factors = planned_blocks(sep_inv, factor, patterns)
    else:
        factors = factor_halves(factor)
        blocks = assemble_full(patterns, lax.all_gather(sep_inv, "pr", axis=0, tiled=True))
    return products(widths, blocks, factors, dinv)


def solution(mesh):
    placed = (
        P(("cfg", "pr"), None),
        P("cfg", "pr"),
        P("pr", None),
        P("pr", None),
        P(("cfg", "pr")),
    )
    return jax.shard_map(
        shards,
        mesh=mesh,
        in_specs=placed,
        out_specs=(P("cfg", "pr"), P(("cfg", "pr"))),
        check_vma=False,
    )
```

```python
import functools

import jax
import jax.numpy as jnp
from jax import lax
from jax.experimental import pallas as pl
from jax.experimental.pallas import tpu as pltpu
from jax.sharding import PartitionSpec as P

TILE = 128
HALF = TILE // 2
MIB = 1024 * 1024

ORDER = (0, 2, 1, 3, 4, 6, 5, 7)
PIECES = {
    "near": (2, True, (4, 6, 5, 7, 1, 3)),
    "side": (1, True, (3, 4, 6, 5, 7)),
    "mid": (4, True, (6, 5, 7)),
    "side_near": (3, True, (5, 7, 4, 6)),
    "far": (6, True, ()),
    "side_mid": (5, True, (7,)),
    "side_far": (7, True, ()),
    "far_rest": (6, False, (5, 7)),
}
ROUNDS = (("near", "side"), ("mid", "side_near", "far"), ("side_mid", "side_far", "far_rest"))
KINDS = ("rows",) + tuple(PIECES)
DEVICES = 16
LISTS = 6
WHOLE = (0, 0, 0, 1, 1, 2, 2, 2)
CLASSES = DEVICES // 2


def class_of(device, seen_from):
    place, here = device >> 2, seen_from >> 2
    outer = ((place >> 1) ^ place ^ 1) & 1
    z = jnp.where((place ^ here) >> 1 != 0, 2 + outer, (place ^ here) & 1)
    return 2 * z + (((device ^ seen_from) >> 1) & 1)


def device_of(column, seen_from, core):
    here, z = seen_from >> 2, column >> 1
    half = (here >> 1) ^ (z >> 1)
    inner_first = half ^ 1 ^ (z & 1)
    place = 2 * half + (inner_first if z >= 2 else (here & 1) ^ z)
    return 4 * place + 2 * (((seen_from >> 1) & 1) ^ (column & 1)) + core


def piece_rows(*names):
    return sum((TILE + HALF if PIECES[name][1] else 0) + 2 * TILE * len(PIECES[name][2]) for name in names)


def piece_table():
    table = [0] * (CLASSES * CLASSES)
    for name, (owner, own, classes) in PIECES.items():
        kind = KINDS.index(name)
        for place, column in enumerate(classes):
            table[owner * CLASSES + column] = kind * 64 + (3 if own else 0) + 4 * place
        if own:
            table[owner * CLASSES + owner] = kind * 64 + 2
    return jnp.array(table, jnp.int32)


def call(kernel, name, given, out_shape, out_specs, after=(), vmem=6, cost=0, **more):
    places = {"smem": pltpu.SMEM, "vmem": pltpu.VMEM, "any": pl.ANY}
    arrays = [pltpu.with_memory_space_constraint(x, pltpu.VMEM) if space == "vmem" else x for space, x in given]
    inputs = len(given)

    def body(*refs):
        kernel(*refs[:inputs], *refs[inputs + len(after) :])

    return pl.pallas_call(
        body,
        out_shape=out_shape,
        in_specs=[pl.BlockSpec(memory_space=places[space]) for space, _ in given] + [pl.BlockSpec(memory_space=pl.ANY)] * len(after),
        out_specs=out_specs,
        compiler_params=pltpu.CompilerParams(vmem_limit_bytes=vmem * MIB),
        cost_estimate=pl.CostEstimate(flops=0, bytes_accessed=cost, transcendentals=0),
        name=name,
        **more,
    )(*arrays, *after)


SMEM = pl.BlockSpec(memory_space=pltpu.SMEM)
VMEM = pl.BlockSpec(memory_space=pltpu.VMEM)
US = 3_000_000


def split(value):
    high = value.astype(jnp.bfloat16)
    low = (value - high.astype(jnp.float32)).astype(jnp.bfloat16)
    return high, low


def pack_kernel(sets, me_ref, rows_ref, *packed_refs):
    me = me_ref[0]

    def tile(q):
        return rows_ref[:, pl.ds(pl.multiple_of(q * TILE, TILE), TILE)]

    diagonal, pair = tile(me), tile(me ^ 1)
    half = jnp.where(me % 2 == 0, pair[:HALF, :], pair.T[HALF:, :])
    for names, packed_ref in zip(sets, packed_refs, strict=True):
        row = 0
        for name in names:
            owner, own, classes = PIECES[name]
            receiver = device_of(owner, me, 0) if owner < 4 else me ^ 12
            if own:
                packed_ref[row : row + TILE, :] = diagonal
                packed_ref[row + TILE : row + TILE + HALF, :] = half
                row += TILE + HALF
            for column in classes:
                for core in range(2):
                    packed_ref[row : row + TILE, :] = tile(device_of(column, receiver, core))
                    row += TILE


def pack(sets, me, sep_rows):
    return call(
        functools.partial(pack_kernel, sets),
        "pack",
        [("smem", me), ("vmem", sep_rows)],
        [pltpu.VMEM((piece_rows(*names), TILE), jnp.float32) for names in sets],
        [VMEM] * len(sets),
    )


def jobs_kernel(nodes, sides, me_ref, table_ref, patterns_ref, jobs_ref, count_ref, slots_ref):
    me = me_ref[0]
    ranks = sum(ORDER.index(c) << (3 * c) for c in range(CLASSES))
    phases = sum(WHOLE[c] << (2 * c) for c in range(CLASSES))
    for s in range(LISTS * len(KINDS)):
        count_ref[s] = 0

    def one(node, _):
        tiles = [patterns_ref[node, a] for a in range(sides)]
        classes = [class_of(tile, me) for tile in tiles]
        order = [(ranks >> (3 * c)) & 7 for c in classes]
        phase = [(phases >> (2 * c)) & 3 for c in classes]
        slots = []
        for a in range(sides):
            slot = sum(((phase[b] < phase[a]) if b > a else (phase[b] <= phase[a])).astype(jnp.int32) for b in range(sides) if b != a)
            slots_ref[0, node * sides + a] = slot
            slots_ref[1, node * sides + slot] = a
            slots.append(slot)
        for p in range(len(ROUNDS)):
            slots_ref[2 + p, node] = sum((phase[a] == p).astype(jnp.int32) for a in range(sides))

        def add(which, first, i, j):
            at = count_ref[which]
            code = (first * nodes + node) * sides + i
            jobs_ref[which, at] = ((code * sides + j) * sides + pick(slots, i)) * sides + pick(slots, j)
            count_ref[which] = at + 1

        def pick(values, i):
            value = values[0]
            for k in range(1, sides):
                value = jnp.where(i == k, values[k], value)
            return value

        for a in range(sides):
            r, c = tiles[a], classes[a]
            entry = table_ref[c * CLASSES + c]
            first = jnp.where(c == 0, r, 0)
            add(((entry >> 6) * 2 + ((r ^ me) & 1)) * 3 + 1, first, jnp.int32(a), jnp.int32(a))
        for a in range(sides):
            for b in range(a + 1, sides):
                turned = jnp.where(classes[a] == classes[b], (tiles[a] & 1) == 1, order[a] > order[b])
                r, q = jnp.where(turned, tiles[b], tiles[a]), jnp.where(turned, tiles[a], tiles[b])
                c, d = jnp.where(turned, classes[b], classes[a]), jnp.where(turned, classes[a], classes[b])
                i, j = jnp.where(turned, b, a), jnp.where(turned, a, b)
                entry = table_ref[c * CLASSES + d]
                halved = (c == d) & (c != 0)
                first = (entry & 63) + jnp.where(halved, 0, 2 * (q & 1))
                first = jnp.where(c == 0, q, first)
                which = ((entry >> 6) * 2 + jnp.where(halved, 0, (r ^ me) & 1)) * 3 + jnp.where(halved, 2, 0)
                add(which, first, i, j)

        return 0

    lax.fori_loop(0, nodes, one, 0)


def place(high_ref, low_ref, node, a, b, value):
    rows = pl.ds(pl.multiple_of(a * TILE, TILE), TILE)
    cols = pl.ds(pl.multiple_of(b * TILE, TILE), TILE)
    high_ref[node, rows, cols], low_ref[node, rows, cols] = split(value)


def assemble_kernel(sets, nodes, sides, me_ref, jobs_ref, count_ref, slots_ref, *refs):
    sources, (high_ref, low_ref) = refs[:-2], refs[-2:]
    even = (me_ref[0] & 1) == 0

    def work(name, pair, start):
        def read(which, sort, i):
            code = jobs_ref[which, i]
            fields = []
            for size in (sides, sides, sides, sides, nodes):
                fields.append(lax.rem(code, size))
                code = lax.div(code, size)
            slot_j, slot_i, j, i, node = fields
            other = (which // 3) % 2
            if name == "rows":
                value = pair[other][:, pl.ds(pl.multiple_of(code * TILE, TILE), TILE)]
            elif sort == 2:
                rows = pl.ds(pl.multiple_of(start + code * HALF, HALF), HALF)
                mine, theirs = pair[0][rows, :], pair[1][rows, :]
                value = jnp.concatenate([jnp.where(even, mine, theirs), jnp.where(even, theirs, mine)], axis=0)
            else:
                value = pair[other][pl.ds(pl.multiple_of(start + code * HALF, HALF), TILE), :]
            return node, i, j, slot_i, slot_j, value

        def put(sort, node, i, j, slot_i, slot_j, value):
            place(high_ref, low_ref, node, slot_i, j, value)
            if sort != 1:
                place(high_ref, low_ref, node, slot_j, i, value.T)

        for other in range(2):
            for sort in range(3):
                which = (KINDS.index(name) * 2 + other) * 3 + sort
                if sort == 2 and (other == 1 or name == "rows" or not PIECES[name][1]) or sort == 1 and name == "far_rest":
                    continue
                if sort == 0 and name != "rows" and not PIECES[name][2]:
                    continue
                number = count_ref[which]

                def two(i, _):
                    first, second = read(which, sort, 2 * i), read(which, sort, 2 * i + 1)
                    put(sort, *first)
                    put(sort, *second)
                    return 0

                lax.fori_loop(0, lax.div(number, 2), two, 0)

                @pl.when(lax.rem(number, 2) == 1)
                def _():
                    put(sort, *read(which, sort, number - 1))

    at = 0
    for names in sets:
        start = 0
        for name in names:
            work(name, sources[at : at + 2], start)
            start += 0 if name == "rows" else piece_rows(name)
        at += 2


def assemble(sets, me, plan, patterns, sources, blocks, after=()):
    nodes, sides = patterns.shape
    side = sides * TILE
    given = [("smem", x) for x in (me, *plan)] + [("vmem", x) for x in (*sources, *blocks)]
    return call(
        functools.partial(assemble_kernel, sets, nodes, sides),
        "assemble_" + sets[0][0],
        given,
        [pltpu.VMEM((nodes, side, side), jnp.bfloat16)] * 2,
        [VMEM] * 2,
        after,
        input_output_aliases={len(given) - len(blocks) + i: i for i in range(len(blocks))},
    )


def assemble_full_kernel(nodes, sides, patterns_ref, whole_ref, high_ref, low_ref):
    def one(step, _):
        node = step // (sides * sides)
        a = lax.rem(step // sides, sides)
        b = lax.rem(step, sides)
        rows = pl.ds(pl.multiple_of(patterns_ref[node, a] * TILE, TILE), TILE)
        cols = pl.ds(pl.multiple_of(patterns_ref[node, b] * TILE, TILE), TILE)
        place(high_ref, low_ref, node, a, b, whole_ref[rows, cols])
        return 0

    lax.fori_loop(0, nodes * sides * sides, one, 0)


def assemble_full(patterns, source):
    nodes, sides = patterns.shape
    side = sides * TILE
    return call(
        functools.partial(assemble_full_kernel, nodes, sides),
        "assemble_full",
        [("smem", patterns), ("vmem", source)],
        [pltpu.VMEM((nodes, side, side), jnp.bfloat16)] * 2,
        [VMEM] * 2,
    )


def halves_kernel(factor_ref, high_ref, low_ref):
    step = 4 * TILE
    for start in range(0, factor_ref.shape[1], step):
        where = slice(start, start + step)
        high_ref[:, where], low_ref[:, where] = split(factor_ref[:, where])


def factor_halves(factor, after=()):
    out = [pltpu.VMEM(factor.shape, jnp.bfloat16)] * 2
    return call(halves_kernel, "factor_halves", [("vmem", factor)], out, [VMEM] * 2, after)


def product_kernel(nodes, sides, phase, widths_ref, slots_ref, high_ref, low_ref, f_high_ref, f_low_ref, before_ref, *refs):
    out_ref, marg_ref, product_ref, sems = refs[-4:]
    dot = functools.partial(jnp.dot, preferred_element_type=jnp.float32)
    most = 4
    marg_ref[...] = before_ref[...]

    def tile_rows(node, slot):
        return pl.ds(pl.multiple_of(slots_ref[1, node * sides + slot] * TILE, TILE), TILE)

    def copies(node, first, tile, height, width):
        cols = pl.ds(pl.multiple_of(tile * TILE, TILE), width * TILE)
        for i in range(height):
            rows = tile_rows(node, first + i)
            yield pltpu.make_async_copy(product_ref.at[rows, cols], out_ref.at[rows, cols], sems.at[tile, i])

    def multiply(node, first, tile, height, width):
        cols = pl.ds(pl.multiple_of(tile * TILE, TILE), width * TILE)
        rows = pl.ds(pl.multiple_of(first * TILE, TILE), height * TILE)
        high, low = high_ref[node, rows, :], low_ref[node, rows, :]
        f_high, f_low = f_high_ref[:, cols], f_low_ref[:, cols]
        product = -(dot(high, f_high) + (dot(high, f_low) + dot(low, f_high)))
        total = jnp.zeros((1, width * TILE), jnp.float32)
        for i in range(height):
            part = product[i * TILE : (i + 1) * TILE, :]
            here = tile_rows(node, first + i)
            product_ref[here, cols] = part
            factor = f_high_ref[here, cols].astype(jnp.float32) + f_low_ref[here, cols].astype(jnp.float32)
            total = total + jnp.sum(factor * part, axis=0, keepdims=True)
        for k in range(width):
            row = pl.ds(tile + k, 1)
            marg_ref[row, :] = marg_ref[row, :] - total[:, k * TILE : (k + 1) * TILE]
        for copy in copies(node, first, tile, height, width):
            copy.start()

    def finish(*place):
        for copy in copies(*place):
            copy.wait()

    def each(step):
        def one(node, start):
            width = widths_ref[0, node]
            first, height = sum((slots_ref[2 + p, node] for p in range(phase)), 0), slots_ref[2 + phase, node]
            for h in range(1, sides + 1):

                @pl.when(height == h)
                def _():
                    def whole(i, _):
                        step(node, first, start + most * i, h, most)
                        return 0

                    lax.fori_loop(0, width // most, whole, 0)
                    rest = width % most
                    for w in range(1, most):
                        pl.when(rest == w)(lambda: step(node, first, start + width - rest, h, w))

            return start + width

        lax.fori_loop(0, nodes, one, 0)

    each(multiply)
    each(finish)


def products(phase, widths, slots, blocks, factors, before, out=()):
    rows, cols = factors[0].shape
    nodes, sides = widths.shape[1], rows // TILE
    given = [("smem", widths), ("smem", slots)]
    given += [("vmem", x) for x in (*blocks, *factors, before)] + [("any", x) for x in out]
    return call(
        functools.partial(product_kernel, nodes, sides, phase),
        f"products_{phase}",
        given,
        [jax.ShapeDtypeStruct((rows, cols), jnp.float32), jax.ShapeDtypeStruct((cols // TILE, TILE), jnp.float32)],
        [pl.BlockSpec(memory_space=pl.ANY), VMEM],
        vmem=14,
        scratch_shapes=[pltpu.VMEM((rows, cols), jnp.float32), pltpu.SemaphoreType.DMA((cols // TILE, sides))],
        input_output_aliases={len(given) - 1: 0} if out else {},
    )


def swap(value, mask):
    return lax.ppermute(value, "pr", [(i, i ^ mask) for i in range(DEVICES)])


def move(value, places):
    pairs = [(4 * old + k, 4 * new + k) for old, new in places.items() for k in range(4)]
    return lax.ppermute(value, "pr", pairs)


def plan_jobs(me, patterns, after):
    nodes, sides = patterns.shape
    shapes = [
        jax.ShapeDtypeStruct((LISTS * len(KINDS), nodes * sides), jnp.int32),
        jax.ShapeDtypeStruct((LISTS * len(KINDS),), jnp.int32),
        jax.ShapeDtypeStruct((2 + len(ROUNDS), nodes * sides), jnp.int32),
    ]
    given = [("smem", me), ("smem", piece_table()), ("smem", patterns)]
    return call(functools.partial(jobs_kernel, nodes, sides), "plan_jobs", given, shapes, [SMEM] * 3, after)


def turn(name, kernel, me, given, rows, held, after=()):
    shapes = [pltpu.VMEM((n, TILE), jnp.float32) for n in rows] + [pltpu.VMEM(x.shape, x.dtype) for x in held]

    def body(me_ref, *refs):
        place = me_ref[0] >> 2
        kernel((place == 1) | (place == 2), *refs[: len(given)], *refs[len(given) + len(held) :][: len(rows)])

    inputs = [("smem", me)] + [("vmem", x) for x in (*given, *held)]
    aliases = {1 + len(given) + i: len(rows) + i for i in range(len(held))}
    return call(body, name, inputs, shapes, [VMEM] * len(shapes), after, input_output_aliases=aliases)


def copy_rows(target_ref, row, source_ref, first=0, count=None):
    count = source_ref.shape[0] - first if count is None else count
    target_ref[row : row + count, :] = source_ref[first : first + count, :]
    return row + count


def turn_1(inner, near_ref, side_ref, part_ref, held_ref, far_ref, far_first_ref):
    copy_rows(part_ref, 0, near_ref, 0, part_ref.shape[0])
    copy_rows(held_ref, copy_rows(held_ref, 0, near_ref), side_ref)
    first, rest = piece_rows("far"), piece_rows("far_rest")
    copy_rows(far_ref, 0, near_ref, 0, first)
    copy_rows(far_ref, first, near_ref, near_ref.shape[0] - rest, rest)
    copy_rows(far_first_ref, 0, near_ref, 0, first)


def turn_2(inner, mid_ref, mid_outer_ref, far_ref, far_outer_ref, side_near_ref, part_ref, held_ref, rest_ref):
    mid, far, onward = piece_rows("mid"), piece_rows("far"), piece_rows("side_mid")

    def take(m_ref, f_ref):
        copy_rows(part_ref, copy_rows(part_ref, 0, m_ref, 0, onward), f_ref, 0, far)
        copy_rows(held_ref, 0, m_ref)
        copy_rows(held_ref, mid + side_near_ref.shape[0], f_ref, 0, far)

    pl.when(inner)(lambda: take(mid_ref, far_ref))
    pl.when(jnp.logical_not(inner))(lambda: take(mid_outer_ref, far_outer_ref))
    copy_rows(held_ref, mid, side_near_ref)
    copy_rows(rest_ref, 0, far_ref, far)


def turn_3(inner, side_last_ref, rest_ref, rest_outer_ref, held_ref):
    row = copy_rows(held_ref, 0, side_last_ref)

    def take(ref):
        copy_rows(held_ref, row, ref)

    pl.when(inner)(lambda: take(rest_ref))
    pl.when(jnp.logical_not(inner))(lambda: take(rest_outer_ref))


def planned(sep_inv, factor, widths, patterns, dinv):
    me = lax.axis_index("pr").astype(jnp.int32).reshape(1)
    between_inner, outward, across = {1: 2, 2: 1}, {1: 0, 2: 3}, {1: 3, 2: 0}

    near, side, mid = pack((("near",), ("side",), ("mid",)), me, sep_inv)
    rows_other = swap(sep_inv, 1)
    near, side, mid = swap(near, 4), swap(side, 2), move(mid, between_inner)
    plan = plan_jobs(me, patterns, (rows_other,))
    factors = factor_halves(factor, plan[1:2])
    blocks = assemble((("rows",),), me, plan, patterns, (sep_inv, rows_other), (), factors[:1])
    rows = (piece_rows("side_near"), piece_rows(*ROUNDS[0]), piece_rows("far", "far_rest"), piece_rows("far"))
    part, held, far, far_first, mid = turn("turn_1", turn_1, me, (near, side), rows, (mid,), blocks[:1])

    def put(sets, sources, blocks, after=()):
        return assemble(sets, me, plan, patterns, sources, blocks, after)

    side_near, mid_outer = swap(part, 2), move(mid, outward)
    far, far_outer = move(far, between_inner), move(far_first, across)
    blocks = put(ROUNDS[:1], (held, swap(held, 1)), blocks)
    out, marg = products(0, widths, plan[2], blocks, factors, dinv)
    rows = (piece_rows("side_mid", "side_far"), piece_rows(*ROUNDS[1]), piece_rows("far_rest"))
    part, held, rest = turn("turn_2", turn_2, me, (mid, mid_outer, far, far_outer, side_near), rows, (), (marg,))

    side_last, rest_outer = swap(part, 2), move(rest, outward)
    blocks = put(ROUNDS[1:2], (held, swap(held, 1)), blocks, (marg,))
    out, marg = products(1, widths, plan[2], blocks, factors, marg, (out,))
    (held,) = turn("turn_3", turn_3, me, (side_last, rest, rest_outer), (piece_rows(*ROUNDS[2]),), (), (marg,))
    blocks = put(ROUNDS[2:], (held, swap(held, 1)), blocks, (marg,))
    return products(2, widths, plan[2], blocks, factors, marg, (out,))


def shards(sep_inv, factor, widths, patterns, dinv):
    own_rows, order = sep_inv.shape
    cols = factor.shape[1]
    dinv = dinv.reshape(cols // TILE, TILE)
    if own_rows == TILE and order == DEVICES * TILE:
        out, marg = planned(sep_inv, factor, widths, patterns, dinv)
    else:
        nodes, sides = patterns.shape
        blocks = assemble_full(patterns, lax.all_gather(sep_inv, "pr", axis=0, tiled=True))
        order = jnp.tile(jnp.arange(sides, dtype=jnp.int32), nodes)
        slots = jnp.stack([order, order, jnp.full_like(order, sides)])
        out, marg = products(0, widths, slots, blocks, factor_halves(factor), dinv)
    return out, marg.reshape(cols)


def solution(mesh):
    placed = (
        P(("cfg", "pr"), None),
        P("cfg", "pr"),
        P("pr", None),
        P("pr", None),
        P(("cfg", "pr")),
    )
    return jax.shard_map(
        shards,
        mesh=mesh,
        in_specs=placed,
        out_specs=(P("cfg", "pr"), P(("cfg", "pr"))),
        check_vma=False,
    )
```

```python
import functools

import jax
import jax.numpy as jnp
from jax import lax
from jax.experimental import pallas as pl
from jax.experimental.pallas import tpu as pltpu
from jax.sharding import PartitionSpec as P

TILE = 128
HALF = TILE // 2
MIB = 1024 * 1024

ORDER = (0, 2, 1, 3, 4, 6, 5, 7)
PIECES = {
    "near": (2, True, (4, 6, 5, 7, 1, 3)),
    "side": (1, True, (3, 4, 6, 5, 7)),
    "mid": (4, True, (6, 5, 7)),
    "side_near": (3, True, (5, 7, 4, 6)),
    "far": (6, True, ()),
    "side_mid": (5, True, (7,)),
    "side_far": (7, True, ()),
    "far_rest": (6, False, (5, 7)),
}
ROUNDS = (("near", "side"), ("mid", "side_near", "far"), ("side_mid", "side_far", "far_rest"))
KINDS = ("rows",) + tuple(PIECES)
DEVICES = 16
LISTS = 6
WHOLE = (0, 0, 0, 1, 1, 2, 2, 2)
CLASSES = DEVICES // 2


def class_of(device, seen_from):
    place, here = device >> 2, seen_from >> 2
    outer = ((place >> 1) ^ place ^ 1) & 1
    z = jnp.where((place ^ here) >> 1 != 0, 2 + outer, (place ^ here) & 1)
    return 2 * z + (((device ^ seen_from) >> 1) & 1)


def device_of(column, seen_from, core):
    here, z = seen_from >> 2, column >> 1
    half = (here >> 1) ^ (z >> 1)
    inner_first = half ^ 1 ^ (z & 1)
    place = 2 * half + (inner_first if z >= 2 else (here & 1) ^ z)
    return 4 * place + 2 * (((seen_from >> 1) & 1) ^ (column & 1)) + core


def piece_rows(*names):
    return sum((TILE + HALF if PIECES[name][1] else 0) + 2 * TILE * len(PIECES[name][2]) for name in names)


def piece_table():
    table = [0] * (CLASSES * CLASSES)
    for name, (owner, own, classes) in PIECES.items():
        kind = KINDS.index(name)
        for place, column in enumerate(classes):
            table[owner * CLASSES + column] = kind * 64 + (3 if own else 0) + 4 * place
        if own:
            table[owner * CLASSES + owner] = kind * 64 + 2
    return jnp.array(table, jnp.int32)


def call(kernel, name, given, out_shape, out_specs, after=(), vmem=6, cost=0, **more):
    places = {"smem": pltpu.SMEM, "vmem": pltpu.VMEM, "any": pl.ANY}
    arrays = [pltpu.with_memory_space_constraint(x, pltpu.VMEM) if space == "vmem" else x for space, x in given]
    inputs = len(given)

    def body(*refs):
        kernel(*refs[:inputs], *refs[inputs + len(after) :])

    return pl.pallas_call(
        body,
        out_shape=out_shape,
        in_specs=[pl.BlockSpec(memory_space=places[space]) for space, _ in given] + [pl.BlockSpec(memory_space=pl.ANY)] * len(after),
        out_specs=out_specs,
        compiler_params=pltpu.CompilerParams(vmem_limit_bytes=vmem * MIB),
        cost_estimate=pl.CostEstimate(flops=0, bytes_accessed=cost, transcendentals=0),
        name=name,
        **more,
    )(*arrays, *after)


SMEM = pl.BlockSpec(memory_space=pltpu.SMEM)
VMEM = pl.BlockSpec(memory_space=pltpu.VMEM)
US = 3_000_000


def split(value):
    high = value.astype(jnp.bfloat16)
    low = (value - high.astype(jnp.float32)).astype(jnp.bfloat16)
    return high, low


def pack_kernel(sets, me_ref, rows_ref, *packed_refs):
    me = me_ref[0]

    def tile(q):
        return rows_ref[:, pl.ds(pl.multiple_of(q * TILE, TILE), TILE)]

    diagonal, pair = tile(me), tile(me ^ 1)
    half = jnp.where(me % 2 == 0, pair[:HALF, :], pair.T[HALF:, :])
    for names, packed_ref in zip(sets, packed_refs, strict=True):
        row = 0
        for name in names:
            owner, own, classes = PIECES[name]
            receiver = device_of(owner, me, 0) if owner < 4 else me ^ 12
            if own:
                packed_ref[row : row + TILE, :] = diagonal
                packed_ref[row + TILE : row + TILE + HALF, :] = half
                row += TILE + HALF
            for column in classes:
                for core in range(2):
                    packed_ref[row : row + TILE, :] = tile(device_of(column, receiver, core))
                    row += TILE


def pack(sets, me, sep_rows):
    return call(
        functools.partial(pack_kernel, sets),
        "pack",
        [("smem", me), ("vmem", sep_rows)],
        [pltpu.VMEM((piece_rows(*names), TILE), jnp.float32) for names in sets],
        [VMEM] * len(sets),
    )


def jobs_kernel(nodes, sides, me_ref, table_ref, patterns_ref, jobs_ref, count_ref, slots_ref):
    me = me_ref[0]
    ranks = sum(ORDER.index(c) << (3 * c) for c in range(CLASSES))
    phases = sum(WHOLE[c] << (2 * c) for c in range(CLASSES))
    for s in range(LISTS * len(KINDS)):
        count_ref[s] = 0

    def one(node, _):
        tiles = [patterns_ref[node, a] for a in range(sides)]
        classes = [class_of(tile, me) for tile in tiles]
        order = [(ranks >> (3 * c)) & 7 for c in classes]
        phase = [(phases >> (2 * c)) & 3 for c in classes]
        slots = []
        for a in range(sides):
            slot = sum(((phase[b] < phase[a]) if b > a else (phase[b] <= phase[a])).astype(jnp.int32) for b in range(sides) if b != a)
            slots_ref[0, node * sides + a] = slot
            slots_ref[1, node * sides + slot] = a
            slots.append(slot)
        for p in range(len(ROUNDS)):
            slots_ref[2 + p, node] = sum((phase[a] == p).astype(jnp.int32) for a in range(sides))

        def add(which, first, i, j):
            at = count_ref[which]
            code = (first * nodes + node) * sides + i
            jobs_ref[which, at] = ((code * sides + j) * sides + pick(slots, i)) * sides + pick(slots, j)
            count_ref[which] = at + 1

        def pick(values, i):
            value = values[0]
            for k in range(1, sides):
                value = jnp.where(i == k, values[k], value)
            return value

        for a in range(sides):
            r, c = tiles[a], classes[a]
            entry = table_ref[c * CLASSES + c]
            first = jnp.where(c == 0, r, 0)
            add(((entry >> 6) * 2 + ((r ^ me) & 1)) * 3 + 1, first, jnp.int32(a), jnp.int32(a))
        for a in range(sides):
            for b in range(a + 1, sides):
                turned = jnp.where(classes[a] == classes[b], (tiles[a] & 1) == 1, order[a] > order[b])
                r, q = jnp.where(turned, tiles[b], tiles[a]), jnp.where(turned, tiles[a], tiles[b])
                c, d = jnp.where(turned, classes[b], classes[a]), jnp.where(turned, classes[a], classes[b])
                i, j = jnp.where(turned, b, a), jnp.where(turned, a, b)
                entry = table_ref[c * CLASSES + d]
                halved = (c == d) & (c != 0)
                first = (entry & 63) + jnp.where(halved, 0, 2 * (q & 1))
                first = jnp.where(c == 0, q, first)
                which = ((entry >> 6) * 2 + jnp.where(halved, 0, (r ^ me) & 1)) * 3 + jnp.where(halved, 2, 0)
                add(which, first, i, j)

        return 0

    lax.fori_loop(0, nodes, one, 0)


def place(high_ref, low_ref, node, a, b, value):
    rows = pl.ds(pl.multiple_of(a * TILE, TILE), TILE)
    cols = pl.ds(pl.multiple_of(b * TILE, TILE), TILE)
    high_ref[node, rows, cols], low_ref[node, rows, cols] = split(value)


def put_tiles(sets, nodes, sides, me_ref, jobs_ref, count_ref, sources, high_ref, low_ref):
    even = (me_ref[0] & 1) == 0

    def work(name, pair, start):
        def read(which, sort, i):
            code = jobs_ref[which, i]
            fields = []
            for size in (sides, sides, sides, sides, nodes):
                fields.append(lax.rem(code, size))
                code = lax.div(code, size)
            slot_j, slot_i, j, i, node = fields
            other = (which // 3) % 2
            if name == "rows":
                value = pair[other][:, pl.ds(pl.multiple_of(code * TILE, TILE), TILE)]
            elif sort == 2:
                rows = pl.ds(pl.multiple_of(start + code * HALF, HALF), HALF)
                mine, theirs = pair[0][rows, :], pair[1][rows, :]
                value = jnp.concatenate([jnp.where(even, mine, theirs), jnp.where(even, theirs, mine)], axis=0)
            else:
                value = pair[other][pl.ds(pl.multiple_of(start + code * HALF, HALF), TILE), :]
            return node, i, j, slot_i, slot_j, value

        def put(sort, node, i, j, slot_i, slot_j, value):
            place(high_ref, low_ref, node, slot_i, j, value)
            if sort != 1:
                place(high_ref, low_ref, node, slot_j, i, value.T)

        for other in range(2):
            for sort in range(3):
                which = (KINDS.index(name) * 2 + other) * 3 + sort
                if sort == 2 and (other == 1 or name == "rows" or not PIECES[name][1]) or sort == 1 and name == "far_rest":
                    continue
                if sort == 0 and name != "rows" and not PIECES[name][2]:
                    continue
                number = count_ref[which]

                def two(i, _):
                    first, second = read(which, sort, 2 * i), read(which, sort, 2 * i + 1)
                    put(sort, *first)
                    put(sort, *second)
                    return 0

                lax.fori_loop(0, lax.div(number, 2), two, 0)

                @pl.when(lax.rem(number, 2) == 1)
                def _():
                    put(sort, *read(which, sort, number - 1))

    at = 0
    for names in sets:
        start = 0
        for name in names:
            work(name, sources[at : at + 2], start)
            start += 0 if name == "rows" else piece_rows(name)
        at += 2


def assemble_full_kernel(nodes, sides, patterns_ref, whole_ref, high_ref, low_ref):
    def one(step, _):
        node = step // (sides * sides)
        a = lax.rem(step // sides, sides)
        b = lax.rem(step, sides)
        rows = pl.ds(pl.multiple_of(patterns_ref[node, a] * TILE, TILE), TILE)
        cols = pl.ds(pl.multiple_of(patterns_ref[node, b] * TILE, TILE), TILE)
        place(high_ref, low_ref, node, a, b, whole_ref[rows, cols])
        return 0

    lax.fori_loop(0, nodes * sides * sides, one, 0)


def assemble_full(patterns, source):
    nodes, sides = patterns.shape
    side = sides * TILE
    return call(
        functools.partial(assemble_full_kernel, nodes, sides),
        "assemble_full",
        [("smem", patterns), ("vmem", source)],
        [pltpu.VMEM((nodes, side, side), jnp.bfloat16)] * 2,
        [VMEM] * 2,
    )


def halves_kernel(factor_ref, high_ref, low_ref):
    step = 4 * TILE
    for start in range(0, factor_ref.shape[1], step):
        where = slice(start, start + step)
        high_ref[:, where], low_ref[:, where] = split(factor_ref[:, where])


def factor_halves(factor, after=()):
    out = [pltpu.VMEM(factor.shape, jnp.bfloat16)] * 2
    return call(halves_kernel, "factor_halves", [("vmem", factor)], out, [VMEM] * 2, after)


def multiply_rows(phase, sides, widths_ref, slots_ref, high_ref, low_ref, f_high_ref, f_low_ref, out_ref, marg_ref, product_ref, sem):
    dot = functools.partial(jnp.dot, preferred_element_type=jnp.float32)
    nodes = widths_ref.shape[1]
    most = 8
    tall = 2

    def multiply(node, first, tile, height, width):
        cols = pl.ds(pl.multiple_of(tile * TILE, TILE), width * TILE)
        rows = pl.ds(pl.multiple_of(first * TILE, TILE), height * TILE)
        high, low = high_ref[node, rows, :], low_ref[node, rows, :]
        f_high, f_low = f_high_ref[:, cols], f_low_ref[:, cols]
        product = -(dot(high, f_high) + (dot(high, f_low) + dot(low, f_high)))
        total = jnp.zeros((1, width * TILE), jnp.float32)
        for i in range(height):
            part = product[i * TILE : (i + 1) * TILE, :]
            here = pl.ds(pl.multiple_of(slots_ref[1, node * sides + first + i] * TILE, TILE), TILE)
            product_ref[here, cols] = part
            factor = f_high_ref[here, cols].astype(jnp.float32) + f_low_ref[here, cols].astype(jnp.float32)
            total = total + jnp.sum(factor * part, axis=0, keepdims=True)
            pltpu.make_async_copy(product_ref.at[here, cols], out_ref.at[here, cols], sem).start()
        for k in range(width):
            row = pl.ds(tile + k, 1)
            marg_ref[row, :] = marg_ref[row, :] - total[:, k * TILE : (k + 1) * TILE]

    def one(node, carry):
        start, written = carry
        width = widths_ref[0, node]
        first, height = sum((slots_ref[2 + p, node] for p in range(phase)), 0), slots_ref[2 + phase, node]

        def across(row, h):
            def whole(i, _):
                multiply(node, row, start + most * i, h, most)
                return 0

            lax.fori_loop(0, lax.div(width, most), whole, 0)
            rest = lax.rem(width, most)
            for w in range(1, most):
                pl.when(rest == w)(lambda: multiply(node, row, start + width - rest, h, w))

        def down(i, _):
            across(first + tall * i, tall)
            return 0

        lax.fori_loop(0, lax.div(height, tall), down, 0)
        for h in range(1, tall):
            pl.when(lax.rem(height, tall) == h)(lambda: across(first + height - h, h))
        return start + width, written + width * height

    _, written = lax.fori_loop(0, nodes, one, (0, 0))

    def finish():
        rows, cols = product_ref.shape
        size = 1
        while size <= rows * cols // (TILE * TILE):
            wide = min(size, cols // TILE)
            part = (pl.ds(0, TILE * size // wide), pl.ds(0, TILE * wide))
            pl.when((written & size) != 0)(lambda: pltpu.make_async_copy(product_ref.at[part], out_ref.at[part], sem).wait())
            size *= 2

    return finish


def work_kernel(sets, phase, last, sides, *refs):
    me_ref, jobs_ref, count_ref, slots_ref, widths_ref, *refs = refs
    nodes = widths_ref.shape[1]
    sources, refs = refs[: 2 * len(sets)], refs[2 * len(sets) :]
    if phase is None:
        put_tiles(sets, nodes, sides, me_ref, jobs_ref, count_ref, sources, *refs[-2:])
        return
    f_high_ref, f_low_ref, before_ref, *_ = refs
    if not last:
        high_to, low_to, marg_ref, out_ref, product_ref, sems = refs[-6:]
    else:
        high_to, low_to, marg_out, out_ref, product_ref, sems, marg_ref = refs[-7:]
    if sets:
        put_tiles(sets, nodes, sides, me_ref, jobs_ref, count_ref, sources, high_to, low_to)
    marg_ref[...] = before_ref[...]
    finish = multiply_rows(
        phase, sides, widths_ref, slots_ref, high_to, low_to, f_high_ref, f_low_ref, out_ref, marg_ref, product_ref, sems.at[0]
    )
    if last:
        copy = pltpu.make_async_copy(marg_ref, marg_out, sems.at[1])
        copy.start()
        copy.wait()
    finish()


def work(me, plan, widths, sides, blocks, sets=(), sources=(), phase=None, factors=(), before=None, out=(), last=False, after=()):
    given = [("smem", x) for x in (me, *plan, widths)] + [("vmem", x) for x in sources]
    shapes = [pltpu.VMEM((widths.shape[1], sides * TILE, sides * TILE), jnp.bfloat16)] * 2
    specs, scratch, aliases = [VMEM] * 2, [], {}
    if phase is not None:
        given += [("vmem", x) for x in (*factors, before)]
    if blocks:
        aliases = {len(given): 0, len(given) + 1: 1}
        given += [("vmem", x) for x in blocks]
    if phase is not None:
        given += [("any", x) for x in out]
        rows, cols = factors[0].shape
        if out:
            aliases[len(given) - 1] = 3
        anywhere = pl.BlockSpec(memory_space=pl.ANY)
        marg = jax.ShapeDtypeStruct(before.shape, jnp.float32) if last else pltpu.VMEM(before.shape, jnp.float32)
        shapes += [marg, jax.ShapeDtypeStruct((rows, cols), jnp.float32)]
        specs += [anywhere if last else VMEM, anywhere]
        scratch = [pltpu.VMEM((rows, cols), jnp.float32), pltpu.SemaphoreType.DMA((2,))]
        scratch += [pltpu.VMEM(before.shape, jnp.float32)] if last else []
    name = "_".join([f"put_{names[0]}" for names in sets[:1]] + [f"multiply_{phase}"] * (phase is not None))
    kernel = functools.partial(work_kernel, sets, phase, last, sides)
    return call(
        kernel, name, given, shapes, specs, after, vmem=14 if scratch else 6, scratch_shapes=scratch, input_output_aliases=aliases
    )


def swap(value, mask):
    return lax.ppermute(value, "pr", [(i, i ^ mask) for i in range(DEVICES)])


def move(value, places):
    pairs = [(4 * old + k, 4 * new + k) for old, new in places.items() for k in range(4)]
    return lax.ppermute(value, "pr", pairs)


def plan_jobs(me, patterns, after):
    nodes, sides = patterns.shape
    shapes = [
        jax.ShapeDtypeStruct((LISTS * len(KINDS), nodes * sides), jnp.int32),
        jax.ShapeDtypeStruct((LISTS * len(KINDS),), jnp.int32),
        jax.ShapeDtypeStruct((2 + len(ROUNDS), nodes * sides), jnp.int32),
    ]
    given = [("smem", me), ("smem", piece_table()), ("smem", patterns)]
    return call(functools.partial(jobs_kernel, nodes, sides), "plan_jobs", given, shapes, [SMEM] * 3, after)


def turn(name, kernel, me, given, rows, held, after=()):
    shapes = [pltpu.VMEM((n, TILE), jnp.float32) for n in rows] + [pltpu.VMEM(x.shape, x.dtype) for x in held]

    def body(me_ref, *refs):
        place = me_ref[0] >> 2
        kernel((place == 1) | (place == 2), *refs[: len(given)], *refs[len(given) + len(held) :][: len(rows)])

    inputs = [("smem", me)] + [("vmem", x) for x in (*given, *held)]
    aliases = {1 + len(given) + i: len(rows) + i for i in range(len(held))}
    return call(body, name, inputs, shapes, [VMEM] * len(shapes), after, input_output_aliases=aliases)


def copy_rows(target_ref, row, source_ref, first=0, count=None):
    count = source_ref.shape[0] - first if count is None else count
    target_ref[row : row + count, :] = source_ref[first : first + count, :]
    return row + count


def turn_1(inner, near_ref, side_ref, part_ref, held_ref, far_ref, far_first_ref):
    copy_rows(part_ref, 0, near_ref, 0, part_ref.shape[0])
    copy_rows(held_ref, copy_rows(held_ref, 0, near_ref), side_ref)
    first, rest = piece_rows("far"), piece_rows("far_rest")
    copy_rows(far_ref, 0, near_ref, 0, first)
    copy_rows(far_ref, first, near_ref, near_ref.shape[0] - rest, rest)
    copy_rows(far_first_ref, 0, near_ref, 0, first)


def turn_2(inner, mid_ref, mid_outer_ref, far_ref, far_outer_ref, side_near_ref, part_ref, held_ref, rest_ref):
    mid, far, onward = piece_rows("mid"), piece_rows("far"), piece_rows("side_mid")

    def take(m_ref, f_ref):
        copy_rows(part_ref, copy_rows(part_ref, 0, m_ref, 0, onward), f_ref, 0, far)
        copy_rows(held_ref, 0, m_ref)
        copy_rows(held_ref, mid + side_near_ref.shape[0], f_ref, 0, far)

    pl.when(inner)(lambda: take(mid_ref, far_ref))
    pl.when(jnp.logical_not(inner))(lambda: take(mid_outer_ref, far_outer_ref))
    copy_rows(held_ref, mid, side_near_ref)
    copy_rows(rest_ref, 0, far_ref, far)


def turn_3(inner, side_last_ref, rest_ref, rest_outer_ref, held_ref):
    row = copy_rows(held_ref, 0, side_last_ref)

    def take(ref):
        copy_rows(held_ref, row, ref)

    pl.when(inner)(lambda: take(rest_ref))
    pl.when(jnp.logical_not(inner))(lambda: take(rest_outer_ref))


def planned(sep_inv, factor, widths, patterns, dinv):
    me = lax.axis_index("pr").astype(jnp.int32).reshape(1)
    between_inner, outward, across = {1: 2, 2: 1}, {1: 0, 2: 3}, {1: 3, 2: 0}

    near, side, mid = pack((("near",), ("side",), ("mid",)), me, sep_inv)
    rows_other = swap(sep_inv, 1)
    near, side, mid = swap(near, 4), swap(side, 2), move(mid, between_inner)
    plan = plan_jobs(me, patterns, (rows_other,))
    factors = factor_halves(factor, plan[1:2])
    do = functools.partial(work, me, plan, widths, patterns.shape[1])
    blocks = do((), (("rows",),), (sep_inv, rows_other), after=factors[:1])
    rows = (piece_rows("side_near"), piece_rows(*ROUNDS[0]), piece_rows("far", "far_rest"), piece_rows("far"))
    part, held, far, far_first, mid = turn("turn_1", turn_1, me, (near, side), rows, (mid,), blocks[:1])

    side_near, mid_outer = swap(part, 2), move(mid, outward)
    far, far_outer = move(far, between_inner), move(far_first, across)
    *blocks, marg, out = do(blocks, ROUNDS[:1], (held, swap(held, 1)), 0, factors, dinv)
    rows = (piece_rows("side_mid", "side_far"), piece_rows(*ROUNDS[1]), piece_rows("far_rest"))
    part, held, rest = turn("turn_2", turn_2, me, (mid, mid_outer, far, far_outer, side_near), rows, (), (marg,))

    side_last, rest_outer = swap(part, 2), move(rest, outward)
    *blocks, marg, out = do(blocks, ROUNDS[1:2], (held, swap(held, 1)), 1, factors, marg, (out,))
    (held,) = turn("turn_3", turn_3, me, (side_last, rest, rest_outer), (piece_rows(*ROUNDS[2]),), (), (marg,))
    *_, marg, out = do(blocks, ROUNDS[2:], (held, swap(held, 1)), 2, factors, marg, (out,), last=True)
    return out, marg


def shards(sep_inv, factor, widths, patterns, dinv):
    own_rows, order = sep_inv.shape
    cols = factor.shape[1]
    dinv = dinv.reshape(cols // TILE, TILE)
    if own_rows == TILE and order == DEVICES * TILE:
        out, marg = planned(sep_inv, factor, widths, patterns, dinv)
    else:
        nodes, sides = patterns.shape
        blocks = assemble_full(patterns, lax.all_gather(sep_inv, "pr", axis=0, tiled=True))
        order = jnp.tile(jnp.arange(sides, dtype=jnp.int32), nodes)
        nothing = jnp.zeros((1,), jnp.int32)
        plan = (nothing, nothing, jnp.stack([order, order, jnp.full_like(order, sides)]))
        *_, marg, out = work(nothing, plan, widths, sides, blocks, phase=0, factors=factor_halves(factor), before=dinv, last=True)
    return out, marg.reshape(cols)


def solution(mesh):
    placed = (
        P(("cfg", "pr"), None),
        P("cfg", "pr"),
        P("pr", None),
        P("pr", None),
        P(("cfg", "pr")),
    )
    return jax.shard_map(
        shards,
        mesh=mesh,
        in_specs=placed,
        out_specs=(P("cfg", "pr"), P(("cfg", "pr"))),
        check_vma=False,
    )
```

```python
import functools

import jax
import jax.numpy as jnp
from jax import lax
from jax.experimental import pallas as pl
from jax.experimental.pallas import tpu as pltpu
from jax.sharding import PartitionSpec as P

TILE = 128
HALF = TILE // 2
MIB = 1024 * 1024

ORDER = (0, 2, 1, 3, 4, 6, 5, 7)
PIECES = {
    "near": (2, True, (4, 6, 5, 7, 1, 3)),
    "side": (1, True, (3, 4, 6, 5, 7)),
    "mid": (4, True, (6, 5, 7)),
    "side_near": (3, True, (5, 7, 4, 6)),
    "far": (6, True, ()),
    "side_mid": (5, True, (7,)),
    "side_far": (7, True, ()),
    "far_rest": (6, False, (5, 7)),
}
ROUNDS = (("near", "side"), ("mid", "side_near", "far"), ("side_mid", "side_far", "far_rest"))
KINDS = ("rows",) + tuple(PIECES)
DEVICES = 16
LISTS = 6
WHOLE = (0, 0, 0, 1, 1, 2, 2, 2)
CLASSES = DEVICES // 2


def class_of(device, seen_from):
    place, here = device >> 2, seen_from >> 2
    outer = ((place >> 1) ^ place ^ 1) & 1
    z = jnp.where((place ^ here) >> 1 != 0, 2 + outer, (place ^ here) & 1)
    return 2 * z + (((device ^ seen_from) >> 1) & 1)


def device_of(column, seen_from, core):
    here, z = seen_from >> 2, column >> 1
    half = (here >> 1) ^ (z >> 1)
    inner_first = half ^ 1 ^ (z & 1)
    place = 2 * half + (inner_first if z >= 2 else (here & 1) ^ z)
    return 4 * place + 2 * (((seen_from >> 1) & 1) ^ (column & 1)) + core


def piece_rows(*names):
    return sum((TILE + HALF if PIECES[name][1] else 0) + 2 * TILE * len(PIECES[name][2]) for name in names)


def piece_table():
    table = [0] * (CLASSES * CLASSES)
    for name, (owner, own, classes) in PIECES.items():
        kind = KINDS.index(name)
        for place, column in enumerate(classes):
            table[owner * CLASSES + column] = kind * 64 + (3 if own else 0) + 4 * place
        if own:
            table[owner * CLASSES + owner] = kind * 64 + 2
    return jnp.array(table, jnp.int32)


def call(kernel, name, given, out_shape, out_specs, after=(), vmem=6, cost=0, **more):
    places = {"smem": pltpu.SMEM, "vmem": pltpu.VMEM, "any": pl.ANY}
    arrays = [pltpu.with_memory_space_constraint(x, pltpu.VMEM) if space == "vmem" else x for space, x in given]
    inputs = len(given)

    def body(*refs):
        kernel(*refs[:inputs], *refs[inputs + len(after) :])

    return pl.pallas_call(
        body,
        out_shape=out_shape,
        in_specs=[pl.BlockSpec(memory_space=places[space]) for space, _ in given] + [pl.BlockSpec(memory_space=pl.ANY)] * len(after),
        out_specs=out_specs,
        compiler_params=pltpu.CompilerParams(vmem_limit_bytes=vmem * MIB),
        cost_estimate=pl.CostEstimate(flops=0, bytes_accessed=cost, transcendentals=0),
        name=name,
        **more,
    )(*arrays, *after)


SMEM = pl.BlockSpec(memory_space=pltpu.SMEM)
VMEM = pl.BlockSpec(memory_space=pltpu.VMEM)
US = 3_000_000


def split(value):
    high = value.astype(jnp.bfloat16)
    low = (value - high.astype(jnp.float32)).astype(jnp.bfloat16)
    return high, low


def pack_kernel(sets, me_ref, rows_ref, *refs):
    packed_refs, pair_ref, half_ref, pair_sem, half_sem, sems = refs[: len(sets)], *refs[len(sets) :]
    me = me_ref[0]

    def tile(q):
        return rows_ref.at[:, pl.ds(pl.multiple_of(q * TILE, TILE), TILE)]

    pair = pltpu.make_async_copy(tile(me ^ 1), pair_ref, pair_sem)
    pair.start()
    copies, halves = [], []
    for names, packed_ref in zip(sets, packed_refs, strict=True):
        row = 0
        for name in names:
            owner, own, classes = PIECES[name]
            receiver = device_of(owner, me, 0) if owner < 4 else me ^ 12
            columns = [device_of(column, receiver, core) for column in classes for core in range(2)]
            if own:
                copies.append((tile(me), packed_ref.at[pl.ds(row, TILE), :]))
                halves.append((half_ref, packed_ref.at[pl.ds(row + TILE, HALF), :]))
                row += TILE + HALF
            for q in columns:
                copies.append((tile(q), packed_ref.at[pl.ds(row, TILE), :]))
                row += TILE
    copies = [pltpu.make_async_copy(*ends, sems.at[i]) for i, ends in enumerate(copies)]
    halves = [pltpu.make_async_copy(*ends, half_sem.at[i]) for i, ends in enumerate(halves)]
    for copy in copies:
        copy.start()
    pair.wait()
    half_ref[...] = jnp.where(me % 2 == 0, pair_ref[:HALF, :], pair_ref[...].T[HALF:, :])
    for copy in halves:
        copy.start()
    for copy in (*copies, *halves):
        copy.wait()


def pack(sets, me, sep_rows):
    names = [name for names in sets for name in names]
    tiles = sum(PIECES[name][1] + 2 * len(PIECES[name][2]) for name in names)
    anywhere = pl.BlockSpec(memory_space=pl.ANY)
    return call(
        functools.partial(pack_kernel, sets),
        "pack",
        [("smem", me), ("any", sep_rows)],
        [jax.ShapeDtypeStruct((piece_rows(*names), TILE), jnp.float32) for names in sets],
        [anywhere] * len(sets),
        scratch_shapes=[
            pltpu.VMEM((TILE, TILE), jnp.float32),
            pltpu.VMEM((HALF, TILE), jnp.float32),
            pltpu.SemaphoreType.DMA(()),
            pltpu.SemaphoreType.DMA((len(names),)),
            pltpu.SemaphoreType.DMA((tiles,)),
        ],
    )


def jobs_kernel(nodes, sides, me_ref, table_ref, patterns_ref, jobs_ref, count_ref, slots_ref):
    me = me_ref[0]
    ranks = sum(ORDER.index(c) << (3 * c) for c in range(CLASSES))
    phases = sum(WHOLE[c] << (2 * c) for c in range(CLASSES))
    for s in range(LISTS * len(KINDS)):
        count_ref[s] = 0

    def one(node, _):
        tiles = [patterns_ref[node, a] for a in range(sides)]
        classes = [class_of(tile, me) for tile in tiles]
        order = [(ranks >> (3 * c)) & 7 for c in classes]
        phase = [(phases >> (2 * c)) & 3 for c in classes]
        slots = []
        for a in range(sides):
            slot = sum(((phase[b] < phase[a]) if b > a else (phase[b] <= phase[a])).astype(jnp.int32) for b in range(sides) if b != a)
            slots_ref[0, node * sides + a] = slot
            slots_ref[1, node * sides + slot] = a
            slots.append(slot)
        for p in range(len(ROUNDS)):
            slots_ref[2 + p, node] = sum((phase[a] == p).astype(jnp.int32) for a in range(sides))

        def add(which, first, i, j):
            at = count_ref[which]
            code = (first * nodes + node) * sides + i
            jobs_ref[which, at] = ((code * sides + j) * sides + pick(slots, i)) * sides + pick(slots, j)
            count_ref[which] = at + 1

        def pick(values, i):
            value = values[0]
            for k in range(1, sides):
                value = jnp.where(i == k, values[k], value)
            return value

        for a in range(sides):
            r, c = tiles[a], classes[a]
            entry = table_ref[c * CLASSES + c]
            first = jnp.where(c == 0, r, 0)
            add(((entry >> 6) * 2 + ((r ^ me) & 1)) * 3 + 1, first, jnp.int32(a), jnp.int32(a))
        for a in range(sides):
            for b in range(a + 1, sides):
                turned = jnp.where(classes[a] == classes[b], (tiles[a] & 1) == 1, order[a] > order[b])
                r, q = jnp.where(turned, tiles[b], tiles[a]), jnp.where(turned, tiles[a], tiles[b])
                c, d = jnp.where(turned, classes[b], classes[a]), jnp.where(turned, classes[a], classes[b])
                i, j = jnp.where(turned, b, a), jnp.where(turned, a, b)
                entry = table_ref[c * CLASSES + d]
                halved = (c == d) & (c != 0)
                first = (entry & 63) + jnp.where(halved, 0, 2 * (q & 1))
                first = jnp.where(c == 0, q, first)
                which = ((entry >> 6) * 2 + jnp.where(halved, 0, (r ^ me) & 1)) * 3 + jnp.where(halved, 2, 0)
                add(which, first, i, j)

        return 0

    lax.fori_loop(0, nodes, one, 0)


def place(high_ref, low_ref, node, a, b, value):
    rows = pl.ds(pl.multiple_of(a * TILE, TILE), TILE)
    cols = pl.ds(pl.multiple_of(b * TILE, TILE), TILE)
    high_ref[node, rows, cols], low_ref[node, rows, cols] = split(value)


def put_tiles(sets, nodes, sides, me_ref, jobs_ref, count_ref, sources, high_ref, low_ref):
    even = (me_ref[0] & 1) == 0

    def work(name, pair, start):
        def read(which, sort, i):
            code = jobs_ref[which, i]
            fields = []
            for size in (sides, sides, sides, sides, nodes):
                fields.append(lax.rem(code, size))
                code = lax.div(code, size)
            slot_j, slot_i, j, i, node = fields
            other = (which // 3) % 2
            if name == "rows":
                value = pair[other][:, pl.ds(pl.multiple_of(code * TILE, TILE), TILE)]
            elif sort == 2:
                rows = pl.ds(pl.multiple_of(start + code * HALF, HALF), HALF)
                mine, theirs = pair[0][rows, :], pair[1][rows, :]
                value = jnp.concatenate([jnp.where(even, mine, theirs), jnp.where(even, theirs, mine)], axis=0)
            else:
                value = pair[other][pl.ds(pl.multiple_of(start + code * HALF, HALF), TILE), :]
            return node, i, j, slot_i, slot_j, value

        def put(sort, node, i, j, slot_i, slot_j, value):
            place(high_ref, low_ref, node, slot_i, j, value)
            if sort != 1:
                place(high_ref, low_ref, node, slot_j, i, value.T)

        for other in range(2):
            for sort in range(3):
                which = (KINDS.index(name) * 2 + other) * 3 + sort
                if sort == 2 and (other == 1 or name == "rows" or not PIECES[name][1]) or sort == 1 and name == "far_rest":
                    continue
                if sort == 0 and name != "rows" and not PIECES[name][2]:
                    continue
                number = count_ref[which]

                def two(i, _):
                    first, second = read(which, sort, 2 * i), read(which, sort, 2 * i + 1)
                    put(sort, *first)
                    put(sort, *second)
                    return 0

                lax.fori_loop(0, lax.div(number, 2), two, 0)

                @pl.when(lax.rem(number, 2) == 1)
                def _():
                    put(sort, *read(which, sort, number - 1))

    at = 0
    for names in sets:
        start = 0
        for name in names:
            work(name, sources[at : at + 2], start)
            start += 0 if name == "rows" else piece_rows(name)
        at += 2


def assemble_full_kernel(nodes, sides, patterns_ref, whole_ref, high_ref, low_ref):
    def one(step, _):
        node = step // (sides * sides)
        a = lax.rem(step // sides, sides)
        b = lax.rem(step, sides)
        rows = pl.ds(pl.multiple_of(patterns_ref[node, a] * TILE, TILE), TILE)
        cols = pl.ds(pl.multiple_of(patterns_ref[node, b] * TILE, TILE), TILE)
        place(high_ref, low_ref, node, a, b, whole_ref[rows, cols])
        return 0

    lax.fori_loop(0, nodes * sides * sides, one, 0)


def assemble_full(patterns, source):
    nodes, sides = patterns.shape
    side = sides * TILE
    return call(
        functools.partial(assemble_full_kernel, nodes, sides),
        "assemble_full",
        [("smem", patterns), ("vmem", source)],
        [pltpu.VMEM((nodes, side, side), jnp.bfloat16)] * 2,
        [VMEM] * 2,
    )


def halves_kernel(factor_ref, high_ref, low_ref):
    step = 4 * TILE
    for start in range(0, factor_ref.shape[1], step):
        where = slice(start, start + step)
        high_ref[:, where], low_ref[:, where] = split(factor_ref[:, where])


def factor_halves(factor, after=()):
    out = [pltpu.VMEM(factor.shape, jnp.bfloat16)] * 2
    return call(halves_kernel, "factor_halves", [("vmem", factor)], out, [VMEM] * 2, after)


def multiply_rows(phase, sides, widths_ref, slots_ref, high_ref, low_ref, f_high_ref, f_low_ref, out_ref, marg_ref, product_ref, sem):
    dot = functools.partial(jnp.dot, preferred_element_type=jnp.float32)
    nodes = widths_ref.shape[1]
    most = 8
    tall = 2

    def multiply(node, first, tile, height, width):
        cols = pl.ds(pl.multiple_of(tile * TILE, TILE), width * TILE)
        rows = pl.ds(pl.multiple_of(first * TILE, TILE), height * TILE)
        high, low = high_ref[node, rows, :], low_ref[node, rows, :]
        f_high, f_low = f_high_ref[:, cols], f_low_ref[:, cols]
        product = -(dot(high, f_high) + (dot(high, f_low) + dot(low, f_high)))
        total = jnp.zeros((1, width * TILE), jnp.float32)
        for i in range(height):
            part = product[i * TILE : (i + 1) * TILE, :]
            here = pl.ds(pl.multiple_of(slots_ref[1, node * sides + first + i] * TILE, TILE), TILE)
            product_ref[here, cols] = part
            factor = f_high_ref[here, cols].astype(jnp.float32) + f_low_ref[here, cols].astype(jnp.float32)
            total = total + jnp.sum(factor * part, axis=0, keepdims=True)
            pltpu.make_async_copy(product_ref.at[here, cols], out_ref.at[here, cols], sem).start()
        for k in range(width):
            row = pl.ds(tile + k, 1)
            marg_ref[row, :] = marg_ref[row, :] - total[:, k * TILE : (k + 1) * TILE]

    def one(node, carry):
        start, written = carry
        width = widths_ref[0, node]
        first, height = sum((slots_ref[2 + p, node] for p in range(phase)), 0), slots_ref[2 + phase, node]

        def across(row, h):
            def whole(i, _):
                multiply(node, row, start + most * i, h, most)
                return 0

            lax.fori_loop(0, lax.div(width, most), whole, 0)
            rest = lax.rem(width, most)
            for w in range(1, most):
                pl.when(rest == w)(lambda: multiply(node, row, start + width - rest, h, w))

        def down(i, _):
            across(first + tall * i, tall)
            return 0

        lax.fori_loop(0, lax.div(height, tall), down, 0)
        for h in range(1, tall):
            pl.when(lax.rem(height, tall) == h)(lambda: across(first + height - h, h))
        return start + width, written + width * height

    _, written = lax.fori_loop(0, nodes, one, (0, 0))

    def finish():
        rows, cols = product_ref.shape
        size = 1
        while size <= rows * cols // (TILE * TILE):
            wide = min(size, cols // TILE)
            part = (pl.ds(0, TILE * size // wide), pl.ds(0, TILE * wide))
            pl.when((written & size) != 0)(lambda: pltpu.make_async_copy(product_ref.at[part], out_ref.at[part], sem).wait())
            size *= 2

    return finish


def work_kernel(sets, phase, last, sides, *refs):
    me_ref, jobs_ref, count_ref, slots_ref, widths_ref, *refs = refs
    nodes = widths_ref.shape[1]
    sources, refs = refs[: 2 * len(sets)], refs[2 * len(sets) :]
    if phase is None:
        put_tiles(sets, nodes, sides, me_ref, jobs_ref, count_ref, sources, *refs[-2:])
        return
    f_high_ref, f_low_ref, before_ref, *_ = refs
    if not last:
        high_to, low_to, marg_ref, out_ref, product_ref, sems = refs[-6:]
    else:
        high_to, low_to, marg_out, out_ref, product_ref, sems, marg_ref = refs[-7:]
    if sets:
        put_tiles(sets, nodes, sides, me_ref, jobs_ref, count_ref, sources, high_to, low_to)
    marg_ref[...] = before_ref[...]
    finish = multiply_rows(
        phase, sides, widths_ref, slots_ref, high_to, low_to, f_high_ref, f_low_ref, out_ref, marg_ref, product_ref, sems.at[0]
    )
    if last:
        copy = pltpu.make_async_copy(marg_ref, marg_out, sems.at[1])
        copy.start()
        copy.wait()
    finish()


def work(me, plan, widths, sides, blocks, sets=(), sources=(), phase=None, factors=(), before=None, out=(), last=False, after=()):
    given = [("smem", x) for x in (me, *plan, widths)] + [("vmem", x) for x in sources]
    shapes = [pltpu.VMEM((widths.shape[1], sides * TILE, sides * TILE), jnp.bfloat16)] * 2
    specs, scratch, aliases = [VMEM] * 2, [], {}
    if phase is not None:
        given += [("vmem", x) for x in (*factors, before)]
    if blocks:
        aliases = {len(given): 0, len(given) + 1: 1}
        given += [("vmem", x) for x in blocks]
    if phase is not None:
        given += [("any", x) for x in out]
        rows, cols = factors[0].shape
        if out:
            aliases[len(given) - 1] = 3
        anywhere = pl.BlockSpec(memory_space=pl.ANY)
        marg = jax.ShapeDtypeStruct(before.shape, jnp.float32) if last else pltpu.VMEM(before.shape, jnp.float32)
        shapes += [marg, jax.ShapeDtypeStruct((rows, cols), jnp.float32)]
        specs += [anywhere if last else VMEM, anywhere]
        scratch = [pltpu.VMEM((rows, cols), jnp.float32), pltpu.SemaphoreType.DMA((2,))]
        scratch += [pltpu.VMEM(before.shape, jnp.float32)] if last else []
    name = "_".join([f"put_{names[0]}" for names in sets[:1]] + [f"multiply_{phase}"] * (phase is not None))
    kernel = functools.partial(work_kernel, sets, phase, last, sides)
    return call(
        kernel, name, given, shapes, specs, after, vmem=14 if scratch else 6, scratch_shapes=scratch, input_output_aliases=aliases
    )


def swap(value, mask):
    return lax.ppermute(value, "pr", [(i, i ^ mask) for i in range(DEVICES)])


def move(value, places):
    pairs = [(4 * old + k, 4 * new + k) for old, new in places.items() for k in range(4)]
    return lax.ppermute(value, "pr", pairs)


def plan_jobs(me, patterns, after):
    nodes, sides = patterns.shape
    shapes = [
        jax.ShapeDtypeStruct((LISTS * len(KINDS), nodes * sides), jnp.int32),
        jax.ShapeDtypeStruct((LISTS * len(KINDS),), jnp.int32),
        jax.ShapeDtypeStruct((2 + len(ROUNDS), nodes * sides), jnp.int32),
    ]
    given = [("smem", me), ("smem", piece_table()), ("smem", patterns)]
    return call(functools.partial(jobs_kernel, nodes, sides), "plan_jobs", given, shapes, [SMEM] * 3, after)


def turn(name, kernel, me, given, rows, held, after=()):
    shapes = [pltpu.VMEM((n, TILE), jnp.float32) for n in rows] + [pltpu.VMEM(x.shape, x.dtype) for x in held]

    def body(me_ref, *refs):
        place = me_ref[0] >> 2
        kernel((place == 1) | (place == 2), *refs[: len(given)], *refs[len(given) + len(held) :][: len(rows)])

    inputs = [("smem", me)] + [("vmem", x) for x in (*given, *held)]
    aliases = {1 + len(given) + i: len(rows) + i for i in range(len(held))}
    return call(body, name, inputs, shapes, [VMEM] * len(shapes), after, input_output_aliases=aliases)


def copy_rows(target_ref, row, source_ref, first=0, count=None):
    count = source_ref.shape[0] - first if count is None else count
    target_ref[row : row + count, :] = source_ref[first : first + count, :]
    return row + count


def turn_1(inner, near_ref, side_ref, part_ref, held_ref, far_ref):
    copy_rows(part_ref, 0, near_ref, 0, part_ref.shape[0])
    copy_rows(held_ref, copy_rows(held_ref, 0, near_ref), side_ref)
    first, rest = piece_rows("far"), piece_rows("far_rest")
    copy_rows(far_ref, 0, near_ref, 0, first)
    copy_rows(far_ref, first, near_ref, near_ref.shape[0] - rest, rest)


def turn_2(inner, mid_ref, mid_outer_ref, far_ref, far_outer_ref, side_near_ref, part_ref, held_ref, rest_ref):
    mid, far, onward = piece_rows("mid"), piece_rows("far"), piece_rows("side_mid")

    def take(m_ref, f_ref):
        copy_rows(part_ref, copy_rows(part_ref, 0, m_ref, 0, onward), f_ref, 0, far)
        copy_rows(held_ref, 0, m_ref)
        copy_rows(held_ref, mid + side_near_ref.shape[0], f_ref, 0, far)

    pl.when(inner)(lambda: take(mid_ref, far_ref))
    pl.when(jnp.logical_not(inner))(lambda: take(mid_outer_ref, far_outer_ref))
    copy_rows(held_ref, mid, side_near_ref)
    copy_rows(rest_ref, 0, far_ref, far)


def turn_3(inner, side_last_ref, rest_ref, rest_outer_ref, held_ref):
    row = copy_rows(held_ref, 0, side_last_ref)

    def take(ref):
        copy_rows(held_ref, row, ref)

    pl.when(inner)(lambda: take(rest_ref))
    pl.when(jnp.logical_not(inner))(lambda: take(rest_outer_ref))


def planned(sep_inv, factor, widths, patterns, dinv):
    me = lax.axis_index("pr").astype(jnp.int32).reshape(1)
    between_inner, between_outer, outward = {1: 2, 2: 1}, {0: 3, 3: 0}, {1: 0, 2: 3}

    near, side, mid, first = pack((("near",), ("side",), ("mid",), ("far",)), me, sep_inv)
    rows_other = swap(sep_inv, 1)
    near, side, mid = swap(near, 4), swap(side, 2), move(mid, between_inner)
    plan = plan_jobs(me, patterns, (rows_other,))
    factors = factor_halves(factor, plan[1:2])
    do = functools.partial(work, me, plan, widths, patterns.shape[1])
    blocks = do((), (("rows",),), (sep_inv, rows_other), after=factors[:1])
    rows = (piece_rows("side_near"), piece_rows(*ROUNDS[0]), piece_rows("far", "far_rest"))
    part, held, far, mid = turn("turn_1", turn_1, me, (near, side), rows, (mid,), blocks[:1])

    side_near, mid_outer = swap(part, 2), move(mid, outward)
    far, far_outer = move(far, between_inner), move(first, between_outer)
    *blocks, marg, out = do(blocks, ROUNDS[:1], (held, swap(held, 1)), 0, factors, dinv)
    rows = (piece_rows("side_mid", "side_far"), piece_rows(*ROUNDS[1]), piece_rows("far_rest"))
    part, held, rest = turn("turn_2", turn_2, me, (mid, mid_outer, far, far_outer, side_near), rows, (), (marg,))

    side_last, rest_outer = swap(part, 2), move(rest, outward)
    *blocks, marg, out = do(blocks, ROUNDS[1:2], (held, swap(held, 1)), 1, factors, marg, (out,))
    (held,) = turn("turn_3", turn_3, me, (side_last, rest, rest_outer), (piece_rows(*ROUNDS[2]),), (), (marg,))
    *_, marg, out = do(blocks, ROUNDS[2:], (held, swap(held, 1)), 2, factors, marg, (out,), last=True)
    return out, marg


def shards(sep_inv, factor, widths, patterns, dinv):
    own_rows, order = sep_inv.shape
    cols = factor.shape[1]
    dinv = dinv.reshape(cols // TILE, TILE)
    if own_rows == TILE and order == DEVICES * TILE:
        out, marg = planned(sep_inv, factor, widths, patterns, dinv)
    else:
        nodes, sides = patterns.shape
        blocks = assemble_full(patterns, lax.all_gather(sep_inv, "pr", axis=0, tiled=True))
        order = jnp.tile(jnp.arange(sides, dtype=jnp.int32), nodes)
        nothing = jnp.zeros((1,), jnp.int32)
        plan = (nothing, nothing, jnp.stack([order, order, jnp.full_like(order, sides)]))
        *_, marg, out = work(nothing, plan, widths, sides, blocks, phase=0, factors=factor_halves(factor), before=dinv, last=True)
    return out, marg.reshape(cols)


def solution(mesh):
    placed = (
        P(("cfg", "pr"), None),
        P("cfg", "pr"),
        P("pr", None),
        P("pr", None),
        P(("cfg", "pr")),
    )
    return jax.shard_map(
        shards,
        mesh=mesh,
        in_specs=placed,
        out_specs=(P("cfg", "pr"), P(("cfg", "pr"))),
        check_vma=False,
    )
```

```python
import functools

import jax
import jax.numpy as jnp
from jax import lax
from jax.experimental import pallas as pl
from jax.experimental.pallas import tpu as pltpu
from jax.sharding import PartitionSpec as P

TILE = 128
HALF = TILE // 2
QUARTER = TILE // 4
FOLD, PAIR, FIRST = HALF, HALF + QUARTER, TILE + QUARTER
MIB = 1024 * 1024

ORDER = (0, 2, 1, 3, 4, 6, 5, 7)
PIECES = {
    "near": (2, True, (4, 6, 5, 7, 1, 3)),
    "side": (1, True, (3, 4, 6, 5, 7)),
    "mid": (4, True, (6, 5, 7)),
    "side_near": (3, True, (5, 7, 4, 6)),
    "far": (6, True, ()),
    "side_mid": (5, True, (7,)),
    "side_far": (7, True, ()),
    "far_rest": (6, False, (5, 7)),
}
ROUNDS = (("near", "side"), ("mid", "side_near", "far"), ("side_mid", "side_far", "far_rest"))
KINDS = ("rows",) + tuple(PIECES)
DEVICES = 16
LISTS = 6
WHOLE = (0, 0, 0, 1, 1, 2, 2, 2)
CLASSES = DEVICES // 2


def class_of(device, seen_from):
    place, here = device >> 2, seen_from >> 2
    outer = ((place >> 1) ^ place ^ 1) & 1
    z = jnp.where((place ^ here) >> 1 != 0, 2 + outer, (place ^ here) & 1)
    return 2 * z + (((device ^ seen_from) >> 1) & 1)


def device_of(column, seen_from, core):
    here, z = seen_from >> 2, column >> 1
    half = (here >> 1) ^ (z >> 1)
    inner_first = half ^ 1 ^ (z & 1)
    place = 2 * half + (inner_first if z >= 2 else (here & 1) ^ z)
    return 4 * place + 2 * (((seen_from >> 1) & 1) ^ (column & 1)) + core


def diagonal_rows(name):
    return TILE if name in ROUNDS[-1] else PAIR


def first_rows(name):
    return diagonal_rows(name) + HALF if PIECES[name][1] else 0


def piece_rows(*names):
    return sum(first_rows(name) + 2 * TILE * len(PIECES[name][2]) for name in names)


def piece_table():
    table = [0] * (CLASSES * CLASSES)
    for name, (owner, own, classes) in PIECES.items():
        kind = KINDS.index(name)
        for place, column in enumerate(classes):
            table[owner * CLASSES + column] = kind * 64 + first_rows(name) // QUARTER + 8 * place
        if own:
            table[owner * CLASSES + owner] = kind * 64 + diagonal_rows(name) // QUARTER
    return jnp.array(table, jnp.int32)


def call(kernel, name, given, out_shape, out_specs, after=(), vmem=6, cost=0, **more):
    places = {"smem": pltpu.SMEM, "vmem": pltpu.VMEM, "any": pl.ANY}
    arrays = [pltpu.with_memory_space_constraint(x, pltpu.VMEM) if space == "vmem" else x for space, x in given]
    inputs = len(given)

    def body(*refs):
        kernel(*refs[:inputs], *refs[inputs + len(after) :])

    return pl.pallas_call(
        body,
        out_shape=out_shape,
        in_specs=[pl.BlockSpec(memory_space=places[space]) for space, _ in given] + [pl.BlockSpec(memory_space=pl.ANY)] * len(after),
        out_specs=out_specs,
        compiler_params=pltpu.CompilerParams(vmem_limit_bytes=vmem * MIB),
        cost_estimate=pl.CostEstimate(flops=0, bytes_accessed=cost, transcendentals=0),
        name=name,
        **more,
    )(*arrays, *after)


SMEM = pl.BlockSpec(memory_space=pltpu.SMEM)
VMEM = pl.BlockSpec(memory_space=pltpu.VMEM)
US = 3_000_000


def split(value):
    high = value.astype(jnp.bfloat16)
    low = (value - high.astype(jnp.float32)).astype(jnp.bfloat16)
    return high, low


def pack_kernel(sets, me_ref, rows_ref, *refs):
    packed_refs, own_ref, first_sems, sems = refs[: len(sets)], *refs[len(sets) :]
    me = me_ref[0]

    def tile(q):
        return rows_ref.at[:, pl.ds(pl.multiple_of(q * TILE, TILE), TILE)]

    copies, firsts = [], []
    for names, packed_ref in zip(sets, packed_refs, strict=True):
        row = 0
        for name in names:
            owner, own, classes = PIECES[name]
            receiver = device_of(owner, me, 0) if owner < 4 else me ^ 12
            if own:
                firsts.append((own_ref, packed_ref.at[pl.ds(row, FIRST), :]))
                row += FIRST
            for q in [device_of(column, receiver, core) for column in classes for core in range(2)]:
                copies.append((tile(q), packed_ref.at[pl.ds(row, TILE), :]))
                row += TILE
    copies = [pltpu.make_async_copy(*ends, sems.at[i]) for i, ends in enumerate(copies)]
    firsts = [pltpu.make_async_copy(*ends, first_sems.at[i]) for i, ends in enumerate(firsts)]
    for copy in copies:
        copy.start()
    diagonal, pair = tile(me)[...], tile(me ^ 1)[...]
    own_ref[:FOLD, :] = diagonal[:HALF, :]
    first, second = diagonal[HALF : HALF + QUARTER, :], diagonal[HALF + QUARTER :, :]
    left = lax.broadcasted_iota(jnp.int32, first.shape, 1) < HALF
    own_ref[FOLD:PAIR, :] = jnp.where(left, pltpu.roll(first, HALF, 1), second)
    own_ref[PAIR:FIRST, :] = jnp.where(me % 2 == 0, pair[:HALF, :], pair.T[HALF:, :])
    for copy in firsts:
        copy.start()
    for copy in (*copies, *firsts):
        copy.wait()


def unfold(value):
    top, fold = value[:HALF, :], value[FOLD:PAIR, :]
    upper = jnp.concatenate([top, pltpu.roll(fold, HALF, 1), fold], axis=0)
    row, column = (lax.broadcasted_iota(jnp.int32, upper.shape, k) for k in range(2))
    return jnp.where((row >= HALF) & (column < HALF), upper.T, upper)


def pack(sets, me, sep_rows, after=()):
    names = [name for names in sets for name in names]
    tiles = sum(2 * len(PIECES[name][2]) for name in names)
    return call(
        functools.partial(pack_kernel, sets),
        "pack_" + names[0],
        [("smem", me), ("vmem", sep_rows)],
        [pltpu.HBM((piece_rows(*names), TILE), jnp.float32) for names in sets],
        [pl.BlockSpec(memory_space=pltpu.HBM)] * len(sets),
        after,
        scratch_shapes=[
            pltpu.VMEM((FIRST, TILE), jnp.float32),
            pltpu.SemaphoreType.DMA((len(names),)),
            pltpu.SemaphoreType.DMA((max(tiles, 1),)),
        ],
    )


def jobs_kernel(nodes, sides, me_ref, table_ref, patterns_ref, jobs_ref, count_ref, slots_ref):
    me = me_ref[0]
    ranks = sum(ORDER.index(c) << (3 * c) for c in range(CLASSES))
    phases = sum(WHOLE[c] << (2 * c) for c in range(CLASSES))
    for s in range(LISTS * len(KINDS)):
        count_ref[s] = 0

    def one(node, _):
        tiles = [patterns_ref[node, a] for a in range(sides)]
        classes = [class_of(tile, me) for tile in tiles]
        order = [(ranks >> (3 * c)) & 7 for c in classes]
        phase = [(phases >> (2 * c)) & 3 for c in classes]
        slots = []
        for a in range(sides):
            slot = sum(((phase[b] < phase[a]) if b > a else (phase[b] <= phase[a])).astype(jnp.int32) for b in range(sides) if b != a)
            slots_ref[0, node * sides + a] = slot
            slots_ref[1, node * sides + slot] = a
            slots.append(slot)
        for p in range(len(ROUNDS)):
            slots_ref[2 + p, node] = sum((phase[a] == p).astype(jnp.int32) for a in range(sides))

        def add(which, first, i, j):
            at = count_ref[which]
            code = (first * nodes + node) * sides + i
            jobs_ref[which, at] = ((code * sides + j) * sides + pick(slots, i)) * sides + pick(slots, j)
            count_ref[which] = at + 1

        def pick(values, i):
            value = values[0]
            for k in range(1, sides):
                value = jnp.where(i == k, values[k], value)
            return value

        for a in range(sides):
            r, c = tiles[a], classes[a]
            entry = table_ref[c * CLASSES + c]
            first = jnp.where(c == 0, r, 0)
            add(((entry >> 6) * 2 + ((r ^ me) & 1)) * 3 + 1, first, jnp.int32(a), jnp.int32(a))
        for a in range(sides):
            for b in range(a + 1, sides):
                turned = jnp.where(classes[a] == classes[b], (tiles[a] & 1) == 1, order[a] > order[b])
                r, q = jnp.where(turned, tiles[b], tiles[a]), jnp.where(turned, tiles[a], tiles[b])
                c, d = jnp.where(turned, classes[b], classes[a]), jnp.where(turned, classes[a], classes[b])
                i, j = jnp.where(turned, b, a), jnp.where(turned, a, b)
                entry = table_ref[c * CLASSES + d]
                halved = (c == d) & (c != 0)
                first = (entry & 63) + jnp.where(halved, 0, 4 * (q & 1))
                first = jnp.where(c == 0, q, first)
                which = ((entry >> 6) * 2 + jnp.where(halved, 0, (r ^ me) & 1)) * 3 + jnp.where(halved, 2, 0)
                add(which, first, i, j)

        return 0

    lax.fori_loop(0, nodes, one, 0)


def place(high_ref, low_ref, node, a, b, value):
    rows = pl.ds(pl.multiple_of(a * TILE, TILE), TILE)
    cols = pl.ds(pl.multiple_of(b * TILE, TILE), TILE)
    high_ref[node, rows, cols], low_ref[node, rows, cols] = split(value)


def put_tiles(sets, nodes, sides, me_ref, jobs_ref, count_ref, sources, high_ref, low_ref):
    even = (me_ref[0] & 1) == 0

    def work(name, pair, start):
        def read(which, sort, i):
            code = jobs_ref[which, i]
            fields = []
            for size in (sides, sides, sides, sides, nodes):
                fields.append(lax.rem(code, size))
                code = lax.div(code, size)
            slot_j, slot_i, j, i, node = fields
            other = (which // 3) % 2
            if name == "rows":
                value = pair[other][:, pl.ds(pl.multiple_of(code * TILE, TILE), TILE)]
            elif sort == 2:
                rows = pl.ds(pl.multiple_of(start + code * QUARTER, QUARTER), HALF)
                mine, theirs = pair[0][rows, :], pair[1][rows, :]
                value = jnp.concatenate([jnp.where(even, mine, theirs), jnp.where(even, theirs, mine)], axis=0)
            else:
                length = diagonal_rows(name) if sort == 1 else TILE
                value = pair[other][pl.ds(pl.multiple_of(start + code * QUARTER, QUARTER), length), :]
                value = unfold(value) if length == PAIR else value
            return node, i, j, slot_i, slot_j, value

        def put(sort, node, i, j, slot_i, slot_j, value):
            place(high_ref, low_ref, node, slot_i, j, value)
            if sort != 1:
                place(high_ref, low_ref, node, slot_j, i, value.T)

        for other in range(2):
            for sort in range(3):
                which = (KINDS.index(name) * 2 + other) * 3 + sort
                if sort == 2 and (other == 1 or name == "rows" or not PIECES[name][1]) or sort == 1 and name == "far_rest":
                    continue
                if sort == 0 and name != "rows" and not PIECES[name][2]:
                    continue
                number = count_ref[which]

                def two(i, _):
                    first, second = read(which, sort, 2 * i), read(which, sort, 2 * i + 1)
                    put(sort, *first)
                    put(sort, *second)
                    return 0

                lax.fori_loop(0, lax.div(number, 2), two, 0)

                @pl.when(lax.rem(number, 2) == 1)
                def _():
                    put(sort, *read(which, sort, number - 1))

    at = 0
    for names in sets:
        start = 0
        for name in names:
            work(name, sources[at : at + 2], start)
            start += 0 if name == "rows" else piece_rows(name)
        at += 2


def assemble_full_kernel(nodes, sides, patterns_ref, whole_ref, high_ref, low_ref):
    def one(step, _):
        node = step // (sides * sides)
        a = lax.rem(step // sides, sides)
        b = lax.rem(step, sides)
        rows = pl.ds(pl.multiple_of(patterns_ref[node, a] * TILE, TILE), TILE)
        cols = pl.ds(pl.multiple_of(patterns_ref[node, b] * TILE, TILE), TILE)
        place(high_ref, low_ref, node, a, b, whole_ref[rows, cols])
        return 0

    lax.fori_loop(0, nodes * sides * sides, one, 0)


def assemble_full(patterns, source):
    nodes, sides = patterns.shape
    side = sides * TILE
    return call(
        functools.partial(assemble_full_kernel, nodes, sides),
        "assemble_full",
        [("smem", patterns), ("vmem", source)],
        [pltpu.VMEM((nodes, side, side), jnp.bfloat16)] * 2,
        [VMEM] * 2,
    )


def halves_kernel(factor_ref, high_ref, low_ref):
    step = 4 * TILE
    for start in range(0, factor_ref.shape[1], step):
        where = slice(start, start + step)
        high_ref[:, where], low_ref[:, where] = split(factor_ref[:, where])


def factor_halves(factor, after=()):
    out = [pltpu.VMEM(factor.shape, jnp.bfloat16)] * 2
    return call(halves_kernel, "factor_halves", [("vmem", factor)], out, [VMEM] * 2, after)


def multiply_rows(phase, sides, widths_ref, slots_ref, high_ref, low_ref, f_high_ref, f_low_ref, out_ref, marg_ref, product_ref, sem):
    dot = functools.partial(jnp.dot, preferred_element_type=jnp.float32)
    nodes = widths_ref.shape[1]
    most = 8
    tall = 2

    def multiply(node, first, tile, height, width):
        cols = pl.ds(pl.multiple_of(tile * TILE, TILE), width * TILE)
        rows = pl.ds(pl.multiple_of(first * TILE, TILE), height * TILE)
        high, low = high_ref[node, rows, :], low_ref[node, rows, :]
        f_high, f_low = f_high_ref[:, cols], f_low_ref[:, cols]
        product = -(dot(high, f_high) + (dot(high, f_low) + dot(low, f_high)))
        total = jnp.zeros((1, width * TILE), jnp.float32)
        for i in range(height):
            part = product[i * TILE : (i + 1) * TILE, :]
            here = pl.ds(pl.multiple_of(slots_ref[1, node * sides + first + i] * TILE, TILE), TILE)
            product_ref[here, cols] = part
            factor = f_high_ref[here, cols].astype(jnp.float32) + f_low_ref[here, cols].astype(jnp.float32)
            total = total + jnp.sum(factor * part, axis=0, keepdims=True)
            pltpu.make_async_copy(product_ref.at[here, cols], out_ref.at[here, cols], sem).start()
        for k in range(width):
            row = pl.ds(tile + k, 1)
            marg_ref[row, :] = marg_ref[row, :] - total[:, k * TILE : (k + 1) * TILE]

    def one(node, carry):
        start, written = carry
        width = widths_ref[0, node]
        first, height = sum((slots_ref[2 + p, node] for p in range(phase)), 0), slots_ref[2 + phase, node]

        def across(row, h):
            def whole(i, _):
                multiply(node, row, start + most * i, h, most)
                return 0

            lax.fori_loop(0, lax.div(width, most), whole, 0)
            rest = lax.rem(width, most)
            for w in range(1, most):
                pl.when(rest == w)(lambda: multiply(node, row, start + width - rest, h, w))

        def down(i, _):
            across(first + tall * i, tall)
            return 0

        lax.fori_loop(0, lax.div(height, tall), down, 0)
        for h in range(1, tall):
            pl.when(lax.rem(height, tall) == h)(lambda: across(first + height - h, h))
        return start + width, written + width * height

    _, written = lax.fori_loop(0, nodes, one, (0, 0))

    def finish():
        rows, cols = product_ref.shape
        size = 1
        while size <= rows * cols // (TILE * TILE):
            wide = min(size, cols // TILE)
            part = (pl.ds(0, TILE * size // wide), pl.ds(0, TILE * wide))
            pl.when((written & size) != 0)(lambda: pltpu.make_async_copy(product_ref.at[part], out_ref.at[part], sem).wait())
            size *= 2

    return finish


def work_kernel(sets, phase, last, sides, *refs):
    me_ref, jobs_ref, count_ref, slots_ref, widths_ref, *refs = refs
    nodes = widths_ref.shape[1]
    sources, refs = refs[: 2 * len(sets)], refs[2 * len(sets) :]
    if phase is None:
        put_tiles(sets, nodes, sides, me_ref, jobs_ref, count_ref, sources, *refs[-2:])
        return
    f_high_ref, f_low_ref, before_ref, *_ = refs
    if not last:
        high_to, low_to, marg_ref, out_ref, product_ref, sems = refs[-6:]
    else:
        high_to, low_to, marg_out, out_ref, product_ref, sems, marg_ref = refs[-7:]
    if sets:
        put_tiles(sets, nodes, sides, me_ref, jobs_ref, count_ref, sources, high_to, low_to)
    marg_ref[...] = before_ref[...]
    finish = multiply_rows(
        phase, sides, widths_ref, slots_ref, high_to, low_to, f_high_ref, f_low_ref, out_ref, marg_ref, product_ref, sems.at[0]
    )
    if last:
        copy = pltpu.make_async_copy(marg_ref, marg_out, sems.at[1])
        copy.start()
        copy.wait()
    finish()


def work(me, plan, widths, sides, blocks, sets=(), sources=(), phase=None, factors=(), before=None, out=(), last=False, after=()):
    given = [("smem", x) for x in (me, *plan, widths)] + [("vmem", x) for x in sources]
    shapes = [pltpu.VMEM((widths.shape[1], sides * TILE, sides * TILE), jnp.bfloat16)] * 2
    specs, scratch, aliases = [VMEM] * 2, [], {}
    if phase is not None:
        given += [("vmem", x) for x in (*factors, before)]
    if blocks:
        aliases = {len(given): 0, len(given) + 1: 1}
        given += [("vmem", x) for x in blocks]
    if phase is not None:
        given += [("any", x) for x in out]
        rows, cols = factors[0].shape
        if out:
            aliases[len(given) - 1] = 3
        anywhere = pl.BlockSpec(memory_space=pl.ANY)
        marg = jax.ShapeDtypeStruct(before.shape, jnp.float32) if last else pltpu.VMEM(before.shape, jnp.float32)
        shapes += [marg, jax.ShapeDtypeStruct((rows, cols), jnp.float32)]
        specs += [anywhere if last else VMEM, anywhere]
        scratch = [pltpu.VMEM((rows, cols), jnp.float32), pltpu.SemaphoreType.DMA((2,))]
        scratch += [pltpu.VMEM(before.shape, jnp.float32)] if last else []
    name = "_".join([f"put_{names[0]}" for names in sets[:1]] + [f"multiply_{phase}"] * (phase is not None))
    kernel = functools.partial(work_kernel, sets, phase, last, sides)
    return call(
        kernel, name, given, shapes, specs, after, vmem=14 if scratch else 6, scratch_shapes=scratch, input_output_aliases=aliases
    )


def swap(value, mask):
    return lax.ppermute(value, "pr", [(i, i ^ mask) for i in range(DEVICES)])


def move(value, places):
    pairs = [(4 * old + k, 4 * new + k) for old, new in places.items() for k in range(4)]
    return lax.ppermute(value, "pr", pairs)


def plan_jobs(me, patterns, after):
    nodes, sides = patterns.shape
    shapes = [
        jax.ShapeDtypeStruct((LISTS * len(KINDS), nodes * sides), jnp.int32),
        jax.ShapeDtypeStruct((LISTS * len(KINDS),), jnp.int32),
        jax.ShapeDtypeStruct((2 + len(ROUNDS), nodes * sides), jnp.int32),
    ]
    given = [("smem", me), ("smem", piece_table()), ("smem", patterns)]
    return call(functools.partial(jobs_kernel, nodes, sides), "plan_jobs", given, shapes, [SMEM] * 3, after)


def turn(name, kernel, me, given, rows, held, after=()):
    shapes = [pltpu.VMEM((n, TILE), jnp.float32) for n in rows] + [pltpu.VMEM(x.shape, x.dtype) for x in held]

    def body(me_ref, *refs):
        place = me_ref[0] >> 2
        kernel((place == 1) | (place == 2), *refs[: len(given)], *refs[len(given) + len(held) :][: len(rows)])

    inputs = [("smem", me)] + [("vmem", x) for x in (*given, *held)]
    aliases = {1 + len(given) + i: len(rows) + i for i in range(len(held))}
    return call(body, name, inputs, shapes, [VMEM] * len(shapes), after, input_output_aliases=aliases)


def copy_rows(target_ref, row, source_ref, first=0, count=None):
    count = source_ref.shape[0] - first if count is None else count
    target_ref[row : row + count, :] = source_ref[first : first + count, :]
    return row + count


def turn_1(inner, near_ref, side_ref, part_ref, held_ref, far_ref):
    copy_rows(part_ref, 0, near_ref, 0, part_ref.shape[0])
    copy_rows(held_ref, copy_rows(held_ref, 0, near_ref), side_ref)
    first, rest = piece_rows("far"), piece_rows("far_rest")
    copy_rows(far_ref, 0, near_ref, 0, first)
    copy_rows(far_ref, first, near_ref, near_ref.shape[0] - rest, rest)


def turn_2(inner, mid_ref, mid_outer_ref, far_ref, far_outer_ref, side_near_ref, part_ref, held_ref, rest_ref):
    mid, far, onward = piece_rows("mid"), piece_rows("far"), piece_rows("side_mid")

    def take(m_ref, f_ref):
        for row, ref, count in ((0, m_ref, onward), (onward, f_ref, piece_rows("side_far"))):
            part_ref[row : row + TILE, :] = unfold(ref[:PAIR, :])
            copy_rows(part_ref, row + TILE, ref, PAIR, count - TILE)
        copy_rows(held_ref, 0, m_ref)
        copy_rows(held_ref, mid + side_near_ref.shape[0], f_ref, 0, far)

    pl.when(inner)(lambda: take(mid_ref, far_ref))
    pl.when(jnp.logical_not(inner))(lambda: take(mid_outer_ref, far_outer_ref))
    copy_rows(held_ref, mid, side_near_ref)
    copy_rows(rest_ref, 0, far_ref, far)


def turn_3(inner, side_last_ref, rest_ref, rest_outer_ref, held_ref):
    row = copy_rows(held_ref, 0, side_last_ref)

    def take(ref):
        copy_rows(held_ref, row, ref)

    pl.when(inner)(lambda: take(rest_ref))
    pl.when(jnp.logical_not(inner))(lambda: take(rest_outer_ref))


def planned(sep_inv, factor, widths, patterns, dinv):
    me = lax.axis_index("pr").astype(jnp.int32).reshape(1)
    between_inner, between_outer, outward = {1: 2, 2: 1}, {0: 3, 3: 0}, {1: 0, 2: 3}

    near, side = pack((("near",), ("side",)), me, sep_inv)
    mid, first = pack((("mid",), ("far",)), me, sep_inv, (near,))
    rows_other = swap(sep_inv, 1)
    near, side, mid = swap(near, 4), swap(side, 2), move(mid, between_inner)
    plan = plan_jobs(me, patterns, (rows_other,))
    factors = factor_halves(factor, plan[1:2])
    do = functools.partial(work, me, plan, widths, patterns.shape[1])
    blocks = do((), (("rows",),), (sep_inv, rows_other), after=factors[:1])
    rows = (piece_rows("side_near"), piece_rows(*ROUNDS[0]), piece_rows("far", "far_rest"))
    part, held, far, mid = turn("turn_1", turn_1, me, (near, side), rows, (mid,), blocks[:1])

    side_near, mid_outer = swap(part, 2), move(mid, outward)
    far, far_outer = move(far, between_inner), move(first, between_outer)
    *blocks, marg, out = do(blocks, ROUNDS[:1], (held, swap(held, 1)), 0, factors, dinv)
    rows = (piece_rows("side_mid", "side_far"), piece_rows(*ROUNDS[1]), piece_rows("far_rest"))
    part, held, rest = turn("turn_2", turn_2, me, (mid, mid_outer, far, far_outer, side_near), rows, (), (marg,))

    side_last, rest_outer = swap(part, 2), move(rest, outward)
    *blocks, marg, out = do(blocks, ROUNDS[1:2], (held, swap(held, 1)), 1, factors, marg, (out,))
    (held,) = turn("turn_3", turn_3, me, (side_last, rest, rest_outer), (piece_rows(*ROUNDS[2]),), (), (marg,))
    *_, marg, out = do(blocks, ROUNDS[2:], (held, swap(held, 1)), 2, factors, marg, (out,), last=True)
    return out, marg


def shards(sep_inv, factor, widths, patterns, dinv):
    own_rows, order = sep_inv.shape
    cols = factor.shape[1]
    dinv = dinv.reshape(cols // TILE, TILE)
    if own_rows == TILE and order == DEVICES * TILE:
        out, marg = planned(sep_inv, factor, widths, patterns, dinv)
    else:
        nodes, sides = patterns.shape
        blocks = assemble_full(patterns, lax.all_gather(sep_inv, "pr", axis=0, tiled=True))
        order = jnp.tile(jnp.arange(sides, dtype=jnp.int32), nodes)
        nothing = jnp.zeros((1,), jnp.int32)
        plan = (nothing, nothing, jnp.stack([order, order, jnp.full_like(order, sides)]))
        *_, marg, out = work(nothing, plan, widths, sides, blocks, phase=0, factors=factor_halves(factor), before=dinv, last=True)
    return out, marg.reshape(cols)


def solution(mesh):
    placed = (
        P(("cfg", "pr"), None),
        P("cfg", "pr"),
        P("pr", None),
        P("pr", None),
        P(("cfg", "pr")),
    )
    return jax.shard_map(
        shards,
        mesh=mesh,
        in_specs=placed,
        out_specs=(P("cfg", "pr"), P(("cfg", "pr"))),
        check_vma=False,
    )
```

```python
import functools

import jax
import jax.numpy as jnp
from jax import lax
from jax.experimental import pallas as pl
from jax.experimental.pallas import tpu as pltpu
from jax.sharding import PartitionSpec as P

TILE = 128
HALF = TILE // 2
QUARTER = TILE // 4
FOLD, PAIR, FIRST = HALF, HALF + QUARTER, TILE + QUARTER
MIB = 1024 * 1024

ORDER = (0, 2, 1, 3, 4, 6, 5, 7)
PIECES = {
    "near": (2, True, (4, 6, 5, 7, 1, 3)),
    "side": (1, True, (3, 4, 6, 5, 7)),
    "mid": (4, True, (6, 5, 7)),
    "side_near": (3, True, (5, 7, 4, 6)),
    "far": (6, True, ()),
    "side_mid": (5, True, (7,)),
    "side_far": (7, True, ()),
    "far_rest": (6, False, (5, 7)),
}
ROUNDS = (("near", "side"), ("mid", "side_near", "far"), ("side_mid", "side_far", "far_rest"))
KINDS = ("rows",) + tuple(PIECES)
DEVICES = 16
LISTS = 6
WHOLE = (0, 0, 0, 1, 1, 2, 2, 2)
CLASSES = DEVICES // 2


def class_of(device, seen_from):
    place, here = device >> 2, seen_from >> 2
    outer = ((place >> 1) ^ place ^ 1) & 1
    z = jnp.where((place ^ here) >> 1 != 0, 2 + outer, (place ^ here) & 1)
    return 2 * z + (((device ^ seen_from) >> 1) & 1)


def device_of(column, seen_from, core):
    here, z = seen_from >> 2, column >> 1
    half = (here >> 1) ^ (z >> 1)
    inner_first = half ^ 1 ^ (z & 1)
    place = 2 * half + (inner_first if z >= 2 else (here & 1) ^ z)
    return 4 * place + 2 * (((seen_from >> 1) & 1) ^ (column & 1)) + core


def diagonal_rows(name):
    return TILE if name in ROUNDS[-1] else PAIR


def first_rows(name):
    return diagonal_rows(name) + HALF if PIECES[name][1] else 0


def piece_rows(*names):
    return sum(first_rows(name) + 2 * TILE * len(PIECES[name][2]) for name in names)


def piece_table():
    table = [0] * (CLASSES * CLASSES)
    for name, (owner, own, classes) in PIECES.items():
        kind = KINDS.index(name)
        for place, column in enumerate(classes):
            table[owner * CLASSES + column] = kind * 64 + first_rows(name) // QUARTER + 8 * place
        if own:
            table[owner * CLASSES + owner] = kind * 64 + diagonal_rows(name) // QUARTER
    return jnp.array(table, jnp.int32)


def call(kernel, name, given, out_shape, out_specs, after=(), vmem=6, cost=0, **more):
    places = {"smem": pltpu.SMEM, "vmem": pltpu.VMEM, "any": pl.ANY}
    arrays = [pltpu.with_memory_space_constraint(x, pltpu.VMEM) if space == "vmem" else x for space, x in given]
    inputs = len(given)

    def body(*refs):
        kernel(*refs[:inputs], *refs[inputs + len(after) :])

    return pl.pallas_call(
        body,
        out_shape=out_shape,
        in_specs=[pl.BlockSpec(memory_space=places[space]) for space, _ in given] + [pl.BlockSpec(memory_space=pl.ANY)] * len(after),
        out_specs=out_specs,
        compiler_params=pltpu.CompilerParams(vmem_limit_bytes=vmem * MIB),
        cost_estimate=pl.CostEstimate(flops=0, bytes_accessed=cost, transcendentals=0),
        name=name,
        **more,
    )(*arrays, *after)


SMEM = pl.BlockSpec(memory_space=pltpu.SMEM)
VMEM = pl.BlockSpec(memory_space=pltpu.VMEM)
US = 3_000_000


def split(value):
    high = value.astype(jnp.bfloat16)
    low = (value - high.astype(jnp.float32)).astype(jnp.bfloat16)
    return high, low


def pack_kernel(sets, me_ref, rows_ref, *refs):
    packed_refs, own_ref, first_sems, sems = refs[: len(sets)], *refs[len(sets) :]
    me = me_ref[0]

    def tile(q):
        return rows_ref.at[:, pl.ds(pl.multiple_of(q * TILE, TILE), TILE)]

    copies, firsts = [], []
    for names, packed_ref in zip(sets, packed_refs, strict=True):
        row = 0
        for name in names:
            owner, own, classes = PIECES[name]
            receiver = device_of(owner, me, 0) if owner < 4 else me ^ 12
            if own:
                firsts.append((own_ref, packed_ref.at[pl.ds(row, FIRST), :]))
                row += FIRST
            for q in [device_of(column, receiver, core) for column in classes for core in range(2)]:
                copies.append((tile(q), packed_ref.at[pl.ds(row, TILE), :]))
                row += TILE
    copies = [pltpu.make_async_copy(*ends, sems.at[i]) for i, ends in enumerate(copies)]
    firsts = [pltpu.make_async_copy(*ends, first_sems.at[i]) for i, ends in enumerate(firsts)]
    for copy in copies:
        copy.start()
    diagonal, pair = tile(me)[...], tile(me ^ 1)[...]
    own_ref[:FOLD, :] = diagonal[:HALF, :]
    first, second = diagonal[HALF : HALF + QUARTER, :], diagonal[HALF + QUARTER :, :]
    left = lax.broadcasted_iota(jnp.int32, first.shape, 1) < HALF
    own_ref[FOLD:PAIR, :] = jnp.where(left, pltpu.roll(first, HALF, 1), second)
    own_ref[PAIR:FIRST, :] = jnp.where(me % 2 == 0, pair[:HALF, :], pair.T[HALF:, :])
    for copy in firsts:
        copy.start()
    for copy in (*copies, *firsts):
        copy.wait()


def unfold(value):
    top, fold = value[:HALF, :], value[FOLD:PAIR, :]
    upper = jnp.concatenate([top, pltpu.roll(fold, HALF, 1), fold], axis=0)
    row, column = (lax.broadcasted_iota(jnp.int32, upper.shape, k) for k in range(2))
    return jnp.where((row >= HALF) & (column < HALF), upper.T, upper)


def pack(sets, me, sep_rows, after=()):
    names = [name for names in sets for name in names]
    tiles = sum(2 * len(PIECES[name][2]) for name in names)
    return call(
        functools.partial(pack_kernel, sets),
        "pack_" + names[0],
        [("smem", me), ("vmem", sep_rows)],
        [pltpu.HBM((piece_rows(*names), TILE), jnp.float32) for names in sets],
        [pl.BlockSpec(memory_space=pltpu.HBM)] * len(sets),
        after,
        scratch_shapes=[
            pltpu.VMEM((FIRST, TILE), jnp.float32),
            pltpu.SemaphoreType.DMA((len(names),)),
            pltpu.SemaphoreType.DMA((max(tiles, 1),)),
        ],
    )


def jobs_kernel(nodes, sides, me_ref, table_ref, patterns_ref, jobs_ref, count_ref, slots_ref):
    me = me_ref[0]
    ranks = sum(ORDER.index(c) << (3 * c) for c in range(CLASSES))
    phases = sum(WHOLE[c] << (2 * c) for c in range(CLASSES))
    for s in range(LISTS * len(KINDS)):
        count_ref[s] = 0

    def one(node, _):
        tiles = [patterns_ref[node, a] for a in range(sides)]
        classes = [class_of(tile, me) for tile in tiles]
        order = [(ranks >> (3 * c)) & 7 for c in classes]
        phase = [(phases >> (2 * c)) & 3 for c in classes]
        slots = []
        for a in range(sides):
            slot = sum(((phase[b] < phase[a]) if b > a else (phase[b] <= phase[a])).astype(jnp.int32) for b in range(sides) if b != a)
            slots_ref[0, node * sides + a] = slot
            slots_ref[1, node * sides + slot] = a
            slots.append(slot)
        for p in range(len(ROUNDS)):
            slots_ref[2 + p, node] = sum((phase[a] == p).astype(jnp.int32) for a in range(sides))

        def add(which, first, i, j):
            at = count_ref[which]
            code = (first * nodes + node) * sides + i
            jobs_ref[which, at] = ((code * sides + j) * sides + pick(slots, i)) * sides + pick(slots, j)
            count_ref[which] = at + 1

        def pick(values, i):
            value = values[0]
            for k in range(1, sides):
                value = jnp.where(i == k, values[k], value)
            return value

        for a in range(sides):
            r, c = tiles[a], classes[a]
            entry = table_ref[c * CLASSES + c]
            first = jnp.where(c == 0, r, 0)
            add(((entry >> 6) * 2 + ((r ^ me) & 1)) * 3 + 1, first, jnp.int32(a), jnp.int32(a))
        for a in range(sides):
            for b in range(a + 1, sides):
                turned = jnp.where(classes[a] == classes[b], (tiles[a] & 1) == 1, order[a] > order[b])
                r, q = jnp.where(turned, tiles[b], tiles[a]), jnp.where(turned, tiles[a], tiles[b])
                c, d = jnp.where(turned, classes[b], classes[a]), jnp.where(turned, classes[a], classes[b])
                i, j = jnp.where(turned, b, a), jnp.where(turned, a, b)
                entry = table_ref[c * CLASSES + d]
                halved = (c == d) & (c != 0)
                first = (entry & 63) + jnp.where(halved, 0, 4 * (q & 1))
                first = jnp.where(c == 0, q, first)
                which = ((entry >> 6) * 2 + jnp.where(halved, 0, (r ^ me) & 1)) * 3 + jnp.where(halved, 2, 0)
                add(which, first, i, j)

        return 0

    lax.fori_loop(0, nodes, one, 0)


def place(high_ref, low_ref, node, a, b, value):
    rows = pl.ds(pl.multiple_of(a * TILE, TILE), TILE)
    cols = pl.ds(pl.multiple_of(b * TILE, TILE), TILE)
    high_ref[node, rows, cols], low_ref[node, rows, cols] = split(value)


def put_tiles(sets, nodes, sides, me_ref, jobs_ref, count_ref, sources, high_ref, low_ref):
    even = (me_ref[0] & 1) == 0

    def work(name, pair, start):
        def read(which, sort, i):
            code = jobs_ref[which, i]
            fields = []
            for size in (sides, sides, sides, sides, nodes):
                fields.append(lax.rem(code, size))
                code = lax.div(code, size)
            slot_j, slot_i, j, i, node = fields
            other = (which // 3) % 2
            if name == "rows":
                value = pair[other][:, pl.ds(pl.multiple_of(code * TILE, TILE), TILE)]
            elif sort == 2:
                rows = pl.ds(pl.multiple_of(start + code * QUARTER, QUARTER), HALF)
                mine, theirs = pair[0][rows, :], pair[1][rows, :]
                value = jnp.concatenate([jnp.where(even, mine, theirs), jnp.where(even, theirs, mine)], axis=0)
            else:
                length = diagonal_rows(name) if sort == 1 else TILE
                value = pair[other][pl.ds(pl.multiple_of(start + code * QUARTER, QUARTER), length), :]
                value = unfold(value) if length == PAIR else value
            return node, i, j, slot_i, slot_j, value

        def put(sort, node, i, j, slot_i, slot_j, value):
            place(high_ref, low_ref, node, slot_i, j, value)
            if sort != 1:
                place(high_ref, low_ref, node, slot_j, i, value.T)

        def put_all(jobs):
            for sort, job in jobs:
                put(sort, *job)

        def list_of(other, sort):
            return (KINDS.index(name) * 2 + other) * 3 + sort

        def diagonals():
            lists = [list_of(other, 1) for other in range(2)]
            numbers = [count_ref[which] for which in lists]
            both = (numbers[0] > 0) & (numbers[1] > 0)

            def some(chosen):
                def step(i, _):
                    jobs = []
                    for k in chosen:
                        for at in (2 * i, 2 * i + 1):
                            jobs.append((1, read(lists[k], 1, jnp.minimum(at, numbers[k] - 1))))
                    put_all(jobs)
                    return 0

                return step

            most = jnp.maximum(numbers[0], numbers[1])
            lax.fori_loop(0, jnp.where(both, lax.div(most + 1, 2), 0), some((0, 1)), 0)
            for k in range(2):
                lax.fori_loop(0, jnp.where(both, 0, lax.div(numbers[k] + 1, 2)), some((k,)), 0)

        if name != "far_rest":
            diagonals()
        for other in range(2):
            for sort in (0, 2):
                which = list_of(other, sort)
                if sort == 2 and (other == 1 or name == "rows" or not PIECES[name][1]):
                    continue
                if sort == 0 and name != "rows" and not PIECES[name][2]:
                    continue
                number = count_ref[which]

                def two(i, _):
                    put_all([(sort, read(which, sort, 2 * i)), (sort, read(which, sort, 2 * i + 1))])
                    return 0

                lax.fori_loop(0, lax.div(number, 2), two, 0)

                @pl.when(lax.rem(number, 2) == 1)
                def _():
                    put_all([(sort, read(which, sort, number - 1))])

    at = 0
    for names in sets:
        start = 0
        for name in names:
            work(name, sources[at : at + 2], start)
            start += 0 if name == "rows" else piece_rows(name)
        at += 2


def assemble_full_kernel(nodes, sides, patterns_ref, whole_ref, high_ref, low_ref):
    def one(step, _):
        node = step // (sides * sides)
        a = lax.rem(step // sides, sides)
        b = lax.rem(step, sides)
        rows = pl.ds(pl.multiple_of(patterns_ref[node, a] * TILE, TILE), TILE)
        cols = pl.ds(pl.multiple_of(patterns_ref[node, b] * TILE, TILE), TILE)
        place(high_ref, low_ref, node, a, b, whole_ref[rows, cols])
        return 0

    lax.fori_loop(0, nodes * sides * sides, one, 0)


def assemble_full(patterns, source):
    nodes, sides = patterns.shape
    side = sides * TILE
    return call(
        functools.partial(assemble_full_kernel, nodes, sides),
        "assemble_full",
        [("smem", patterns), ("vmem", source)],
        [pltpu.VMEM((nodes, side, side), jnp.bfloat16)] * 2,
        [VMEM] * 2,
    )


def halves_kernel(factor_ref, high_ref, low_ref):
    step = 4 * TILE
    for start in range(0, factor_ref.shape[1], step):
        where = slice(start, start + step)
        high_ref[:, where], low_ref[:, where] = split(factor_ref[:, where])


def factor_halves(factor, after=()):
    out = [pltpu.VMEM(factor.shape, jnp.bfloat16)] * 2
    return call(halves_kernel, "factor_halves", [("vmem", factor)], out, [VMEM] * 2, after)


def multiply_rows(phase, sides, widths_ref, slots_ref, high_ref, low_ref, f_high_ref, f_low_ref, out_ref, marg_ref, product_ref, sem):
    dot = functools.partial(jnp.dot, preferred_element_type=jnp.float32)
    nodes = widths_ref.shape[1]
    most = 8
    tall = 2

    def multiply(node, first, tile, height, width):
        cols = pl.ds(pl.multiple_of(tile * TILE, TILE), width * TILE)
        rows = pl.ds(pl.multiple_of(first * TILE, TILE), height * TILE)
        high, low = high_ref[node, rows, :], low_ref[node, rows, :]
        f_high, f_low = f_high_ref[:, cols], f_low_ref[:, cols]
        product = -(dot(high, f_high) + (dot(high, f_low) + dot(low, f_high)))
        total = jnp.zeros((1, width * TILE), jnp.float32)
        for i in range(height):
            part = product[i * TILE : (i + 1) * TILE, :]
            here = pl.ds(pl.multiple_of(slots_ref[1, node * sides + first + i] * TILE, TILE), TILE)
            product_ref[here, cols] = part
            factor = f_high_ref[here, cols].astype(jnp.float32) + f_low_ref[here, cols].astype(jnp.float32)
            total = total + jnp.sum(factor * part, axis=0, keepdims=True)
            pltpu.make_async_copy(product_ref.at[here, cols], out_ref.at[here, cols], sem).start()
        for k in range(width):
            row = pl.ds(tile + k, 1)
            marg_ref[row, :] = marg_ref[row, :] - total[:, k * TILE : (k + 1) * TILE]

    def one(node, carry):
        start, written = carry
        width = widths_ref[0, node]
        first, height = sum((slots_ref[2 + p, node] for p in range(phase)), 0), slots_ref[2 + phase, node]

        def across(row, h):
            def whole(i, _):
                multiply(node, row, start + most * i, h, most)
                return 0

            lax.fori_loop(0, lax.div(width, most), whole, 0)
            rest = lax.rem(width, most)
            for w in range(1, most):
                pl.when(rest == w)(lambda: multiply(node, row, start + width - rest, h, w))

        def down(i, _):
            across(first + tall * i, tall)
            return 0

        lax.fori_loop(0, lax.div(height, tall), down, 0)
        for h in range(1, tall):
            pl.when(lax.rem(height, tall) == h)(lambda: across(first + height - h, h))
        return start + width, written + width * height

    _, written = lax.fori_loop(0, nodes, one, (0, 0))

    def finish():
        rows, cols = product_ref.shape
        size = 1
        while size <= rows * cols // (TILE * TILE):
            wide = min(size, cols // TILE)
            part = (pl.ds(0, TILE * size // wide), pl.ds(0, TILE * wide))
            pl.when((written & size) != 0)(lambda: pltpu.make_async_copy(product_ref.at[part], out_ref.at[part], sem).wait())
            size *= 2

    return finish


def work_kernel(sets, phase, last, sides, *refs):
    me_ref, jobs_ref, count_ref, slots_ref, widths_ref, *refs = refs
    nodes = widths_ref.shape[1]
    sources, refs = refs[: 2 * len(sets)], refs[2 * len(sets) :]
    if phase is None:
        put_tiles(sets, nodes, sides, me_ref, jobs_ref, count_ref, sources, *refs[-2:])
        return
    f_high_ref, f_low_ref, before_ref, *_ = refs
    if not last:
        high_to, low_to, marg_ref, out_ref, product_ref, sems = refs[-6:]
    else:
        high_to, low_to, marg_out, out_ref, product_ref, sems, marg_ref = refs[-7:]
    if sets:
        put_tiles(sets, nodes, sides, me_ref, jobs_ref, count_ref, sources, high_to, low_to)
    marg_ref[...] = before_ref[...]
    finish = multiply_rows(
        phase, sides, widths_ref, slots_ref, high_to, low_to, f_high_ref, f_low_ref, out_ref, marg_ref, product_ref, sems.at[0]
    )
    if last:
        copy = pltpu.make_async_copy(marg_ref, marg_out, sems.at[1])
        copy.start()
        copy.wait()
    finish()


def work(me, plan, widths, sides, blocks, sets=(), sources=(), phase=None, factors=(), before=None, out=(), last=False, after=()):
    given = [("smem", x) for x in (me, *plan, widths)] + [("vmem", x) for x in sources]
    shapes = [pltpu.VMEM((widths.shape[1], sides * TILE, sides * TILE), jnp.bfloat16)] * 2
    specs, scratch, aliases = [VMEM] * 2, [], {}
    if phase is not None:
        given += [("vmem", x) for x in (*factors, before)]
    if blocks:
        aliases = {len(given): 0, len(given) + 1: 1}
        given += [("vmem", x) for x in blocks]
    if phase is not None:
        given += [("any", x) for x in out]
        rows, cols = factors[0].shape
        if out:
            aliases[len(given) - 1] = 3
        anywhere = pl.BlockSpec(memory_space=pl.ANY)
        marg = jax.ShapeDtypeStruct(before.shape, jnp.float32) if last else pltpu.VMEM(before.shape, jnp.float32)
        shapes += [marg, jax.ShapeDtypeStruct((rows, cols), jnp.float32)]
        specs += [anywhere if last else VMEM, anywhere]
        scratch = [pltpu.VMEM((rows, cols), jnp.float32), pltpu.SemaphoreType.DMA((2,))]
        scratch += [pltpu.VMEM(before.shape, jnp.float32)] if last else []
    name = "_".join([f"put_{names[0]}" for names in sets[:1]] + [f"multiply_{phase}"] * (phase is not None))
    kernel = functools.partial(work_kernel, sets, phase, last, sides)
    return call(
        kernel, name, given, shapes, specs, after, vmem=14 if scratch else 6, scratch_shapes=scratch, input_output_aliases=aliases
    )


def swap(value, mask):
    return lax.ppermute(value, "pr", [(i, i ^ mask) for i in range(DEVICES)])


def move(value, places):
    pairs = [(4 * old + k, 4 * new + k) for old, new in places.items() for k in range(4)]
    return lax.ppermute(value, "pr", pairs)


def plan_jobs(me, patterns, after):
    nodes, sides = patterns.shape
    shapes = [
        jax.ShapeDtypeStruct((LISTS * len(KINDS), nodes * sides), jnp.int32),
        jax.ShapeDtypeStruct((LISTS * len(KINDS),), jnp.int32),
        jax.ShapeDtypeStruct((2 + len(ROUNDS), nodes * sides), jnp.int32),
    ]
    given = [("smem", me), ("smem", piece_table()), ("smem", patterns)]
    return call(functools.partial(jobs_kernel, nodes, sides), "plan_jobs", given, shapes, [SMEM] * 3, after)


def turn(name, kernel, me, given, rows, held, after=()):
    shapes = [pltpu.VMEM((n, TILE), jnp.float32) for n in rows] + [pltpu.VMEM(x.shape, x.dtype) for x in held]

    def body(me_ref, *refs):
        place = me_ref[0] >> 2
        kernel((place == 1) | (place == 2), *refs[: len(given)], *refs[len(given) + len(held) :][: len(rows)])

    inputs = [("smem", me)] + [("vmem", x) for x in (*given, *held)]
    aliases = {1 + len(given) + i: len(rows) + i for i in range(len(held))}
    return call(body, name, inputs, shapes, [VMEM] * len(shapes), after, input_output_aliases=aliases)


def copy_rows(target_ref, row, source_ref, first=0, count=None):
    count = source_ref.shape[0] - first if count is None else count
    target_ref[row : row + count, :] = source_ref[first : first + count, :]
    return row + count


def turn_1(inner, near_ref, side_ref, part_ref, held_ref, far_ref):
    copy_rows(part_ref, 0, near_ref, 0, part_ref.shape[0])
    copy_rows(held_ref, copy_rows(held_ref, 0, near_ref), side_ref)
    first, rest = piece_rows("far"), piece_rows("far_rest")
    copy_rows(far_ref, 0, near_ref, 0, first)
    copy_rows(far_ref, first, near_ref, near_ref.shape[0] - rest, rest)


def turn_2(inner, mid_ref, mid_outer_ref, far_ref, far_outer_ref, side_near_ref, part_ref, held_ref, rest_ref):
    mid, far, onward = piece_rows("mid"), piece_rows("far"), piece_rows("side_mid")

    def take(m_ref, f_ref):
        for row, ref, count in ((0, m_ref, onward), (onward, f_ref, piece_rows("side_far"))):
            part_ref[row : row + TILE, :] = unfold(ref[:PAIR, :])
            copy_rows(part_ref, row + TILE, ref, PAIR, count - TILE)
        copy_rows(held_ref, 0, m_ref)
        copy_rows(held_ref, mid + side_near_ref.shape[0], f_ref, 0, far)

    pl.when(inner)(lambda: take(mid_ref, far_ref))
    pl.when(jnp.logical_not(inner))(lambda: take(mid_outer_ref, far_outer_ref))
    copy_rows(held_ref, mid, side_near_ref)
    copy_rows(rest_ref, 0, far_ref, far)


def turn_3(inner, side_last_ref, rest_ref, rest_outer_ref, held_ref):
    row = copy_rows(held_ref, 0, side_last_ref)

    def take(ref):
        copy_rows(held_ref, row, ref)

    pl.when(inner)(lambda: take(rest_ref))
    pl.when(jnp.logical_not(inner))(lambda: take(rest_outer_ref))


def planned(sep_inv, factor, widths, patterns, dinv):
    me = lax.axis_index("pr").astype(jnp.int32).reshape(1)
    between_inner, between_outer, outward = {1: 2, 2: 1}, {0: 3, 3: 0}, {1: 0, 2: 3}

    near, side = pack((("near",), ("side",)), me, sep_inv)
    mid, first = pack((("mid",), ("far",)), me, sep_inv, (near,))
    rows_other = swap(sep_inv, 1)
    near, side, mid = swap(near, 4), swap(side, 2), move(mid, between_inner)
    plan = plan_jobs(me, patterns, (rows_other,))
    factors = factor_halves(factor, plan[1:2])
    do = functools.partial(work, me, plan, widths, patterns.shape[1])
    blocks = do((), (("rows",),), (sep_inv, rows_other), after=factors[:1])
    rows = (piece_rows("side_near"), piece_rows(*ROUNDS[0]), piece_rows("far", "far_rest"))
    part, held, far, mid = turn("turn_1", turn_1, me, (near, side), rows, (mid,), blocks[:1])

    side_near, mid_outer = swap(part, 2), move(mid, outward)
    far, far_outer = move(far, between_inner), move(first, between_outer)
    *blocks, marg, out = do(blocks, ROUNDS[:1], (held, swap(held, 1)), 0, factors, dinv)
    rows = (piece_rows("side_mid", "side_far"), piece_rows(*ROUNDS[1]), piece_rows("far_rest"))
    part, held, rest = turn("turn_2", turn_2, me, (mid, mid_outer, far, far_outer, side_near), rows, (), (marg,))

    side_last, rest_outer = swap(part, 2), move(rest, outward)
    *blocks, marg, out = do(blocks, ROUNDS[1:2], (held, swap(held, 1)), 1, factors, marg, (out,))
    (held,) = turn("turn_3", turn_3, me, (side_last, rest, rest_outer), (piece_rows(*ROUNDS[2]),), (), (marg,))
    *_, marg, out = do(blocks, ROUNDS[2:], (held, swap(held, 1)), 2, factors, marg, (out,), last=True)
    return out, marg


def shards(sep_inv, factor, widths, patterns, dinv):
    own_rows, order = sep_inv.shape
    cols = factor.shape[1]
    dinv = dinv.reshape(cols // TILE, TILE)
    if own_rows == TILE and order == DEVICES * TILE:
        out, marg = planned(sep_inv, factor, widths, patterns, dinv)
    else:
        nodes, sides = patterns.shape
        blocks = assemble_full(patterns, lax.all_gather(sep_inv, "pr", axis=0, tiled=True))
        order = jnp.tile(jnp.arange(sides, dtype=jnp.int32), nodes)
        nothing = jnp.zeros((1,), jnp.int32)
        plan = (nothing, nothing, jnp.stack([order, order, jnp.full_like(order, sides)]))
        *_, marg, out = work(nothing, plan, widths, sides, blocks, phase=0, factors=factor_halves(factor), before=dinv, last=True)
    return out, marg.reshape(cols)


def solution(mesh):
    placed = (
        P(("cfg", "pr"), None),
        P("cfg", "pr"),
        P("pr", None),
        P("pr", None),
        P(("cfg", "pr")),
    )
    return jax.shard_map(
        shards,
        mesh=mesh,
        in_specs=placed,
        out_specs=(P("cfg", "pr"), P(("cfg", "pr"))),
        check_vma=False,
    )
```

```python
import functools

import jax
import jax.numpy as jnp
from jax import lax
from jax.experimental import pallas as pl
from jax.experimental.pallas import tpu as pltpu
from jax.sharding import PartitionSpec as P

TILE = 128
HALF = TILE // 2
QUARTER = TILE // 4
FOLD, PAIR, FIRST = HALF, HALF + QUARTER, TILE + QUARTER
MIB = 1024 * 1024

ORDER = (0, 2, 1, 3, 4, 6, 5, 7)
PIECES = {
    "near": (2, True, (4, 6, 5, 7, 1, 3)),
    "side": (1, True, (3, 4, 6, 5, 7)),
    "mid": (4, True, (6, 5, 7)),
    "side_near": (3, True, (5, 7, 4, 6)),
    "far": (6, True, ()),
    "side_mid": (5, True, (7,)),
    "side_far": (7, True, ()),
    "far_rest": (6, False, (5, 7)),
}
ROUNDS = (("near", "side"), ("mid", "side_near", "far"), ("side_mid", "side_far", "far_rest"))
KINDS = ("rows",) + tuple(PIECES)
DEVICES = 16
LISTS = 6
WHOLE = (0, 0, 0, 1, 1, 2, 2, 2)
CLASSES = DEVICES // 2


def class_of(device, seen_from):
    place, here = device >> 2, seen_from >> 2
    outer = ((place >> 1) ^ place ^ 1) & 1
    z = jnp.where((place ^ here) >> 1 != 0, 2 + outer, (place ^ here) & 1)
    return 2 * z + (((device ^ seen_from) >> 1) & 1)


def device_of(column, seen_from, core):
    here, z = seen_from >> 2, column >> 1
    half = (here >> 1) ^ (z >> 1)
    inner_first = half ^ 1 ^ (z & 1)
    place = 2 * half + (inner_first if z >= 2 else (here & 1) ^ z)
    return 4 * place + 2 * (((seen_from >> 1) & 1) ^ (column & 1)) + core


def diagonal_rows(name):
    return TILE if name in ROUNDS[-1] else PAIR


def first_rows(name):
    return diagonal_rows(name) + HALF if PIECES[name][1] else 0


def piece_rows(*names):
    return sum(first_rows(name) + 2 * TILE * len(PIECES[name][2]) for name in names)


def piece_table():
    table = [0] * (CLASSES * CLASSES)
    for name, (owner, own, classes) in PIECES.items():
        kind = KINDS.index(name)
        for place, column in enumerate(classes):
            table[owner * CLASSES + column] = kind * 64 + first_rows(name) // QUARTER + 8 * place
        if own:
            table[owner * CLASSES + owner] = kind * 64 + diagonal_rows(name) // QUARTER
    return jnp.array(table, jnp.int32)


def call(kernel, name, given, out_shape, out_specs, after=(), vmem=6, cost=0, **more):
    places = {"smem": pltpu.SMEM, "vmem": pltpu.VMEM, "any": pl.ANY}
    arrays = [pltpu.with_memory_space_constraint(x, pltpu.VMEM) if space == "vmem" else x for space, x in given]
    inputs = len(given)

    def body(*refs):
        kernel(*refs[:inputs], *refs[inputs + len(after) :])

    return pl.pallas_call(
        body,
        out_shape=out_shape,
        in_specs=[pl.BlockSpec(memory_space=places[space]) for space, _ in given] + [pl.BlockSpec(memory_space=pl.ANY)] * len(after),
        out_specs=out_specs,
        compiler_params=pltpu.CompilerParams(vmem_limit_bytes=vmem * MIB),
        cost_estimate=pl.CostEstimate(flops=0, bytes_accessed=cost, transcendentals=0),
        name=name,
        **more,
    )(*arrays, *after)


SMEM = pl.BlockSpec(memory_space=pltpu.SMEM)
VMEM = pl.BlockSpec(memory_space=pltpu.VMEM)
US = 3_000_000


def split(value):
    high = value.astype(jnp.bfloat16)
    low = (value - high.astype(jnp.float32)).astype(jnp.bfloat16)
    return high, low


def pack_kernel(sets, me_ref, rows_ref, *refs):
    packed_refs, own_ref, first_sems, sems = refs[: len(sets)], *refs[len(sets) :]
    me = me_ref[0]

    def tile(q):
        return rows_ref.at[:, pl.ds(pl.multiple_of(q * TILE, TILE), TILE)]

    copies, firsts = [], []
    for names, packed_ref in zip(sets, packed_refs, strict=True):
        row = 0
        for name in names:
            owner, own, classes = PIECES[name]
            receiver = device_of(owner, me, 0) if owner < 4 else me ^ 12
            if own:
                firsts.append((own_ref, packed_ref.at[pl.ds(row, FIRST), :]))
                row += FIRST
            for q in [device_of(column, receiver, core) for column in classes for core in range(2)]:
                copies.append((tile(q), packed_ref.at[pl.ds(row, TILE), :]))
                row += TILE
    copies = [pltpu.make_async_copy(*ends, sems.at[i]) for i, ends in enumerate(copies)]
    firsts = [pltpu.make_async_copy(*ends, first_sems.at[i]) for i, ends in enumerate(firsts)]
    for copy in copies:
        copy.start()
    diagonal, pair = tile(me)[...], tile(me ^ 1)[...]
    own_ref[:FOLD, :] = diagonal[:HALF, :]
    first, second = diagonal[HALF : HALF + QUARTER, :], diagonal[HALF + QUARTER :, :]
    left = lax.broadcasted_iota(jnp.int32, first.shape, 1) < HALF
    own_ref[FOLD:PAIR, :] = jnp.where(left, pltpu.roll(first, HALF, 1), second)
    own_ref[PAIR:FIRST, :] = jnp.where(me % 2 == 0, pair[:HALF, :], pair.T[HALF:, :])
    for copy in firsts:
        copy.start()
    for copy in (*copies, *firsts):
        copy.wait()


def unfold(value):
    top, fold = value[:HALF, :], value[FOLD:PAIR, :]
    upper = jnp.concatenate([top, pltpu.roll(fold, HALF, 1), fold], axis=0)
    row, column = (lax.broadcasted_iota(jnp.int32, upper.shape, k) for k in range(2))
    return jnp.where((row >= HALF) & (column < HALF), upper.T, upper)


def pack(sets, me, sep_rows, after=()):
    names = [name for names in sets for name in names]
    tiles = sum(2 * len(PIECES[name][2]) for name in names)
    return call(
        functools.partial(pack_kernel, sets),
        "pack_" + names[0],
        [("smem", me), ("vmem", sep_rows)],
        [pltpu.HBM((piece_rows(*names), TILE), jnp.float32) for names in sets],
        [pl.BlockSpec(memory_space=pltpu.HBM)] * len(sets),
        after,
        scratch_shapes=[
            pltpu.VMEM((FIRST, TILE), jnp.float32),
            pltpu.SemaphoreType.DMA((len(names),)),
            pltpu.SemaphoreType.DMA((max(tiles, 1),)),
        ],
    )


def jobs_kernel(nodes, sides, me_ref, table_ref, patterns_ref, jobs_ref, count_ref, slots_ref):
    me = me_ref[0]
    ranks = sum(ORDER.index(c) << (3 * c) for c in range(CLASSES))
    phases = sum(WHOLE[c] << (2 * c) for c in range(CLASSES))
    for s in range(LISTS * len(KINDS)):
        count_ref[s] = 0

    def one(node, _):
        tiles = [patterns_ref[node, a] for a in range(sides)]
        classes = [class_of(tile, me) for tile in tiles]
        order = [(ranks >> (3 * c)) & 7 for c in classes]
        phase = [(phases >> (2 * c)) & 3 for c in classes]
        slots = []
        for a in range(sides):
            slot = sum(((phase[b] < phase[a]) if b > a else (phase[b] <= phase[a])).astype(jnp.int32) for b in range(sides) if b != a)
            slots_ref[0, node * sides + a] = slot
            slots_ref[1, node * sides + slot] = a
            slots.append(slot)
        for p in range(len(ROUNDS)):
            slots_ref[2 + p, node] = sum((phase[a] == p).astype(jnp.int32) for a in range(sides))

        def add(which, first, i, j):
            at = count_ref[which]
            code = (first * nodes + node) * sides + i
            jobs_ref[which, at] = ((code * sides + j) * sides + pick(slots, i)) * sides + pick(slots, j)
            count_ref[which] = at + 1

        def pick(values, i):
            value = values[0]
            for k in range(1, sides):
                value = jnp.where(i == k, values[k], value)
            return value

        for a in range(sides):
            r, c = tiles[a], classes[a]
            entry = table_ref[c * CLASSES + c]
            first = jnp.where(c == 0, r, 0)
            add(((entry >> 6) * 2 + ((r ^ me) & 1)) * 3 + 1, first, jnp.int32(a), jnp.int32(a))
        for a in range(sides):
            for b in range(a + 1, sides):
                turned = jnp.where(classes[a] == classes[b], (tiles[a] & 1) == 1, order[a] > order[b])
                r, q = jnp.where(turned, tiles[b], tiles[a]), jnp.where(turned, tiles[a], tiles[b])
                c, d = jnp.where(turned, classes[b], classes[a]), jnp.where(turned, classes[a], classes[b])
                i, j = jnp.where(turned, b, a), jnp.where(turned, a, b)
                entry = table_ref[c * CLASSES + d]
                halved = (c == d) & (c != 0)
                first = (entry & 63) + jnp.where(halved, 0, 4 * (q & 1))
                first = jnp.where(c == 0, q, first)
                which = ((entry >> 6) * 2 + jnp.where(halved, 0, (r ^ me) & 1)) * 3 + jnp.where(halved, 2, 0)
                add(which, first, i, j)

        return 0

    lax.fori_loop(0, nodes, one, 0)


def place(high_ref, low_ref, node, a, b, value):
    rows = pl.ds(pl.multiple_of(a * TILE, TILE), TILE)
    cols = pl.ds(pl.multiple_of(b * TILE, TILE), TILE)
    high_ref[node, rows, cols], low_ref[node, rows, cols] = split(value)


def put_tiles(sets, nodes, sides, me_ref, jobs_ref, count_ref, sources, high_ref, low_ref):
    even = (me_ref[0] & 1) == 0

    def work(name, pair, start):
        def read(which, sort, i):
            code = jobs_ref[which, i]
            fields = []
            for size in (sides, sides, sides, sides, nodes):
                fields.append(lax.rem(code, size))
                code = lax.div(code, size)
            slot_j, slot_i, j, i, node = fields
            other = (which // 3) % 2
            if name == "rows":
                value = pair[other][:, pl.ds(pl.multiple_of(code * TILE, TILE), TILE)]
            elif sort == 2:
                rows = pl.ds(pl.multiple_of(start + code * QUARTER, QUARTER), HALF)
                mine, theirs = pair[0][rows, :], pair[1][rows, :]
                value = jnp.concatenate([jnp.where(even, mine, theirs), jnp.where(even, theirs, mine)], axis=0)
            else:
                length = diagonal_rows(name) if sort == 1 else TILE
                value = pair[other][pl.ds(pl.multiple_of(start + code * QUARTER, QUARTER), length), :]
                value = unfold(value) if length == PAIR else value
            return node, i, j, slot_i, slot_j, value

        def put(sort, node, i, j, slot_i, slot_j, value):
            place(high_ref, low_ref, node, slot_i, j, value)
            if sort != 1:
                place(high_ref, low_ref, node, slot_j, i, value.T)

        def put_all(jobs):
            for sort, job in jobs:
                put(sort, *job)

        def list_of(other, sort):
            return (KINDS.index(name) * 2 + other) * 3 + sort

        def by_fours(sort):
            lists = [list_of(other, sort) for other in range(2)]
            numbers = [count_ref[which] for which in lists]
            both = (numbers[0] > 0) & (numbers[1] > 0)

            def some(chosen):
                def step(i, _):
                    jobs = []
                    for k in chosen:
                        for at in (2 * i, 2 * i + 1):
                            jobs.append((sort, read(lists[k], sort, jnp.minimum(at, numbers[k] - 1))))
                    put_all(jobs)
                    return 0

                return step

            most = jnp.maximum(numbers[0], numbers[1])
            lax.fori_loop(0, jnp.where(both, lax.div(most + 1, 2), 0), some((0, 1)), 0)
            for k in range(2):
                lax.fori_loop(0, jnp.where(both, 0, lax.div(numbers[k] + 1, 2)), some((k,)), 0)

        if name != "far_rest":
            by_fours(1)
        if name == "rows" or PIECES[name][2]:
            by_fours(0)
        if name == "rows" or not PIECES[name][1]:
            return
        which = list_of(0, 2)
        number = count_ref[which]

        def two(i, _):
            put_all([(2, read(which, 2, 2 * i)), (2, read(which, 2, 2 * i + 1))])
            return 0

        lax.fori_loop(0, lax.div(number, 2), two, 0)

        @pl.when(lax.rem(number, 2) == 1)
        def _():
            put_all([(2, read(which, 2, number - 1))])

    at = 0
    for names in sets:
        start = 0
        for name in names:
            work(name, sources[at : at + 2], start)
            start += 0 if name == "rows" else piece_rows(name)
        at += 2


def assemble_full_kernel(nodes, sides, patterns_ref, whole_ref, high_ref, low_ref):
    def one(step, _):
        node = step // (sides * sides)
        a = lax.rem(step // sides, sides)
        b = lax.rem(step, sides)
        rows = pl.ds(pl.multiple_of(patterns_ref[node, a] * TILE, TILE), TILE)
        cols = pl.ds(pl.multiple_of(patterns_ref[node, b] * TILE, TILE), TILE)
        place(high_ref, low_ref, node, a, b, whole_ref[rows, cols])
        return 0

    lax.fori_loop(0, nodes * sides * sides, one, 0)


def assemble_full(patterns, source):
    nodes, sides = patterns.shape
    side = sides * TILE
    return call(
        functools.partial(assemble_full_kernel, nodes, sides),
        "assemble_full",
        [("smem", patterns), ("vmem", source)],
        [pltpu.VMEM((nodes, side, side), jnp.bfloat16)] * 2,
        [VMEM] * 2,
    )


def halves_kernel(factor_ref, high_ref, low_ref):
    step = 4 * TILE
    for start in range(0, factor_ref.shape[1], step):
        where = slice(start, start + step)
        high_ref[:, where], low_ref[:, where] = split(factor_ref[:, where])


def factor_halves(factor, after=()):
    out = [pltpu.VMEM(factor.shape, jnp.bfloat16)] * 2
    return call(halves_kernel, "factor_halves", [("vmem", factor)], out, [VMEM] * 2, after)


def multiply_rows(phase, sides, widths_ref, slots_ref, high_ref, low_ref, f_high_ref, f_low_ref, out_ref, marg_ref, product_ref, sem):
    dot = functools.partial(jnp.dot, preferred_element_type=jnp.float32)
    nodes = widths_ref.shape[1]
    most = 8
    tall = 2

    def multiply(node, first, tile, height, width):
        cols = pl.ds(pl.multiple_of(tile * TILE, TILE), width * TILE)
        rows = pl.ds(pl.multiple_of(first * TILE, TILE), height * TILE)
        high, low = high_ref[node, rows, :], low_ref[node, rows, :]
        f_high, f_low = f_high_ref[:, cols], f_low_ref[:, cols]
        product = -(dot(high, f_high) + (dot(high, f_low) + dot(low, f_high)))
        total = jnp.zeros((1, width * TILE), jnp.float32)
        for i in range(height):
            part = product[i * TILE : (i + 1) * TILE, :]
            here = pl.ds(pl.multiple_of(slots_ref[1, node * sides + first + i] * TILE, TILE), TILE)
            product_ref[here, cols] = part
            factor = f_high_ref[here, cols].astype(jnp.float32) + f_low_ref[here, cols].astype(jnp.float32)
            total = total + jnp.sum(factor * part, axis=0, keepdims=True)
            pltpu.make_async_copy(product_ref.at[here, cols], out_ref.at[here, cols], sem).start()
        for k in range(width):
            row = pl.ds(tile + k, 1)
            marg_ref[row, :] = marg_ref[row, :] - total[:, k * TILE : (k + 1) * TILE]

    def one(node, carry):
        start, written = carry
        width = widths_ref[0, node]
        first, height = sum((slots_ref[2 + p, node] for p in range(phase)), 0), slots_ref[2 + phase, node]

        def across(row, h):
            def whole(i, _):
                multiply(node, row, start + most * i, h, most)
                return 0

            lax.fori_loop(0, lax.div(width, most), whole, 0)
            rest = lax.rem(width, most)
            for w in range(1, most):
                pl.when(rest == w)(lambda: multiply(node, row, start + width - rest, h, w))

        def down(i, _):
            across(first + tall * i, tall)
            return 0

        lax.fori_loop(0, lax.div(height, tall), down, 0)
        for h in range(1, tall):
            pl.when(lax.rem(height, tall) == h)(lambda: across(first + height - h, h))
        return start + width, written + width * height

    _, written = lax.fori_loop(0, nodes, one, (0, 0))

    def finish():
        rows, cols = product_ref.shape
        size = 1
        while size <= rows * cols // (TILE * TILE):
            wide = min(size, cols // TILE)
            part = (pl.ds(0, TILE * size // wide), pl.ds(0, TILE * wide))
            pl.when((written & size) != 0)(lambda: pltpu.make_async_copy(product_ref.at[part], out_ref.at[part], sem).wait())
            size *= 2

    return finish


def work_kernel(sets, phase, last, sides, *refs):
    me_ref, jobs_ref, count_ref, slots_ref, widths_ref, *refs = refs
    nodes = widths_ref.shape[1]
    sources, refs = refs[: 2 * len(sets)], refs[2 * len(sets) :]
    if phase is None:
        put_tiles(sets, nodes, sides, me_ref, jobs_ref, count_ref, sources, *refs[-2:])
        return
    f_high_ref, f_low_ref, before_ref, *_ = refs
    if not last:
        high_to, low_to, marg_ref, out_ref, product_ref, sems = refs[-6:]
    else:
        high_to, low_to, marg_out, out_ref, product_ref, sems, marg_ref = refs[-7:]
    if sets:
        put_tiles(sets, nodes, sides, me_ref, jobs_ref, count_ref, sources, high_to, low_to)
    marg_ref[...] = before_ref[...]
    finish = multiply_rows(
        phase, sides, widths_ref, slots_ref, high_to, low_to, f_high_ref, f_low_ref, out_ref, marg_ref, product_ref, sems.at[0]
    )
    if last:
        copy = pltpu.make_async_copy(marg_ref, marg_out, sems.at[1])
        copy.start()
        copy.wait()
    finish()


def work(me, plan, widths, sides, blocks, sets=(), sources=(), phase=None, factors=(), before=None, out=(), last=False, after=()):
    given = [("smem", x) for x in (me, *plan, widths)] + [("vmem", x) for x in sources]
    shapes = [pltpu.VMEM((widths.shape[1], sides * TILE, sides * TILE), jnp.bfloat16)] * 2
    specs, scratch, aliases = [VMEM] * 2, [], {}
    if phase is not None:
        given += [("vmem", x) for x in (*factors, before)]
    if blocks:
        aliases = {len(given): 0, len(given) + 1: 1}
        given += [("vmem", x) for x in blocks]
    if phase is not None:
        given += [("any", x) for x in out]
        rows, cols = factors[0].shape
        if out:
            aliases[len(given) - 1] = 3
        anywhere = pl.BlockSpec(memory_space=pl.ANY)
        marg = jax.ShapeDtypeStruct(before.shape, jnp.float32) if last else pltpu.VMEM(before.shape, jnp.float32)
        shapes += [marg, jax.ShapeDtypeStruct((rows, cols), jnp.float32)]
        specs += [anywhere if last else VMEM, anywhere]
        scratch = [pltpu.VMEM((rows, cols), jnp.float32), pltpu.SemaphoreType.DMA((2,))]
        scratch += [pltpu.VMEM(before.shape, jnp.float32)] if last else []
    name = "_".join([f"put_{names[0]}" for names in sets[:1]] + [f"multiply_{phase}"] * (phase is not None))
    kernel = functools.partial(work_kernel, sets, phase, last, sides)
    return call(
        kernel, name, given, shapes, specs, after, vmem=14 if scratch else 6, scratch_shapes=scratch, input_output_aliases=aliases
    )


def swap(value, mask):
    return lax.ppermute(value, "pr", [(i, i ^ mask) for i in range(DEVICES)])


def move(value, places):
    pairs = [(4 * old + k, 4 * new + k) for old, new in places.items() for k in range(4)]
    return lax.ppermute(value, "pr", pairs)


def plan_jobs(me, patterns, after):
    nodes, sides = patterns.shape
    shapes = [
        jax.ShapeDtypeStruct((LISTS * len(KINDS), nodes * sides), jnp.int32),
        jax.ShapeDtypeStruct((LISTS * len(KINDS),), jnp.int32),
        jax.ShapeDtypeStruct((2 + len(ROUNDS), nodes * sides), jnp.int32),
    ]
    given = [("smem", me), ("smem", piece_table()), ("smem", patterns)]
    return call(functools.partial(jobs_kernel, nodes, sides), "plan_jobs", given, shapes, [SMEM] * 3, after)


def turn(name, kernel, me, given, rows, held, after=()):
    shapes = [pltpu.VMEM((n, TILE), jnp.float32) for n in rows] + [pltpu.VMEM(x.shape, x.dtype) for x in held]

    def body(me_ref, *refs):
        place = me_ref[0] >> 2
        kernel((place == 1) | (place == 2), *refs[: len(given)], *refs[len(given) + len(held) :][: len(rows)])

    inputs = [("smem", me)] + [("vmem", x) for x in (*given, *held)]
    aliases = {1 + len(given) + i: len(rows) + i for i in range(len(held))}
    return call(body, name, inputs, shapes, [VMEM] * len(shapes), after, input_output_aliases=aliases)


def copy_rows(target_ref, row, source_ref, first=0, count=None):
    count = source_ref.shape[0] - first if count is None else count
    target_ref[row : row + count, :] = source_ref[first : first + count, :]
    return row + count


def turn_1(inner, near_ref, side_ref, part_ref, held_ref, far_ref):
    copy_rows(part_ref, 0, near_ref, 0, part_ref.shape[0])
    copy_rows(held_ref, copy_rows(held_ref, 0, near_ref), side_ref)
    first, rest = piece_rows("far"), piece_rows("far_rest")
    copy_rows(far_ref, 0, near_ref, 0, first)
    copy_rows(far_ref, first, near_ref, near_ref.shape[0] - rest, rest)


def turn_2(inner, mid_ref, mid_outer_ref, far_ref, far_outer_ref, side_near_ref, part_ref, held_ref, rest_ref):
    mid, far, onward = piece_rows("mid"), piece_rows("far"), piece_rows("side_mid")

    def take(m_ref, f_ref):
        for row, ref, count in ((0, m_ref, onward), (onward, f_ref, piece_rows("side_far"))):
            part_ref[row : row + TILE, :] = unfold(ref[:PAIR, :])
            copy_rows(part_ref, row + TILE, ref, PAIR, count - TILE)
        copy_rows(held_ref, 0, m_ref)
        copy_rows(held_ref, mid + side_near_ref.shape[0], f_ref, 0, far)

    pl.when(inner)(lambda: take(mid_ref, far_ref))
    pl.when(jnp.logical_not(inner))(lambda: take(mid_outer_ref, far_outer_ref))
    copy_rows(held_ref, mid, side_near_ref)
    copy_rows(rest_ref, 0, far_ref, far)


def turn_3(inner, rest_ref, rest_outer_ref, held_ref):
    pl.when(inner)(lambda: copy_rows(held_ref, 0, rest_ref) and None)
    pl.when(jnp.logical_not(inner))(lambda: copy_rows(held_ref, 0, rest_outer_ref) and None)


def hold(value, after):
    out = pltpu.VMEM(value.shape, value.dtype)
    return call(lambda *refs: None, "hold", [("vmem", value)], out, VMEM, after, input_output_aliases={0: 0})


def planned(sep_inv, factor, widths, patterns, dinv):
    me = lax.axis_index("pr").astype(jnp.int32).reshape(1)
    between_inner, between_outer, outward = {1: 2, 2: 1}, {0: 3, 3: 0}, {1: 0, 2: 3}

    near, side = pack((("near",), ("side",)), me, sep_inv)
    mid, first = pack((("mid",), ("far",)), me, sep_inv, (near,))
    rows_other = swap(sep_inv, 1)
    near, side, mid = swap(near, 4), swap(side, 2), move(mid, between_inner)
    plan = plan_jobs(me, patterns, (rows_other,))
    factors = factor_halves(factor, plan[1:2])
    do = functools.partial(work, me, plan, widths, patterns.shape[1])
    blocks = do((), (("rows",),), (sep_inv, rows_other), after=factors[:1])
    rows = (piece_rows("side_near"), piece_rows(*ROUNDS[0]), piece_rows("far", "far_rest"))
    part, held, far, mid = turn("turn_1", turn_1, me, (near, side), rows, (mid,), blocks[:1])

    side_near, mid_outer = swap(part, 2), move(mid, outward)
    far, far_outer = move(far, between_inner), move(first, between_outer)
    *blocks, marg, out = do(blocks, ROUNDS[:1], (held, swap(held, 1)), 0, factors, dinv)
    rows = (piece_rows("side_mid", "side_far"), piece_rows(*ROUNDS[1]), piece_rows("far_rest"))
    part, held, rest = turn("turn_2", turn_2, me, (mid, mid_outer, far, far_outer, side_near), rows, (), (marg,))

    side_last, rest_outer = swap(part, 2), move(rest, outward)
    *blocks, marg, out = do(blocks, ROUNDS[1:2], (held, swap(held, 1)), 1, factors, marg, (out,))
    side_last = hold(side_last, (marg,))
    (rest,) = turn("turn_3", turn_3, me, (rest, rest_outer), (piece_rows("far_rest"),), (), (marg, side_last))
    sets, sources = (ROUNDS[2][:2], ROUNDS[2][2:]), (side_last, swap(side_last, 1), rest, swap(rest, 1))
    *_, marg, out = do(blocks, sets, sources, 2, factors, marg, (out,), last=True)
    return out, marg


def shards(sep_inv, factor, widths, patterns, dinv):
    own_rows, order = sep_inv.shape
    cols = factor.shape[1]
    dinv = dinv.reshape(cols // TILE, TILE)
    if own_rows == TILE and order == DEVICES * TILE:
        out, marg = planned(sep_inv, factor, widths, patterns, dinv)
    else:
        nodes, sides = patterns.shape
        blocks = assemble_full(patterns, lax.all_gather(sep_inv, "pr", axis=0, tiled=True))
        order = jnp.tile(jnp.arange(sides, dtype=jnp.int32), nodes)
        nothing = jnp.zeros((1,), jnp.int32)
        plan = (nothing, nothing, jnp.stack([order, order, jnp.full_like(order, sides)]))
        *_, marg, out = work(nothing, plan, widths, sides, blocks, phase=0, factors=factor_halves(factor), before=dinv, last=True)
    return out, marg.reshape(cols)


def solution(mesh):
    placed = (
        P(("cfg", "pr"), None),
        P("cfg", "pr"),
        P("pr", None),
        P("pr", None),
        P(("cfg", "pr")),
    )
    return jax.shard_map(
        shards,
        mesh=mesh,
        in_specs=placed,
        out_specs=(P("cfg", "pr"), P(("cfg", "pr"))),
        check_vma=False,
    )
```

```python
import functools

import jax
import jax.numpy as jnp
from jax import lax
from jax.experimental import pallas as pl
from jax.experimental.pallas import tpu as pltpu
from jax.sharding import PartitionSpec as P

TILE = 128
HALF = TILE // 2
QUARTER = TILE // 4
FOLD, PAIR, FIRST = HALF, HALF + QUARTER, TILE + QUARTER
MIB = 1024 * 1024

ORDER = (0, 2, 1, 3, 4, 6, 5, 7)
PIECES = {
    "near": (2, True, (4, 6, 5, 7, 1, 3)),
    "side": (1, True, (3, 4, 6, 5, 7)),
    "mid": (4, True, (6, 5, 7)),
    "side_near": (3, True, (5, 7, 4, 6)),
    "far": (6, True, ()),
    "side_mid": (5, True, (7,)),
    "side_far": (7, True, ()),
    "far_rest": (6, False, (5, 7)),
}
ROUNDS = (("near", "side"), ("mid", "side_near", "far"), ("side_mid", "side_far", "far_rest"))
KINDS = ("rows",) + tuple(PIECES)
DEVICES = 16
LISTS = 6
WHOLE = (0, 0, 0, 1, 1, 2, 2, 2)
CLASSES = DEVICES // 2


def class_of(device, seen_from):
    place, here = device >> 2, seen_from >> 2
    outer = ((place >> 1) ^ place ^ 1) & 1
    z = jnp.where((place ^ here) >> 1 != 0, 2 + outer, (place ^ here) & 1)
    return 2 * z + (((device ^ seen_from) >> 1) & 1)


def device_of(column, seen_from, core):
    here, z = seen_from >> 2, column >> 1
    half = (here >> 1) ^ (z >> 1)
    inner_first = half ^ 1 ^ (z & 1)
    place = 2 * half + (inner_first if z >= 2 else (here & 1) ^ z)
    return 4 * place + 2 * (((seen_from >> 1) & 1) ^ (column & 1)) + core


def diagonal_rows(name):
    return TILE if name in ROUNDS[-1] else PAIR


def first_rows(name):
    return diagonal_rows(name) + HALF if PIECES[name][1] else 0


def piece_rows(*names):
    return sum(first_rows(name) + 2 * TILE * len(PIECES[name][2]) for name in names)


def piece_table():
    table = [0] * (CLASSES * CLASSES)
    for name, (owner, own, classes) in PIECES.items():
        kind = KINDS.index(name)
        for place, column in enumerate(classes):
            table[owner * CLASSES + column] = kind * 64 + first_rows(name) // QUARTER + 8 * place
        if own:
            table[owner * CLASSES + owner] = kind * 64 + diagonal_rows(name) // QUARTER
    return jnp.array(table, jnp.int32)


def call(kernel, name, given, out_shape, out_specs, after=(), vmem=6, cost=0, **more):
    places = {"smem": pltpu.SMEM, "vmem": pltpu.VMEM, "any": pl.ANY}
    arrays = [pltpu.with_memory_space_constraint(x, pltpu.VMEM) if space == "vmem" else x for space, x in given]
    inputs = len(given)

    def body(*refs):
        kernel(*refs[:inputs], *refs[inputs + len(after) :])

    return pl.pallas_call(
        body,
        out_shape=out_shape,
        in_specs=[pl.BlockSpec(memory_space=places[space]) for space, _ in given] + [pl.BlockSpec(memory_space=pl.ANY)] * len(after),
        out_specs=out_specs,
        compiler_params=pltpu.CompilerParams(vmem_limit_bytes=vmem * MIB),
        cost_estimate=pl.CostEstimate(flops=0, bytes_accessed=cost, transcendentals=0),
        name=name,
        **more,
    )(*arrays, *after)


SMEM = pl.BlockSpec(memory_space=pltpu.SMEM)
VMEM = pl.BlockSpec(memory_space=pltpu.VMEM)
US = 3_000_000


def split(value):
    high = value.astype(jnp.bfloat16)
    low = (value - high.astype(jnp.float32)).astype(jnp.bfloat16)
    return high, low


def pack_kernel(sets, me_ref, rows_ref, *refs):
    packed_refs, own_ref, first_sems, sems = refs[: len(sets)], *refs[len(sets) :]
    me = me_ref[0]

    def tile(q):
        return rows_ref.at[:, pl.ds(pl.multiple_of(q * TILE, TILE), TILE)]

    copies, firsts = [], []
    for names, packed_ref in zip(sets, packed_refs, strict=True):
        row = 0
        for name in names:
            owner, own, classes = PIECES[name]
            receiver = device_of(owner, me, 0) if owner < 4 else me ^ 12
            if own:
                firsts.append((own_ref, packed_ref.at[pl.ds(row, FIRST), :]))
                row += FIRST
            for q in [device_of(column, receiver, core) for column in classes for core in range(2)]:
                copies.append((tile(q), packed_ref.at[pl.ds(row, TILE), :]))
                row += TILE
    copies = [pltpu.make_async_copy(*ends, sems.at[i]) for i, ends in enumerate(copies)]
    firsts = [pltpu.make_async_copy(*ends, first_sems.at[i]) for i, ends in enumerate(firsts)]
    for copy in copies:
        copy.start()
    diagonal, pair = tile(me)[...], tile(me ^ 1)[...]
    own_ref[:FOLD, :] = diagonal[:HALF, :]
    first, second = diagonal[HALF : HALF + QUARTER, :], diagonal[HALF + QUARTER :, :]
    left = lax.broadcasted_iota(jnp.int32, first.shape, 1) < HALF
    own_ref[FOLD:PAIR, :] = jnp.where(left, pltpu.roll(first, HALF, 1), second)
    own_ref[PAIR:FIRST, :] = jnp.where(me % 2 == 0, pair[:HALF, :], pair.T[HALF:, :])
    for copy in firsts:
        copy.start()
    for copy in (*copies, *firsts):
        copy.wait()


def unfold(value):
    top, fold = value[:HALF, :], value[FOLD:PAIR, :]
    upper = jnp.concatenate([top, pltpu.roll(fold, HALF, 1), fold], axis=0)
    row, column = (lax.broadcasted_iota(jnp.int32, upper.shape, k) for k in range(2))
    return jnp.where((row >= HALF) & (column < HALF), upper.T, upper)


def pack(sets, me, sep_rows, after=()):
    names = [name for names in sets for name in names]
    tiles = sum(2 * len(PIECES[name][2]) for name in names)
    return call(
        functools.partial(pack_kernel, sets),
        "pack_" + names[0],
        [("smem", me), ("vmem", sep_rows)],
        [pltpu.HBM((piece_rows(*names), TILE), jnp.float32) for names in sets],
        [pl.BlockSpec(memory_space=pltpu.HBM)] * len(sets),
        after,
        scratch_shapes=[
            pltpu.VMEM((FIRST, TILE), jnp.float32),
            pltpu.SemaphoreType.DMA((len(names),)),
            pltpu.SemaphoreType.DMA((max(tiles, 1),)),
        ],
    )


def jobs_kernel(nodes, sides, me_ref, table_ref, patterns_ref, jobs_ref, count_ref, slots_ref):
    me = me_ref[0]
    ranks = sum(ORDER.index(c) << (3 * c) for c in range(CLASSES))
    phases = sum(WHOLE[c] << (2 * c) for c in range(CLASSES))
    for s in range(LISTS * len(KINDS)):
        count_ref[s] = 0

    def one(node, _):
        tiles = [patterns_ref[node, a] for a in range(sides)]
        classes = [class_of(tile, me) for tile in tiles]
        order = [(ranks >> (3 * c)) & 7 for c in classes]
        phase = [(phases >> (2 * c)) & 3 for c in classes]
        slots = []
        for a in range(sides):
            slot = sum(((phase[b] < phase[a]) if b > a else (phase[b] <= phase[a])).astype(jnp.int32) for b in range(sides) if b != a)
            slots_ref[0, node * sides + a] = slot
            slots_ref[1, node * sides + slot] = a
            slots.append(slot)
        for p in range(len(ROUNDS)):
            slots_ref[2 + p, node] = sum((phase[a] == p).astype(jnp.int32) for a in range(sides))

        def add(which, first, i, j):
            at = count_ref[which]
            code = (first * nodes + node) * sides + i
            jobs_ref[which, at] = ((code * sides + j) * sides + pick(slots, i)) * sides + pick(slots, j)
            count_ref[which] = at + 1

        def pick(values, i):
            value = values[0]
            for k in range(1, sides):
                value = jnp.where(i == k, values[k], value)
            return value

        for a in range(sides):
            r, c = tiles[a], classes[a]
            entry = table_ref[c * CLASSES + c]
            first = jnp.where(c == 0, r, 0)
            add(((entry >> 6) * 2 + ((r ^ me) & 1)) * 3 + 1, first, jnp.int32(a), jnp.int32(a))
        for a in range(sides):
            for b in range(a + 1, sides):
                turned = jnp.where(classes[a] == classes[b], (tiles[a] & 1) == 1, order[a] > order[b])
                r, q = jnp.where(turned, tiles[b], tiles[a]), jnp.where(turned, tiles[a], tiles[b])
                c, d = jnp.where(turned, classes[b], classes[a]), jnp.where(turned, classes[a], classes[b])
                i, j = jnp.where(turned, b, a), jnp.where(turned, a, b)
                entry = table_ref[c * CLASSES + d]
                halved = (c == d) & (c != 0)
                first = (entry & 63) + jnp.where(halved, 0, 4 * (q & 1))
                first = jnp.where(c == 0, q, first)
                which = ((entry >> 6) * 2 + jnp.where(halved, 0, (r ^ me) & 1)) * 3 + jnp.where(halved, 2, 0)
                add(which, first, i, j)

        return 0

    lax.fori_loop(0, nodes, one, 0)


def place(high_ref, low_ref, node, a, b, value):
    rows = pl.ds(pl.multiple_of(a * TILE, TILE), TILE)
    cols = pl.ds(pl.multiple_of(b * TILE, TILE), TILE)
    high_ref[node, rows, cols], low_ref[node, rows, cols] = split(value)


def put_tiles(sets, nodes, sides, me_ref, jobs_ref, count_ref, sources, high_ref, low_ref):
    even = (me_ref[0] & 1) == 0

    def work(name, pair, start):
        def read(which, sort, i):
            code = jobs_ref[which, i]
            fields = []
            for size in (sides, sides, sides, sides, nodes):
                fields.append(lax.rem(code, size))
                code = lax.div(code, size)
            slot_j, slot_i, j, i, node = fields
            other = (which // 3) % 2
            if name == "rows":
                value = pair[other][:, pl.ds(pl.multiple_of(code * TILE, TILE), TILE)]
            elif sort == 2:
                rows = pl.ds(pl.multiple_of(start + code * QUARTER, QUARTER), HALF)
                mine, theirs = pair[0][rows, :], pair[1][rows, :]
                value = jnp.concatenate([jnp.where(even, mine, theirs), jnp.where(even, theirs, mine)], axis=0)
            else:
                length = diagonal_rows(name) if sort == 1 else TILE
                value = pair[other][pl.ds(pl.multiple_of(start + code * QUARTER, QUARTER), length), :]
                value = unfold(value) if length == PAIR else value
            return node, i, j, slot_i, slot_j, value

        def put(sort, node, i, j, slot_i, slot_j, value):
            place(high_ref, low_ref, node, slot_i, j, value)
            if sort != 1:
                place(high_ref, low_ref, node, slot_j, i, value.T)

        def put_all(jobs):
            for sort, job in jobs:
                put(sort, *job)

        def list_of(other, sort):
            return (KINDS.index(name) * 2 + other) * 3 + sort

        def by_fours(sort):
            lists = [list_of(other, sort) for other in range(2)]
            numbers = [count_ref[which] for which in lists]
            both = (numbers[0] > 0) & (numbers[1] > 0)

            def some(chosen):
                def step(i, _):
                    jobs = []
                    for k in chosen:
                        for at in (2 * i, 2 * i + 1):
                            jobs.append((sort, read(lists[k], sort, jnp.minimum(at, numbers[k] - 1))))
                    put_all(jobs)
                    return 0

                return step

            most = jnp.maximum(numbers[0], numbers[1])
            lax.fori_loop(0, jnp.where(both, lax.div(most + 1, 2), 0), some((0, 1)), 0)
            for k in range(2):
                lax.fori_loop(0, jnp.where(both, 0, lax.div(numbers[k] + 1, 2)), some((k,)), 0)

        if name != "far_rest":
            by_fours(1)
        if name == "rows" or PIECES[name][2]:
            by_fours(0)
        if name == "rows" or not PIECES[name][1]:
            return
        which = list_of(0, 2)
        number = count_ref[which]

        def two(i, _):
            put_all([(2, read(which, 2, 2 * i)), (2, read(which, 2, 2 * i + 1))])
            return 0

        lax.fori_loop(0, lax.div(number, 2), two, 0)

        @pl.when(lax.rem(number, 2) == 1)
        def _():
            put_all([(2, read(which, 2, number - 1))])

    at = 0
    for names in sets:
        start = 0
        for name in names:
            work(name, sources[at : at + 2], start)
            start += 0 if name == "rows" else piece_rows(name)
        at += 2


def assemble_full_kernel(nodes, sides, patterns_ref, whole_ref, high_ref, low_ref):
    def one(step, _):
        node = step // (sides * sides)
        a = lax.rem(step // sides, sides)
        b = lax.rem(step, sides)
        rows = pl.ds(pl.multiple_of(patterns_ref[node, a] * TILE, TILE), TILE)
        cols = pl.ds(pl.multiple_of(patterns_ref[node, b] * TILE, TILE), TILE)
        place(high_ref, low_ref, node, a, b, whole_ref[rows, cols])
        return 0

    lax.fori_loop(0, nodes * sides * sides, one, 0)


def assemble_full(patterns, source):
    nodes, sides = patterns.shape
    side = sides * TILE
    return call(
        functools.partial(assemble_full_kernel, nodes, sides),
        "assemble_full",
        [("smem", patterns), ("vmem", source)],
        [pltpu.VMEM((nodes, side, side), jnp.bfloat16)] * 2,
        [VMEM] * 2,
    )


def halves_kernel(factor_ref, high_ref, low_ref):
    step = 4 * TILE
    for start in range(0, factor_ref.shape[1], step):
        where = slice(start, start + step)
        high_ref[:, where], low_ref[:, where] = split(factor_ref[:, where])


def factor_halves(factor, after=()):
    out = [pltpu.VMEM(factor.shape, jnp.bfloat16)] * 2
    return call(halves_kernel, "factor_halves", [("vmem", factor)], out, [VMEM] * 2, after)


def multiply_rows(phase, sides, widths_ref, slots_ref, high_ref, low_ref, f_high_ref, f_low_ref, out_ref, marg_ref, product_ref, sem):
    dot = functools.partial(jnp.dot, preferred_element_type=jnp.float32)
    nodes = widths_ref.shape[1]
    most = 8
    tall = 2

    def multiply(node, first, tile, height, width):
        cols = pl.ds(pl.multiple_of(tile * TILE, TILE), width * TILE)
        rows = pl.ds(pl.multiple_of(first * TILE, TILE), height * TILE)
        high, low = high_ref[node, rows, :], low_ref[node, rows, :]
        f_high, f_low = f_high_ref[:, cols], f_low_ref[:, cols]
        product = -(dot(high, f_high) + (dot(high, f_low) + dot(low, f_high)))
        total = jnp.zeros((1, width * TILE), jnp.float32)
        for i in range(height):
            part = product[i * TILE : (i + 1) * TILE, :]
            here = pl.ds(pl.multiple_of(slots_ref[1, node * sides + first + i] * TILE, TILE), TILE)
            product_ref[here, cols] = part
            factor = f_high_ref[here, cols].astype(jnp.float32) + f_low_ref[here, cols].astype(jnp.float32)
            total = total + jnp.sum(factor * part, axis=0, keepdims=True)
            pltpu.make_async_copy(product_ref.at[here, cols], out_ref.at[here, cols], sem).start()
        for k in range(width):
            row = pl.ds(tile + k, 1)
            marg_ref[row, :] = marg_ref[row, :] - total[:, k * TILE : (k + 1) * TILE]

    def one(node, carry):
        start, written = carry
        width = widths_ref[0, node]
        first, height = sum((slots_ref[2 + p, node] for p in range(phase)), 0), slots_ref[2 + phase, node]

        def across(row, h):
            def whole(i, _):
                multiply(node, row, start + most * i, h, most)
                return 0

            lax.fori_loop(0, lax.div(width, most), whole, 0)
            rest = lax.rem(width, most)
            for w in range(1, most):
                pl.when(rest == w)(lambda: multiply(node, row, start + width - rest, h, w))

        def down(i, _):
            across(first + tall * i, tall)
            return 0

        lax.fori_loop(0, lax.div(height, tall), down, 0)
        for h in range(1, tall):
            pl.when(lax.rem(height, tall) == h)(lambda: across(first + height - h, h))
        return start + width, written + width * height

    _, written = lax.fori_loop(0, nodes, one, (0, 0))

    def finish():
        rows, cols = product_ref.shape
        size = 1
        while size <= rows * cols // (TILE * TILE):
            wide = min(size, cols // TILE)
            part = (pl.ds(0, TILE * size // wide), pl.ds(0, TILE * wide))
            pl.when((written & size) != 0)(lambda: pltpu.make_async_copy(product_ref.at[part], out_ref.at[part], sem).wait())
            size *= 2

    return finish


def work_kernel(sets, phase, last, sides, *refs):
    me_ref, jobs_ref, count_ref, slots_ref, widths_ref, *refs = refs
    nodes = widths_ref.shape[1]
    sources, refs = refs[: 2 * len(sets)], refs[2 * len(sets) :]
    if phase is None:
        put_tiles(sets, nodes, sides, me_ref, jobs_ref, count_ref, sources, *refs[-2:])
        return
    f_high_ref, f_low_ref, before_ref, *_ = refs
    if not last:
        high_to, low_to, marg_ref, out_ref, product_ref, sems = refs[-6:]
    else:
        high_to, low_to, marg_out, out_ref, product_ref, sems, marg_ref = refs[-7:]
    if sets:
        put_tiles(sets, nodes, sides, me_ref, jobs_ref, count_ref, sources, high_to, low_to)
    marg_ref[...] = before_ref[...]
    finish = multiply_rows(
        phase, sides, widths_ref, slots_ref, high_to, low_to, f_high_ref, f_low_ref, out_ref, marg_ref, product_ref, sems.at[0]
    )
    if last:
        copy = pltpu.make_async_copy(marg_ref, marg_out, sems.at[1])
        copy.start()
        copy.wait()
    finish()


def work(me, plan, widths, sides, blocks, sets=(), sources=(), phase=None, factors=(), before=None, out=(), last=False, after=()):
    given = [("smem", x) for x in (me, *plan, widths)] + [("vmem", x) for x in sources]
    shapes = [pltpu.VMEM((widths.shape[1], sides * TILE, sides * TILE), jnp.bfloat16)] * 2
    specs, scratch, aliases = [VMEM] * 2, [], {}
    if phase is not None:
        given += [("vmem", x) for x in (*factors, before)]
    if blocks:
        aliases = {len(given): 0, len(given) + 1: 1}
        given += [("vmem", x) for x in blocks]
    if phase is not None:
        given += [("any", x) for x in out]
        rows, cols = factors[0].shape
        if out:
            aliases[len(given) - 1] = 3
        anywhere = pl.BlockSpec(memory_space=pl.ANY)
        marg = jax.ShapeDtypeStruct(before.shape, jnp.float32) if last else pltpu.VMEM(before.shape, jnp.float32)
        shapes += [marg, jax.ShapeDtypeStruct((rows, cols), jnp.float32)]
        specs += [anywhere if last else VMEM, anywhere]
        scratch = [pltpu.VMEM((rows, cols), jnp.float32), pltpu.SemaphoreType.DMA((2,))]
        scratch += [pltpu.VMEM(before.shape, jnp.float32)] if last else []
    name = "_".join([f"put_{names[0]}" for names in sets[:1]] + [f"multiply_{phase}"] * (phase is not None))
    kernel = functools.partial(work_kernel, sets, phase, last, sides)
    return call(
        kernel, name, given, shapes, specs, after, vmem=14 if scratch else 6, scratch_shapes=scratch, input_output_aliases=aliases
    )


def swap(value, mask):
    return lax.ppermute(value, "pr", [(i, i ^ mask) for i in range(DEVICES)])


def move(value, places):
    pairs = [(4 * old + k, 4 * new + k) for old, new in places.items() for k in range(4)]
    return lax.ppermute(value, "pr", pairs)


def plan_jobs(me, patterns, after):
    nodes, sides = patterns.shape
    shapes = [
        jax.ShapeDtypeStruct((LISTS * len(KINDS), nodes * sides), jnp.int32),
        jax.ShapeDtypeStruct((LISTS * len(KINDS),), jnp.int32),
        jax.ShapeDtypeStruct((2 + len(ROUNDS), nodes * sides), jnp.int32),
    ]
    given = [("smem", me), ("smem", piece_table()), ("smem", patterns)]
    return call(functools.partial(jobs_kernel, nodes, sides), "plan_jobs", given, shapes, [SMEM] * 3, after)


def turn(name, kernel, me, given, rows, held, after=()):
    shapes = [pltpu.VMEM((n, TILE), jnp.float32) for n in rows] + [pltpu.VMEM(x.shape, x.dtype) for x in held]

    def body(me_ref, *refs):
        place = me_ref[0] >> 2
        kernel((place == 1) | (place == 2), *refs[: len(given)], *refs[len(given) + len(held) :][: len(rows)])

    inputs = [("smem", me)] + [("vmem", x) for x in (*given, *held)]
    aliases = {1 + len(given) + i: len(rows) + i for i in range(len(held))}
    return call(body, name, inputs, shapes, [VMEM] * len(shapes), after, input_output_aliases=aliases)


def copy_rows(target_ref, row, source_ref, first=0, count=None):
    count = source_ref.shape[0] - first if count is None else count
    target_ref[row : row + count, :] = source_ref[first : first + count, :]
    return row + count


def turn_1(inner, near_ref, side_ref, part_ref, held_ref, far_ref):
    copy_rows(part_ref, 0, near_ref, 0, part_ref.shape[0])
    copy_rows(held_ref, copy_rows(held_ref, 0, near_ref), side_ref)
    first, rest = piece_rows("far"), piece_rows("far_rest")
    copy_rows(far_ref, 0, near_ref, 0, first)
    copy_rows(far_ref, first, near_ref, near_ref.shape[0] - rest, rest)


def turn_2(inner, mid_ref, mid_outer_ref, far_ref, far_outer_ref, side_near_ref, part_ref, held_ref, rest_ref):
    mid, far, onward = piece_rows("mid"), piece_rows("far"), piece_rows("side_mid")

    def take(m_ref, f_ref):
        for row, ref, count in ((0, m_ref, onward), (onward, f_ref, piece_rows("side_far"))):
            part_ref[row : row + TILE, :] = unfold(ref[:PAIR, :])
            copy_rows(part_ref, row + TILE, ref, PAIR, count - TILE)
        copy_rows(held_ref, 0, m_ref)
        copy_rows(held_ref, mid + side_near_ref.shape[0], f_ref, 0, far)

    pl.when(inner)(lambda: take(mid_ref, far_ref))
    pl.when(jnp.logical_not(inner))(lambda: take(mid_outer_ref, far_outer_ref))
    copy_rows(held_ref, mid, side_near_ref)
    copy_rows(rest_ref, 0, far_ref, far)


def turn_3(inner, rest_ref, rest_outer_ref, held_ref):
    pl.when(inner)(lambda: copy_rows(held_ref, 0, rest_ref) and None)
    pl.when(jnp.logical_not(inner))(lambda: copy_rows(held_ref, 0, rest_outer_ref) and None)


def hold(value, after):
    out = pltpu.VMEM(value.shape, value.dtype)
    return call(lambda *refs: None, "hold", [("vmem", value)], out, VMEM, after, input_output_aliases={0: 0})


def planned(sep_inv, factor, widths, patterns, dinv):
    me = lax.axis_index("pr").astype(jnp.int32).reshape(1)
    between_inner, between_outer, outward = {1: 2, 2: 1}, {0: 3, 3: 0}, {1: 0, 2: 3}

    near, side = pack((("near",), ("side",)), me, sep_inv)
    mid, first = pack((("mid",), ("far",)), me, sep_inv, (side,))
    rows_other = swap(sep_inv, 1)
    near, side, mid = swap(near, 4), swap(side, 2), move(mid, between_inner)
    plan = plan_jobs(me, patterns, (rows_other,))
    factors = factor_halves(factor, plan[1:2])
    do = functools.partial(work, me, plan, widths, patterns.shape[1])
    blocks = do((), (("rows",),), (sep_inv, rows_other), after=factors[:1])
    rows = (piece_rows("side_near"), piece_rows(*ROUNDS[0]), piece_rows("far", "far_rest"))
    part, held, far, mid = turn("turn_1", turn_1, me, (near, side), rows, (mid,), blocks[:1])

    side_near, mid_outer = swap(part, 2), move(mid, outward)
    far, far_outer = move(far, between_inner), move(first, between_outer)
    *blocks, marg, out = do(blocks, ROUNDS[:1], (held, swap(held, 1)), 0, factors, dinv)
    rows = (piece_rows("side_mid", "side_far"), piece_rows(*ROUNDS[1]), piece_rows("far_rest"))
    part, held, rest = turn("turn_2", turn_2, me, (mid, mid_outer, far, far_outer, side_near), rows, (), (marg,))

    side_last, rest_outer = swap(part, 2), move(rest, outward)
    *blocks, marg, out = do(blocks, ROUNDS[1:2], (held, swap(held, 1)), 1, factors, marg, (out,))
    side_last = hold(side_last, (marg,))
    (rest,) = turn("turn_3", turn_3, me, (rest, rest_outer), (piece_rows("far_rest"),), (), (marg, side_last))
    sets, sources = (ROUNDS[2][:2], ROUNDS[2][2:]), (side_last, swap(side_last, 1), rest, swap(rest, 1))
    *_, marg, out = do(blocks, sets, sources, 2, factors, marg, (out,), last=True)
    return out, marg


def shards(sep_inv, factor, widths, patterns, dinv):
    own_rows, order = sep_inv.shape
    cols = factor.shape[1]
    dinv = dinv.reshape(cols // TILE, TILE)
    if own_rows == TILE and order == DEVICES * TILE:
        out, marg = planned(sep_inv, factor, widths, patterns, dinv)
    else:
        nodes, sides = patterns.shape
        blocks = assemble_full(patterns, lax.all_gather(sep_inv, "pr", axis=0, tiled=True))
        order = jnp.tile(jnp.arange(sides, dtype=jnp.int32), nodes)
        nothing = jnp.zeros((1,), jnp.int32)
        plan = (nothing, nothing, jnp.stack([order, order, jnp.full_like(order, sides)]))
        *_, marg, out = work(nothing, plan, widths, sides, blocks, phase=0, factors=factor_halves(factor), before=dinv, last=True)
    return out, marg.reshape(cols)


def solution(mesh):
    placed = (
        P(("cfg", "pr"), None),
        P("cfg", "pr"),
        P("pr", None),
        P("pr", None),
        P(("cfg", "pr")),
    )
    return jax.shard_map(
        shards,
        mesh=mesh,
        in_specs=placed,
        out_specs=(P("cfg", "pr"), P(("cfg", "pr"))),
        check_vma=False,
    )
```
